32 devices in a mesh: sensor: 2 (over x), cell: 16 (over z, y, core).
Axes of the slice: x: 2, y: 2, z: 4, core: 2. Of those that a mesh axis runs over, the one named last changes fastest.
Arguments:
- swath: float32 [2, 64, 8192], P('sensor', None, 'cell'), may hold values from -6 to 6
- enc_weight: float32 [2, 64, 192], P('sensor'), may hold values from -0.4375 to 0.4375
- key_weight: float32 [64, 64], replicated, may hold values from -0.75 to 0.75
- value_weight: float32 [64, 64], replicated, may hold values from -0.75 to 0.75
- cell_query: float32 [64, 4096], P(None, 'cell'), may hold values from -6 to 6
- quality: float32 [2, 8192], P('sensor', 'cell'), may hold values from -4 to 302
- sample_cell: int32 [2, 8192], P('sensor', 'cell'), may hold values from 0 to 255
- live: int32 [2, 16], P('sensor', 'cell'), may hold values from 128 to 512
- neighbours: int32 [8, 4096], P(None, 'cell'), may hold values from 0 to 4095, as said below
- hp_weight: float32 [64, 576], replicated, may hold values from -0.25 to 0.25
Outputs:
- joined: float32 [64, 4096], P('sensor', 'cell')
The draws below stay inside these ranges and needn't reach their ends.
Inputs may be any that keep to these rules, and one draw needn't show every extreme that they name: `neighbours`: a cell range is a patch of 16 x 16 cells, local index row * 16 + column; every neighbour lies within 257 cells of its own cell, either in the cell's own range or in an adjacent one, and then in the first column of the next range or the last column of the previous range.
All inputs are finite; a program needn't handle non-finite values.
Results may differ from the reference program's by a relative error of at most 0.0003.
Values sent between devices are 32-bit elements; how exact they have to be, the bound alone decides.
No kernel may reach another device: no remote copies, remote signals or barrier semaphores. Data moves between devices by JAX's collectives and lax.ppermute only.
A program may use at most 64 MiB of HBM per device.

```python
import math
import jax
import jax.numpy as jnp
from jax import lax

C = 64
KT = 3
NB = 9
SIDE = 16
CELL_DEV = 256
SAMPLES_DEV = 512
RANGES = 16
SENSORS = 2
CELLS = 4096
SAMPLES = 8192


def cell_map(key):
    base = jax.random.fold_in(key, 11)
    first_key, second_key = jax.random.split(base)
    first = jax.random.randint(first_key, (SENSORS, SAMPLES), 0, CELL_DEV)
    second = jax.random.randint(second_key, (SENSORS, SAMPLES), 0, CELL_DEV)
    slots = jnp.arange(SAMPLES, dtype=jnp.int32)
    position = slots % SAMPLES_DEV
    offset = jnp.minimum(first, second)
    offset = jnp.where((position == 0)[None, :], 0, offset)
    offset = jnp.where((position == SAMPLES_DEV - 1)[None, :], CELL_DEV - 1, offset)
    return offset.astype(jnp.int32)


def draw_sample_cell(key, part):
    return cell_map(key)


def draw_quality(key, part):
    base = jax.random.fold_in(key, 23)
    normal_key = jax.random.fold_in(base, 3)
    return jnp.clip(jax.random.normal(normal_key, (SENSORS, SAMPLES), jnp.float32), -4.0, 4.0)


def draw_live(key, part):
    base = jax.random.fold_in(key, 37)
    count_key, top_key, step_key = jax.random.split(base, 3)
    lowest = SAMPLES_DEV // 4
    counts = jax.random.randint(count_key, (SENSORS, RANGES), lowest, SAMPLES_DEV + 1)
    top_col = jax.random.randint(top_key, (SENSORS, 1), 0, RANGES)
    low_col = (top_col + 1 + jax.random.randint(step_key, (SENSORS, 1), 0, RANGES - 1)) % RANGES
    column = jnp.arange(RANGES, dtype=jnp.int32)[None, :]
    counts = jnp.where(column == top_col, SAMPLES_DEV, counts)
    counts = jnp.where(column == low_col, lowest, counts)
    return counts.astype(jnp.int32)


def draw_neighbours(key, part):
    base = jax.random.fold_in(key, 53)
    cells = jnp.arange(CELLS, dtype=jnp.int32)
    range_id = cells // CELL_DEV
    local = cells % CELL_DEV
    row = local // SIDE
    column = local % SIDE
    row_steps = jnp.array([-1, -1, -1, 0, 0, 1, 1, 1], dtype=jnp.int32)
    col_steps = jnp.array([-1, 0, 1, -1, 1, -1, 0, 1], dtype=jnp.int32)
    scores = jax.random.randint(base, (NB - 1, CELLS), 0, 1 << 20) * 8 + jnp.arange(NB - 1, dtype=jnp.int32)[:, None]
    order = jnp.argsort(scores, axis=0).astype(jnp.int32)
    drow = row_steps[order]
    dcol = col_steps[order]
    new_row = jnp.clip(row[None, :] + drow, 0, SIDE - 1)
    raw_col = column[None, :] + dcol
    move = (raw_col >= SIDE).astype(jnp.int32) - (raw_col < 0).astype(jnp.int32)
    new_range = range_id[None, :] + move
    outside = (new_range < 0) | (new_range >= RANGES)
    new_col = jnp.where(outside, jnp.clip(raw_col, 0, SIDE - 1), raw_col - move * SIDE)
    new_range = jnp.where(outside, range_id[None, :], new_range)
    return (new_range * CELL_DEV + new_row * SIDE + new_col).astype(jnp.int32)


def block_scale(own_key, extent, pieces, least, top_value):
    def one(axis_at, parts):
        draws = jax.random.uniform(jax.random.fold_in(jax.random.fold_in(own_key, 6), axis_at), (parts,), jnp.float32, least / len(pieces), top_value / len(pieces))
        return jnp.repeat(jnp.exp(draws), extent[axis_at] // parts).reshape((-1,) + (1,) * (len(extent) - axis_at - 1))

    gain = one(*pieces[0])
    for cut in pieces[1:]:
        gain = gain * one(*cut)
    return gain


def gaussian(own_key, shape, spread, reach, shards=(), kind=jnp.bfloat16):
    values = spread * jax.random.normal(own_key, shape, jnp.float32)
    if shards:
        values = values * block_scale(own_key, shape, shards, -0.22, 0.18)
    return jnp.clip(values, -reach, reach).astype(kind)


def setup_inputs(seed: int = 0) -> dict:
    splits = jax.random.split(jax.random.key(seed), 11)
    swath = gaussian(splits[0], (SENSORS, C, SAMPLES), 1.0, 6.0, ((0, 2), (2, 16)), jnp.float32)
    enc_weight = gaussian(splits[1], (SENSORS, C, KT * C), (KT * C) ** -0.5, 0.4375, ((0, 2),), jnp.float32)
    key_weight = gaussian(splits[2], (C, C), C ** -0.5, 0.75, (), jnp.float32)
    value_weight = gaussian(splits[3], (C, C), C ** -0.5, 0.75, (), jnp.float32)
    cell_query = gaussian(splits[4], (C, CELLS), 1.0, 6.0, ((1, 16),), jnp.float32)
    quality = draw_quality(jax.random.fold_in(splits[10], 71), 0)
    sample_cell = draw_sample_cell(jax.random.fold_in(splits[10], 71), 0)
    live = draw_live(jax.random.fold_in(splits[10], 71), 0)
    neighbours = draw_neighbours(jax.random.fold_in(splits[10], 71), 0)
    hp_weight = gaussian(splits[9], (C, NB * C), (NB * C) ** -0.5, 0.25, (), jnp.float32)
    return dict(swath=swath, enc_weight=enc_weight, key_weight=key_weight, value_weight=value_weight, cell_query=cell_query, quality=quality, sample_cell=sample_cell, live=live, neighbours=neighbours, hp_weight=hp_weight)


floor_value = -1e+30
highest = lax.Precision.HIGHEST

def reference(swath, enc_weight, key_weight, value_weight, cell_query, quality, sample_cell, live, neighbours, hp_weight):
    inv_root = 1.0 / math.sqrt(C)
    slots = jnp.arange(SAMPLES, dtype=jnp.int32)
    position = slots % SAMPLES_DEV
    range_of = slots // SAMPLES_DEV
    range_first = (range_of * CELL_DEV).astype(jnp.int32)
    run_peak = jnp.full((CELLS,), floor_value, dtype=jnp.float32)
    run_total = jnp.zeros((CELLS,), dtype=jnp.float32)
    run_sum = jnp.zeros((C, CELLS), dtype=jnp.float32)
    for sensor_index in range(SENSORS):
        signal = swath[sensor_index]
        padded = jnp.pad(signal, ((0, 0), (2, 0)))
        stacked = jnp.concatenate([padded[:, 0:SAMPLES], padded[:, 1:SAMPLES + 1], padded[:, 2:SAMPLES + 2]], axis=0)
        encoded = jax.nn.gelu(jnp.dot(enc_weight[sensor_index], stacked, precision=highest), approximate=False)
        key_rows = jnp.dot(key_weight, encoded, precision=highest)
        value_rows = jnp.dot(value_weight, encoded, precision=highest)
        cell_ids = (sample_cell[sensor_index] + range_first).astype(jnp.int32)
        query_rows = jnp.take(cell_query, cell_ids, axis=1)
        score = lax.optimization_barrier(jnp.sum(query_rows * key_rows, axis=0)) * inv_root + quality[sensor_index]
        valid = position < live[sensor_index][range_of]
        peak = jnp.maximum(jax.ops.segment_max(jnp.where(valid, score, -jnp.inf), cell_ids, CELLS), floor_value)
        weights_exp = jnp.where(valid, jnp.exp(score - peak[cell_ids]), 0.0)
        total = jax.ops.segment_sum(weights_exp, cell_ids, CELLS)
        summed = jax.ops.segment_sum((value_rows * weights_exp[None, :]).T, cell_ids, CELLS).T
        joint = jnp.maximum(run_peak, peak)
        old_factor = jnp.exp(run_peak - joint)
        new_factor = jnp.exp(peak - joint)
        run_total = run_total * old_factor + total * new_factor
        run_sum = run_sum * old_factor[None, :] + summed * new_factor[None, :]
        run_peak = joint
    prior_key = jnp.dot(key_weight, cell_query, precision=highest)
    prior_value = jnp.dot(value_weight, cell_query, precision=highest)
    prior_score = lax.optimization_barrier(jnp.sum(cell_query * prior_key, axis=0)) * inv_root
    joint = jnp.maximum(run_peak, prior_score)
    pool_factor = jnp.exp(run_peak - joint)
    prior_factor = jnp.exp(prior_score - joint)
    pooled = (run_sum * pool_factor[None, :] + prior_value * prior_factor[None, :]) / (run_total * pool_factor + prior_factor)[None, :]
    hp_cube = hp_weight.reshape(C, NB, C)
    joined = jnp.dot(hp_cube[:, 0, :], pooled, precision=highest)
    for slot_index in range(NB - 1):
        joined = joined + jnp.dot(hp_cube[:, slot_index + 1, :], jnp.take(pooled, neighbours[slot_index], axis=1), precision=highest)
    return joined
```

```python
import functools
import math

import jax
import jax.numpy as jnp
from jax import lax
from jax.experimental import pallas as pl
from jax.experimental.pallas import tpu as pltpu
from jax.sharding import PartitionSpec as P

FLOOR = -1e30
LANES = 128
ROWS = 8
EXACT = lax.Precision.HIGHEST
CLOSE = lax.Precision.HIGH


def dot(left, right, contract, precision=EXACT):
    return lax.dot_general(
        left,
        right,
        (contract, ((), ())),
        precision=precision,
        preferred_element_type=jnp.float32,
    )


NN = ((1,), (0,))
NT = ((1,), (1,))
TN = ((0,), (0,))


def gelu(x):
    return 0.5 * x * (1.0 + lax.erf(x * math.sqrt(0.5)))


def column_of(row):
    return jnp.transpose(jnp.broadcast_to(row, (LANES, row.shape[1])))


def masked_scores(encoded, key_query, cell_row, quality_row):
    cells = key_query.shape[1]
    cell_column = column_of(cell_row)
    quality_column = column_of(quality_row)
    score = dot(encoded, key_query, TN)
    lane = lax.broadcasted_iota(jnp.int32, cell_column.shape, 1).astype(jnp.float32)
    parts = []
    for start in range(0, cells, LANES):
        mine = cell_column == lane + float(start)
        part = score[:, start : start + LANES] + quality_column
        parts.append(jnp.where(mine, part, -jnp.inf))
    return jnp.concatenate(parts, axis=1)


def stats_block(weighted, total, peak):
    place = lax.broadcasted_iota(jnp.int32, (ROWS, total.shape[1]), 0)
    tail = jnp.where(place == 0, total, jnp.where(place == 1, peak, 0.0))
    return jnp.concatenate([weighted, tail], axis=0)


def tail_kernel(swath_ref, out_ref):
    last = swath_ref[0]
    row = lax.broadcasted_iota(jnp.int32, (ROWS, LANES), 0)
    lane = lax.broadcasted_iota(jnp.int32, (ROWS, LANES), 1)
    first = ((lane == LANES - 2 + row) & (row < 2)).astype(jnp.float32)
    second = ((lane == LANES - 1) & (row == 0)).astype(jnp.float32)
    out_ref[...] = jnp.concatenate([dot(first, last, NT), dot(second, last, NT)], axis=1)


def prepare_kernel(
    swath_ref,
    enc_ref,
    key_ref,
    value_ref,
    query_ref,
    quality_ref,
    cell_ref,
    live_ref,
    near_ref,
    hp_ref,
    first_ref,
    kq_ref,
    rest_ref,
    hpv_ref,
    code_ref,
):
    sensor = lax.axis_index("sensor")
    cell = lax.axis_index("cell")
    channels, slots = swath_ref.shape[1:]
    cells = query_ref.shape[1]
    out_rows = hpv_ref.shape[0] * channels // hp_ref.shape[1]

    signal = swath_ref[0]
    one = jnp.concatenate([jnp.zeros((channels, 1), jnp.float32), signal[:, : slots - 1]], axis=1)
    two = jnp.concatenate([jnp.zeros((channels, 2), jnp.float32), signal[:, : slots - 2]], axis=1)
    stacked = jnp.concatenate([two, one, signal], axis=0)
    before = dot(enc_ref[0], stacked, NN)
    first_ref[...] = before[:, :LANES]
    encoded = gelu(before[:, LANES:])

    query = query_ref[...]
    key_query = dot(key_ref[...], query, TN) * (1.0 / math.sqrt(channels))
    kq_ref[...] = key_query
    own_score = jnp.sum(query * key_query, axis=0, keepdims=True)
    own_score = jnp.where(sensor == 0, own_score, -jnp.inf)

    place = lax.broadcasted_iota(jnp.int32, (1, slots), 1)
    cell_row = jnp.where(place < live_ref[0, 0], cell_ref[...], -1).astype(jnp.float32)
    quality_row = quality_ref[...]
    scores = [
        masked_scores(
            encoded[:, start - LANES : start],
            key_query,
            cell_row[:, start : start + LANES],
            quality_row[:, start : start + LANES],
        )
        for start in range(LANES, slots, LANES)
    ]
    peak = jnp.maximum(own_score, FLOOR)
    for score in scores:
        peak = jnp.maximum(peak, jnp.max(score, axis=0, keepdims=True))
    weight = jnp.exp(own_score - peak)
    weighted = query * weight
    weights = jnp.exp(jnp.concatenate(scores, axis=0) - peak)
    total = weight + jnp.sum(weights, axis=0, keepdims=True)
    weighted = weighted + dot(encoded, weights, NN)
    rest_ref[...] = stats_block(weighted, total, peak)

    own_hp = hp_ref[pl.ds(pl.multiple_of(sensor * out_rows, ROWS), out_rows), :]
    value = value_ref[...]
    for k in range(hp_ref.shape[1] // channels):
        part = dot(own_hp[:, k * channels : (k + 1) * channels], value, NN)
        hpv_ref[k * out_rows : (k + 1) * out_rows, :] = part

    side = math.isqrt(cells)
    shift = side.bit_length() - 1
    odd = lax.rem(cell, 2)
    offset = near_ref[...] - cell * cells
    after = cells + odd * side + lax.shift_right_arithmetic(offset - cells, shift)
    ahead = cells + (1 - odd) * side + lax.shift_right_arithmetic(offset + cells, shift)
    code_ref[...] = jnp.where(offset < 0, ahead, jnp.where(offset < cells, offset, after))


def pool_kernel(
    enc_ref,
    quality_ref,
    cell_ref,
    live_ref,
    first_ref,
    kq_ref,
    rest_ref,
    tail_a_ref,
    tail_b_ref,
    stats_ref,
    pack_a_ref,
    pack_b_ref,
):
    cell = lax.axis_index("cell")
    channels, cells = kq_ref.shape
    odd = lax.rem(cell, 2)
    tail = jnp.where(odd == 1, tail_a_ref[...], tail_b_ref[...])
    tail = jnp.where(cell == 0, 0.0, tail)
    tail = jnp.concatenate([tail, jnp.zeros((LANES - ROWS, LANES), jnp.float32)], axis=0)
    before = first_ref[...] + dot(enc_ref[0, :, : 2 * channels], tail, NT)
    encoded = gelu(before)
    place = lax.broadcasted_iota(jnp.int32, (1, LANES), 1)
    cell_row = jnp.where(place < live_ref[0, 0], cell_ref[:, :LANES], -1).astype(jnp.float32)
    score = masked_scores(encoded, kq_ref[...], cell_row, quality_ref[:, :LANES])
    rest_peak = rest_ref[channels + 1 : channels + 2, :]
    peak = jnp.maximum(rest_peak, jnp.max(score, axis=0, keepdims=True))
    factor = jnp.exp(rest_peak - peak)
    weights = jnp.exp(score - peak)
    total = rest_ref[channels : channels + 1, :] * factor + jnp.sum(weights, axis=0, keepdims=True)
    weighted = rest_ref[:channels, :] * factor + dot(encoded, weights, NN)
    stats = stats_block(weighted, total, peak)
    stats_ref[...] = stats
    side = math.isqrt(cells)
    row = lax.broadcasted_iota(jnp.int32, (2 * side, cells), 0)
    lane = lax.broadcasted_iota(jnp.int32, (2 * side, cells), 1)
    right, left = row * side + side - 1, (row - side) * side
    swapped_right, swapped_left = (row - side) * side + side - 1, row * side
    top = row < side
    pick = jnp.where(
        odd == 1,
        jnp.where(top, swapped_left, swapped_right),
        jnp.where(top, right, left),
    )
    packs = dot((lane == pick).astype(jnp.float32), stats, NT)
    wide = jnp.zeros((2 * side, LANES - packs.shape[1]), jnp.float32)
    packs = jnp.concatenate([packs, wide], axis=1)
    pack_a_ref[...] = packs[:side]
    pack_b_ref[...] = packs[side:]


def combine_kernel(own_ref, other_ref, out_ref):
    channels = own_ref.shape[0] - ROWS
    first, second = own_ref[...], other_ref[...]
    peak = jnp.maximum(first[channels + 1 : channels + 2], second[channels + 1 : channels + 2])
    first_factor = jnp.exp(first[channels + 1 : channels + 2] - peak)
    second_factor = jnp.exp(second[channels + 1 : channels + 2] - peak)
    both = first[: channels + 1] * first_factor + second[: channels + 1] * second_factor
    out_ref[...] = stats_block(both[:channels], both[channels : channels + 1], peak)


def mean_of(channels, first, second):
    first_peak, second_peak = (v[channels + 1 : channels + 2] for v in (first, second))
    peak = jnp.maximum(first_peak, second_peak)
    first_factor = jnp.exp(first_peak - peak)
    second_factor = jnp.exp(second_peak - peak)
    total = (
        first[channels : channels + 1] * first_factor
        + second[channels : channels + 1] * second_factor
    )
    return first[:channels] * (first_factor / total) + second[:channels] * (second_factor / total)


def mix_kernel(
    channels,
    own_ref,
    other_ref,
    own_a_ref,
    other_a_ref,
    own_b_ref,
    other_b_ref,
    hpv_ref,
    code_ref,
    out_ref,
):
    out_rows, cells = out_ref.shape
    pooled = mean_of(channels, own_ref[...], other_ref[...])
    halo = jnp.concatenate(
        [
            halo_mean(channels, own_a_ref[...], other_a_ref[...]),
            halo_mean(channels, own_b_ref[...], other_b_ref[...]),
        ],
        axis=0,
    )
    wide = jnp.zeros((LANES - halo.shape[0], channels), jnp.float32)
    halo = jnp.concatenate([halo, wide], axis=0)
    hpv = hpv_ref[...]
    mixed = dot(hpv, pooled, NN, CLOSE)
    edge = dot(hpv, halo, NT, CLOSE)
    sources = [mixed[:, start : start + LANES] for start in range(0, cells, LANES)] + [edge]
    for start in range(0, cells, LANES):
        total = mixed[:out_rows, start : start + LANES]
        for k in range(code_ref.shape[0]):
            code = jnp.broadcast_to(code_ref[k : k + 1, start : start + LANES], total.shape)
            lane = lax.bitwise_and(code, LANES - 1)
            rows = slice((k + 1) * out_rows, (k + 2) * out_rows)
            taken = None
            for i, source in enumerate(sources):
                here = jnp.take_along_axis(source[rows], lane, axis=1, mode="promise_in_bounds")
                taken = here if taken is None else jnp.where(code >= i * LANES, here, taken)
            total = total + taken
        out_ref[:, start : start + LANES] = total


def halo_mean(channels, first, second):
    first_peak, second_peak = (v[:, channels + 1 : channels + 2] for v in (first, second))
    peak = jnp.maximum(first_peak, second_peak)
    first_factor = jnp.exp(first_peak - peak)
    second_factor = jnp.exp(second_peak - peak)
    total = (
        first[:, channels : channels + 1] * first_factor
        + second[:, channels : channels + 1] * second_factor
    )
    return first[:, :channels] * (first_factor / total) + second[:, :channels] * (
        second_factor / total
    )


def shape_of(*shape, dtype=jnp.float32):
    return jax.ShapeDtypeStruct(shape, dtype)


def swaps(sensors, cells):
    def listed(partner):
        return [(s * cells + c, partner(s, c)) for s in range(sensors) for c in range(cells)]

    def near(flip):
        return listed(lambda s, c: (s ^ flip) * cells + (c ^ 1))

    def far(flip):
        def partner(s, c):
            if c in (0, cells - 1):
                return (s ^ 1) * cells + c
            return (s ^ flip) * cells + ((c - 1) ^ 1) + 1

        return listed(partner)

    def across(flip):
        return listed(lambda s, c: (s ^ flip) * cells + c)

    return near, far, across


def on_device(
    swath,
    enc_weight,
    key_weight,
    value_weight,
    cell_query,
    quality,
    sample_cell,
    live,
    neighbours,
    hp_weight,
):
    sensors, ranges = lax.axis_size("sensor"), lax.axis_size("cell")
    channels, slots = swath.shape[1:]
    cells = cell_query.shape[1]
    side = math.isqrt(cells)
    out_rows = channels // sensors
    stencil = hp_weight.shape[1] // channels
    vmem = pl.BlockSpec(memory_space=pltpu.VMEM)
    smem = pl.BlockSpec(memory_space=pltpu.SMEM)
    axes = ("sensor", "cell")
    near, far, across = swaps(sensors, ranges)

    tail = pl.pallas_call(
        tail_kernel,
        grid=(1,),
        in_specs=[pl.BlockSpec((1, channels, LANES), lambda i: (0, 0, slots // LANES - 1))],
        out_specs=pl.BlockSpec((ROWS, LANES), lambda i: (0, 0)),
        out_shape=shape_of(ROWS, LANES),
    )(swath)
    tail_a = lax.ppermute(tail, axes, near(0))
    tail_b = lax.ppermute(tail, axes, far(0))

    first, key_query, rest, hpv, code = pl.pallas_call(
        prepare_kernel,
        in_specs=[vmem] * 7 + [smem] + [vmem] * 2,
        out_specs=[vmem] * 5,
        out_shape=[
            shape_of(channels, LANES),
            shape_of(channels, cells),
            shape_of(channels + ROWS, cells),
            shape_of(stencil * out_rows, channels),
            shape_of(*neighbours.shape, dtype=jnp.int32),
        ],
        cost_estimate=pl.CostEstimate(
            flops=200_000_000, bytes_accessed=800_000, transcendentals=200_000
        ),
    )(
        swath,
        enc_weight,
        key_weight,
        value_weight,
        cell_query,
        quality,
        sample_cell,
        live,
        neighbours,
        hp_weight,
    )

    stats, pack_a, pack_b = pl.pallas_call(
        pool_kernel,
        in_specs=[vmem] * 3 + [smem] + [vmem] * 5,
        out_specs=[vmem] * 3,
        out_shape=[
            shape_of(channels + ROWS, cells),
            shape_of(side, LANES),
            shape_of(side, LANES),
        ],
    )(enc_weight, quality, sample_cell, live, first, key_query, rest, tail_a, tail_b)

    flip = 1
    while flip * 2 < sensors:
        others = [lax.ppermute(v, axes, across(flip)) for v in (stats, pack_a, pack_b)]
        stats = pl.pallas_call(
            combine_kernel,
            in_specs=[vmem] * 2,
            out_specs=vmem,
            out_shape=shape_of(channels + ROWS, cells),
        )(stats, others[0])
        pack_a, pack_b = [
            pl.pallas_call(
                functools.partial(combine_packs, channels),
                in_specs=[vmem] * 2,
                out_specs=vmem,
                out_shape=shape_of(side, LANES),
            )(mine, other)
            for mine, other in ((pack_a, others[1]), (pack_b, others[2]))
        ]
        flip *= 2

    other = lax.ppermute(stats, axes, across(flip))
    own_a = lax.ppermute(pack_a, axes, near(0))
    own_b = lax.ppermute(pack_b, axes, far(0))
    other_a = lax.ppermute(pack_a, axes, near(flip))
    other_b = lax.ppermute(pack_b, axes, far(flip))

    return pl.pallas_call(
        functools.partial(mix_kernel, channels),
        in_specs=[vmem] * 8,
        out_specs=vmem,
        out_shape=shape_of(out_rows, cells),
    )(stats, other, own_a, other_a, own_b, other_b, hpv, code)


def combine_packs(channels, own_ref, other_ref, out_ref):
    first, second = own_ref[...], other_ref[...]
    first_peak, second_peak = (v[:, channels + 1 : channels + 2] for v in (first, second))
    peak = jnp.maximum(first_peak, second_peak)
    both = first * jnp.exp(first_peak - peak) + second * jnp.exp(second_peak - peak)
    lane = lax.broadcasted_iota(jnp.int32, both.shape, 1)
    out_ref[...] = jnp.where(lane == channels + 1, peak, both)


def solution(mesh):
    in_specs = (
        P("sensor", None, "cell"),
        P("sensor", None, None),
        P(),
        P(),
        P(None, "cell"),
        P("sensor", "cell"),
        P("sensor", "cell"),
        P("sensor", "cell"),
        P(None, "cell"),
        P(),
    )
    out_specs = P("sensor", "cell")
    return jax.shard_map(
        on_device, mesh=mesh, in_specs=in_specs, out_specs=out_specs, check_vma=False
    )
```

```python
import functools
import math

import jax
import jax.numpy as jnp
from jax import lax
from jax.experimental import pallas as pl
from jax.experimental.pallas import tpu as pltpu
from jax.sharding import PartitionSpec as P

FLOOR = -1e30
LANES = 128
ROWS = 8
EXACT = lax.Precision.HIGHEST
CLOSE = lax.Precision.HIGH
SMALL = pltpu.CompilerParams(vmem_limit_bytes=8 * 1024 * 1024)


def dot(left, right, contract, precision=EXACT):
    return lax.dot_general(
        left,
        right,
        (contract, ((), ())),
        precision=precision,
        preferred_element_type=jnp.float32,
    )


NN = ((1,), (0,))
NT = ((1,), (1,))
TN = ((0,), (0,))


def gelu(x):
    return 0.5 * x * (1.0 + lax.erf(x * math.sqrt(0.5)))


def column_of(row):
    return jnp.transpose(jnp.broadcast_to(row, (LANES, row.shape[1])))


def masked_scores(encoded, key_query, cell_row, quality_row):
    cells = key_query.shape[1]
    cell_column = column_of(cell_row)
    quality_column = column_of(quality_row)
    score = dot(encoded, key_query, TN)
    lane = lax.broadcasted_iota(jnp.int32, cell_column.shape, 1).astype(jnp.float32)
    parts = []
    for start in range(0, cells, LANES):
        mine = cell_column == lane + float(start)
        part = score[:, start : start + LANES] + quality_column
        parts.append(jnp.where(mine, part, -jnp.inf))
    return jnp.concatenate(parts, axis=1)


def stats_block(weighted, total, peak):
    place = lax.broadcasted_iota(jnp.int32, (ROWS, total.shape[1]), 0)
    tail = jnp.where(place == 0, total, jnp.where(place == 1, peak, 0.0))
    return jnp.concatenate([weighted, tail], axis=0)


def tail_kernel(swath_ref, out_ref):
    last = swath_ref[0]
    row = lax.broadcasted_iota(jnp.int32, (ROWS, LANES), 0)
    lane = lax.broadcasted_iota(jnp.int32, (ROWS, LANES), 1)
    first = ((lane == LANES - 2 + row) & (row < 2)).astype(jnp.float32)
    second = ((lane == LANES - 1) & (row == 0)).astype(jnp.float32)
    out_ref[...] = jnp.concatenate([dot(first, last, NT), dot(second, last, NT)], axis=1)


def prepare_kernel(
    swath_ref,
    enc_ref,
    key_ref,
    value_ref,
    query_ref,
    quality_ref,
    cell_ref,
    live_ref,
    near_ref,
    hp_ref,
    first_ref,
    kq_ref,
    rest_ref,
    hpv_ref,
    code_ref,
):
    sensor = lax.axis_index("sensor")
    cell = lax.axis_index("cell")
    channels, slots = swath_ref.shape[1:]
    cells = query_ref.shape[1]
    out_rows = hpv_ref.shape[0] * channels // hp_ref.shape[1]

    signal = swath_ref[0]
    one = jnp.concatenate([jnp.zeros((channels, 1), jnp.float32), signal[:, : slots - 1]], axis=1)
    two = jnp.concatenate([jnp.zeros((channels, 2), jnp.float32), signal[:, : slots - 2]], axis=1)
    stacked = jnp.concatenate([two, one, signal], axis=0)
    before = dot(enc_ref[0], stacked, NN)
    first_ref[...] = before[:, :LANES]
    encoded = gelu(before[:, LANES:])

    query = query_ref[...]
    key_query = dot(key_ref[...], query, TN) * (1.0 / math.sqrt(channels))
    kq_ref[...] = key_query
    own_score = jnp.sum(query * key_query, axis=0, keepdims=True)
    own_score = jnp.where(sensor == 0, own_score, -jnp.inf)

    place = lax.broadcasted_iota(jnp.int32, (1, slots), 1)
    cell_row = jnp.where(place < live_ref[0, 0], cell_ref[...], -1).astype(jnp.float32)
    quality_row = quality_ref[...]
    scores = [
        masked_scores(
            encoded[:, start - LANES : start],
            key_query,
            cell_row[:, start : start + LANES],
            quality_row[:, start : start + LANES],
        )
        for start in range(LANES, slots, LANES)
    ]
    peak = jnp.maximum(own_score, FLOOR)
    for score in scores:
        peak = jnp.maximum(peak, jnp.max(score, axis=0, keepdims=True))
    weight = jnp.exp(own_score - peak)
    weighted = query * weight
    weights = jnp.exp(jnp.concatenate(scores, axis=0) - peak)
    total = weight + jnp.sum(weights, axis=0, keepdims=True)
    weighted = weighted + dot(encoded, weights, NN)
    rest_ref[...] = stats_block(weighted, total, peak)

    own_hp = hp_ref[pl.ds(pl.multiple_of(sensor * out_rows, ROWS), out_rows), :]
    value = value_ref[...]
    for k in range(hp_ref.shape[1] // channels):
        part = dot(own_hp[:, k * channels : (k + 1) * channels], value, NN)
        hpv_ref[k * out_rows : (k + 1) * out_rows, :] = part

    side = math.isqrt(cells)
    shift = side.bit_length() - 1
    odd = lax.rem(cell, 2)
    offset = near_ref[...] - cell * cells
    after = cells + odd * side + lax.shift_right_arithmetic(offset - cells, shift)
    ahead = cells + (1 - odd) * side + lax.shift_right_arithmetic(offset + cells, shift)
    code_ref[...] = jnp.where(offset < 0, ahead, jnp.where(offset < cells, offset, after))


def pool_kernel(
    enc_ref,
    quality_ref,
    cell_ref,
    live_ref,
    first_ref,
    kq_ref,
    rest_ref,
    tail_a_ref,
    tail_b_ref,
    stats_ref,
    pack_a_ref,
    pack_b_ref,
):
    cell = lax.axis_index("cell")
    channels, cells = kq_ref.shape
    odd = lax.rem(cell, 2)
    tail = jnp.where(odd == 1, tail_a_ref[...], tail_b_ref[...])
    tail = jnp.where(cell == 0, 0.0, tail)
    tail = jnp.concatenate([tail, jnp.zeros((LANES - ROWS, LANES), jnp.float32)], axis=0)
    before = first_ref[...] + dot(enc_ref[0, :, : 2 * channels], tail, NT)
    encoded = gelu(before)
    place = lax.broadcasted_iota(jnp.int32, (1, LANES), 1)
    cell_row = jnp.where(place < live_ref[0, 0], cell_ref[:, :LANES], -1).astype(jnp.float32)
    score = masked_scores(encoded, kq_ref[...], cell_row, quality_ref[:, :LANES])
    rest_peak = rest_ref[channels + 1 : channels + 2, :]
    peak = jnp.maximum(rest_peak, jnp.max(score, axis=0, keepdims=True))
    factor = jnp.exp(rest_peak - peak)
    weights = jnp.exp(score - peak)
    total = rest_ref[channels : channels + 1, :] * factor + jnp.sum(weights, axis=0, keepdims=True)
    weighted = rest_ref[:channels, :] * factor + dot(encoded, weights, NN)
    stats = stats_block(weighted, total, peak)
    stats_ref[...] = stats
    side = math.isqrt(cells)
    row = lax.broadcasted_iota(jnp.int32, (2 * side, cells), 0)
    lane = lax.broadcasted_iota(jnp.int32, (2 * side, cells), 1)
    right, left = row * side + side - 1, (row - side) * side
    swapped_right, swapped_left = (row - side) * side + side - 1, row * side
    top = row < side
    pick = jnp.where(
        odd == 1,
        jnp.where(top, swapped_left, swapped_right),
        jnp.where(top, right, left),
    )
    packs = dot((lane == pick).astype(jnp.float32), stats, NT)
    wide = jnp.zeros((2 * side, LANES - packs.shape[1]), jnp.float32)
    packs = jnp.concatenate([packs, wide], axis=1)
    pack_a_ref[...] = packs[:side]
    pack_b_ref[...] = packs[side:]


def combine_kernel(own_ref, other_ref, out_ref):
    channels = own_ref.shape[0] - ROWS
    first, second = own_ref[...], other_ref[...]
    peak = jnp.maximum(first[channels + 1 : channels + 2], second[channels + 1 : channels + 2])
    first_factor = jnp.exp(first[channels + 1 : channels + 2] - peak)
    second_factor = jnp.exp(second[channels + 1 : channels + 2] - peak)
    both = first[: channels + 1] * first_factor + second[: channels + 1] * second_factor
    out_ref[...] = stats_block(both[:channels], both[channels : channels + 1], peak)


def mean_of(channels, first, second):
    first_peak, second_peak = (v[channels + 1 : channels + 2] for v in (first, second))
    peak = jnp.maximum(first_peak, second_peak)
    first_factor = jnp.exp(first_peak - peak)
    second_factor = jnp.exp(second_peak - peak)
    total = (
        first[channels : channels + 1] * first_factor
        + second[channels : channels + 1] * second_factor
    )
    return first[:channels] * (first_factor / total) + second[:channels] * (second_factor / total)


def mix_kernel(
    channels,
    own_ref,
    other_ref,
    own_a_ref,
    other_a_ref,
    own_b_ref,
    other_b_ref,
    hpv_ref,
    code_ref,
    out_ref,
):
    out_rows, cells = out_ref.shape
    pooled = mean_of(channels, own_ref[...], other_ref[...])
    halo = jnp.concatenate(
        [
            halo_mean(channels, own_a_ref[...], other_a_ref[...]),
            halo_mean(channels, own_b_ref[...], other_b_ref[...]),
        ],
        axis=0,
    )
    wide = jnp.zeros((LANES - halo.shape[0], channels), jnp.float32)
    halo = jnp.concatenate([halo, wide], axis=0)
    hpv = hpv_ref[...]
    mixed = dot(hpv, pooled, NN, CLOSE)
    edge = dot(hpv, halo, NT, CLOSE)
    sources = [mixed[:, start : start + LANES] for start in range(0, cells, LANES)] + [edge]
    for start in range(0, cells, LANES):
        total = mixed[:out_rows, start : start + LANES]
        for k in range(code_ref.shape[0]):
            code = jnp.broadcast_to(code_ref[k : k + 1, start : start + LANES], total.shape)
            lane = lax.bitwise_and(code, LANES - 1)
            rows = slice((k + 1) * out_rows, (k + 2) * out_rows)
            taken = None
            for i, source in enumerate(sources):
                here = jnp.take_along_axis(source[rows], lane, axis=1, mode="promise_in_bounds")
                taken = here if taken is None else jnp.where(code >= i * LANES, here, taken)
            total = total + taken
        out_ref[:, start : start + LANES] = total


def halo_mean(channels, first, second):
    first_peak, second_peak = (v[:, channels + 1 : channels + 2] for v in (first, second))
    peak = jnp.maximum(first_peak, second_peak)
    first_factor = jnp.exp(first_peak - peak)
    second_factor = jnp.exp(second_peak - peak)
    total = (
        first[:, channels : channels + 1] * first_factor
        + second[:, channels : channels + 1] * second_factor
    )
    return first[:, :channels] * (first_factor / total) + second[:, :channels] * (
        second_factor / total
    )


def shape_of(*shape, dtype=jnp.float32):
    return jax.ShapeDtypeStruct(shape, dtype)


def swaps(sensors, cells):
    def listed(partner):
        return [(s * cells + c, partner(s, c)) for s in range(sensors) for c in range(cells)]

    def near(flip):
        return listed(lambda s, c: (s ^ flip) * cells + (c ^ 1))

    def far(flip):
        def partner(s, c):
            if c in (0, cells - 1):
                return (s ^ 1) * cells + c
            return (s ^ flip) * cells + ((c - 1) ^ 1) + 1

        return listed(partner)

    def across(flip):
        return listed(lambda s, c: (s ^ flip) * cells + c)

    return near, far, across


def on_device(
    swath,
    enc_weight,
    key_weight,
    value_weight,
    cell_query,
    quality,
    sample_cell,
    live,
    neighbours,
    hp_weight,
):
    sensors, ranges = lax.axis_size("sensor"), lax.axis_size("cell")
    channels, slots = swath.shape[1:]
    cells = cell_query.shape[1]
    side = math.isqrt(cells)
    out_rows = channels // sensors
    stencil = hp_weight.shape[1] // channels
    vmem = pl.BlockSpec(memory_space=pltpu.VMEM)
    smem = pl.BlockSpec(memory_space=pltpu.SMEM)
    axes = ("sensor", "cell")
    near, far, across = swaps(sensors, ranges)

    tail = pl.pallas_call(
        tail_kernel,
        grid=(1,),
        in_specs=[pl.BlockSpec((1, channels, LANES), lambda i: (0, 0, slots // LANES - 1))],
        out_specs=pl.BlockSpec((ROWS, LANES), lambda i: (0, 0)),
        out_shape=shape_of(ROWS, LANES),
        compiler_params=SMALL,
    )(swath)
    tail_a = lax.ppermute(tail, axes, near(0))
    tail_b = lax.ppermute(tail, axes, far(0))

    first, key_query, rest, hpv, code = pl.pallas_call(
        prepare_kernel,
        in_specs=[vmem] * 7 + [smem] + [vmem] * 2,
        out_specs=[vmem] * 5,
        out_shape=[
            shape_of(channels, LANES),
            shape_of(channels, cells),
            shape_of(channels + ROWS, cells),
            shape_of(stencil * out_rows, channels),
            shape_of(*neighbours.shape, dtype=jnp.int32),
        ],
        compiler_params=SMALL,
        cost_estimate=pl.CostEstimate(
            flops=200_000_000, bytes_accessed=800_000, transcendentals=200_000
        ),
    )(
        swath,
        enc_weight,
        key_weight,
        value_weight,
        cell_query,
        quality,
        sample_cell,
        live,
        neighbours,
        hp_weight,
    )

    stats, pack_a, pack_b = pl.pallas_call(
        pool_kernel,
        in_specs=[vmem] * 3 + [smem] + [vmem] * 5,
        out_specs=[vmem] * 3,
        out_shape=[
            shape_of(channels + ROWS, cells),
            shape_of(side, LANES),
            shape_of(side, LANES),
        ],
        compiler_params=SMALL,
    )(enc_weight, quality, sample_cell, live, first, key_query, rest, tail_a, tail_b)

    flip = 1
    while flip * 2 < sensors:
        others = [lax.ppermute(v, axes, across(flip)) for v in (stats, pack_a, pack_b)]
        stats = pl.pallas_call(
            combine_kernel,
            in_specs=[vmem] * 2,
            out_specs=vmem,
            out_shape=shape_of(channels + ROWS, cells),
            compiler_params=SMALL,
        )(stats, others[0])
        pack_a, pack_b = [
            pl.pallas_call(
                functools.partial(combine_packs, channels),
                in_specs=[vmem] * 2,
                out_specs=vmem,
                out_shape=shape_of(side, LANES),
                compiler_params=SMALL,
            )(mine, other)
            for mine, other in ((pack_a, others[1]), (pack_b, others[2]))
        ]
        flip *= 2

    other = lax.ppermute(stats, axes, across(flip))
    own_a = lax.ppermute(pack_a, axes, near(0))
    own_b = lax.ppermute(pack_b, axes, far(0))
    other_a = lax.ppermute(pack_a, axes, near(flip))
    other_b = lax.ppermute(pack_b, axes, far(flip))

    return pl.pallas_call(
        functools.partial(mix_kernel, channels),
        in_specs=[vmem] * 8,
        out_specs=vmem,
        out_shape=shape_of(out_rows, cells),
        compiler_params=SMALL,
    )(stats, other, own_a, other_a, own_b, other_b, hpv, code)


def combine_packs(channels, own_ref, other_ref, out_ref):
    first, second = own_ref[...], other_ref[...]
    first_peak, second_peak = (v[:, channels + 1 : channels + 2] for v in (first, second))
    peak = jnp.maximum(first_peak, second_peak)
    both = first * jnp.exp(first_peak - peak) + second * jnp.exp(second_peak - peak)
    lane = lax.broadcasted_iota(jnp.int32, both.shape, 1)
    out_ref[...] = jnp.where(lane == channels + 1, peak, both)


def solution(mesh):
    in_specs = (
        P("sensor", None, "cell"),
        P("sensor", None, None),
        P(),
        P(),
        P(None, "cell"),
        P("sensor", "cell"),
        P("sensor", "cell"),
        P("sensor", "cell"),
        P(None, "cell"),
        P(),
    )
    out_specs = P("sensor", "cell")
    return jax.shard_map(
        on_device, mesh=mesh, in_specs=in_specs, out_specs=out_specs, check_vma=False
    )
```

```python
import math

import jax
import jax.numpy as jnp
from jax import lax
from jax.experimental import pallas as pl
from jax.experimental.pallas import tpu as pltpu
from jax.sharding import PartitionSpec as P

FLOOR = -1e30
LANES = 128
ROWS = 8
LATE = 2
EXACT = lax.Precision.HIGHEST
CLOSE = lax.Precision.HIGH
NN = ((1,), (0,))
NT = ((1,), (1,))


def dot(left, right, contract, precision=EXACT):
    return lax.dot_general(
        left,
        right,
        (contract, ((), ())),
        precision=precision,
        preferred_element_type=jnp.float32,
    )


def iota(shape, dim):
    return lax.broadcasted_iota(jnp.int32, shape, dim)


def gelu(x):
    return 0.5 * x * (1.0 + lax.erf(x * math.sqrt(0.5)))


def widened(value, lanes=LANES):
    gap = jnp.zeros((value.shape[0], lanes - value.shape[1]), value.dtype)
    return jnp.concatenate([value, gap], axis=1)


def with_peak(block, peak, channels):
    return jnp.where(iota(block.shape, 1) == channels + 1, peak, block)


def merged(first, second, channels):
    first_peak, second_peak = (v[:, channels + 1 : channels + 2] for v in (first, second))
    peak = jnp.maximum(first_peak, second_peak)
    both = first * jnp.exp(first_peak - peak) + second * jnp.exp(second_peak - peak)
    return both, peak


def mean_of(first, second, channels):
    both, _ = merged(first, second, channels)
    return both / both[:, channels : channels + 1]


def with_late(rest, key_query, late, cell_ids, slot_cells, slot_quality, channels):
    peak = rest[:, channels + 1 : channels + 2]
    scores = []
    for j in range(LATE):
        score = jnp.sum(key_query * late[j : j + 1, :channels], axis=1, keepdims=True)
        score = score + slot_quality[:, j : j + 1]
        score = jnp.where(cell_ids == slot_cells[:, j : j + 1], score, -jnp.inf)
        peak = jnp.maximum(peak, score)
        scores.append(score)
    block = rest * jnp.exp(rest[:, channels + 1 : channels + 2] - peak)
    for j, score in enumerate(scores):
        block = block + jnp.exp(score - peak) * late[j : j + 1, :]
    return with_peak(block, peak, channels)


def load_kernel(*refs):
    count = (len(refs) - 2) // 2
    sources, targets, tail_ref, sems = refs[:count], refs[count:-2], refs[-2], refs[-1]
    copies = [
        pltpu.make_async_copy(source, target, sems.at[i])
        for i, (source, target) in enumerate(zip(sources, targets))
    ]
    for copy in copies:
        copy.start()
    copies[0].wait()
    swath_ref = targets[0]
    last = swath_ref[0, :, swath_ref.shape[2] - LANES :]
    row, lane = iota((ROWS, LANES), 0), iota((ROWS, LANES), 1)
    first = ((lane == LANES - 2 + row) & (row < 2)).astype(jnp.float32)
    second = ((lane == LANES - 1) & (row == 0)).astype(jnp.float32)
    tail_ref[...] = jnp.concatenate([dot(first, last, NT), dot(second, last, NT)], axis=1)
    for copy in copies[1:]:
        copy.wait()


def prepare_kernel(
    swath_ref,
    enc_ref,
    key_ref,
    query_ref,
    quality_ref,
    cell_ref,
    live_ref,
    late_ref,
    kq_ref,
    rest_ref,
    edge_kq_ref,
    edge_rest_ref,
    ids_ref,
):
    sensor = lax.axis_index("sensor")
    odd = lax.rem(lax.axis_index("cell"), 2)
    channels, slots = swath_ref.shape[1:]
    cells = query_ref.shape[1]
    side = math.isqrt(cells)

    signal = swath_ref[0]
    one = jnp.concatenate([jnp.zeros((channels, 1), jnp.float32), signal[:, : slots - 1]], axis=1)
    two = jnp.concatenate([jnp.zeros((channels, 2), jnp.float32), signal[:, : slots - 2]], axis=1)
    stacked = jnp.concatenate([two, one, signal], axis=0)
    before = dot(enc_ref[0], stacked, NN)
    late_ref[...] = jnp.transpose(before[:, :LANES])[:ROWS, :]
    encoded = gelu(before)

    query = jnp.transpose(query_ref[...])
    key_query = dot(query, key_ref[...], NN) * (1.0 / math.sqrt(channels))
    kq_ref[...] = key_query
    own_score = jnp.sum(query * key_query, axis=1, keepdims=True)
    own_score = jnp.where(sensor == 0, own_score, -jnp.inf)

    slot = iota((1, slots), 1)
    ids = jnp.where(slot < live_ref[0, 0], cell_ref[...], -1)
    ids_ref[...] = ids[:, :LANES]
    ids = jnp.where(slot < LATE, -1, ids)
    score = dot(key_query, encoded, NN) + quality_ref[...]
    score = jnp.where(iota((cells, slots), 0) == ids, score, -jnp.inf)
    peak = jnp.maximum(jnp.max(score, axis=1, keepdims=True), jnp.maximum(own_score, FLOOR))
    weights = jnp.exp(score - peak)
    place = iota((LANES - channels, slots), 0)
    tokens = jnp.concatenate([encoded, (place == 0).astype(jnp.float32)], axis=0)
    block = dot(weights, tokens, NT, CLOSE)
    own = widened(query)
    own = jnp.where(iota(own.shape, 1) == channels, 1.0, own)
    rest_ref[...] = with_peak(block + own * jnp.exp(own_score - peak), peak, channels)

    for ref, edge_ref in ((kq_ref, edge_kq_ref), (rest_ref, edge_rest_ref)):
        left = ref[pl.ds(0, side, stride=side), :]
        right = ref[pl.ds(side - 1, side, stride=side), :]
        edge_ref[:side, :] = jnp.where(odd == 1, left, right)
        edge_ref[side:, :] = jnp.where(odd == 1, right, left)


def edge_kernel(
    enc_ref,
    tail_a_ref,
    tail_b_ref,
    late_ref,
    ids_ref,
    quality_ref,
    kq_ref,
    rest_ref,
    edge_ref,
    tokens_ref,
):
    cell = lax.axis_index("cell")
    odd = lax.rem(cell, 2)
    channels = kq_ref.shape[1]
    side = rest_ref.shape[0] // 2
    tail = jnp.where(odd == 1, tail_a_ref[...], tail_b_ref[...])
    tail = jnp.where(cell == 0, 0.0, tail)
    before = late_ref[...] + dot(tail, enc_ref[0, :, : 2 * channels], NT)
    tokens = widened(gelu(before))
    tokens = jnp.where(iota(tokens.shape, 1) == channels, 1.0, tokens)
    tokens_ref[...] = tokens
    row = iota((2 * side, 1), 0)
    top = row < side
    at = jnp.where(top, row, row - side) * side
    at = at + jnp.where(top == (odd == 1), 0, side - 1)
    edge_ref[...] = with_late(
        rest_ref[...], kq_ref[...], tokens, at, ids_ref[...], quality_ref[:, :LANES], channels
    )


def pool_kernel(tokens_ref, ids_ref, quality_ref, kq_ref, rest_ref, stats_ref):
    cells, channels = kq_ref.shape
    stats_ref[...] = with_late(
        rest_ref[...],
        kq_ref[...],
        tokens_ref[...],
        iota((cells, 1), 0),
        ids_ref[...],
        quality_ref[:, :LANES],
        channels,
    )


def merge_kernel(channels, own_ref, other_ref, out_ref):
    both, peak = merged(own_ref[...], other_ref[...], channels)
    out_ref[...] = with_peak(both, peak, channels)


def weights_kernel(value_ref, near_ref, hp_ref, after_ref, hpv_ref, code_ref):
    del after_ref
    sensor = lax.axis_index("sensor")
    cell = lax.axis_index("cell")
    channels = value_ref.shape[0]
    cells = near_ref.shape[1]
    side = math.isqrt(cells)
    out_rows = hpv_ref.shape[0] * channels // hp_ref.shape[1]
    own_hp = hp_ref[pl.ds(pl.multiple_of(sensor * out_rows, ROWS), out_rows), :]
    value = value_ref[...]
    taps = [
        own_hp[:, k * channels : (k + 1) * channels] for k in range(hp_ref.shape[1] // channels)
    ]
    hpv_ref[...] = dot(jnp.concatenate(taps, axis=0), value, NN)

    shift = side.bit_length() - 1
    odd = lax.rem(cell, 2)
    offset = near_ref[...] - cell * cells
    after = cells + odd * side + lax.shift_right_arithmetic(offset - cells, shift)
    ahead = cells + (1 - odd) * side + lax.shift_right_arithmetic(offset + cells, shift)
    code_ref[...] = jnp.where(offset < 0, ahead, jnp.where(offset < cells, offset, after))


def edge_mean_kernel(channels, own_ref, other_ref, a_ref, b_ref):
    mean = mean_of(own_ref[...], other_ref[...], channels)
    side = a_ref.shape[0]
    a_ref[...] = mean[:side]
    b_ref[...] = mean[side:]


def picked(sources, first, code_ref, total, start, out_rows, base):
    for k in range(code_ref.shape[0]):
        code = jnp.broadcast_to(code_ref[k : k + 1, start : start + LANES], total.shape)
        lane = lax.bitwise_and(code, LANES - 1)
        rows = slice((k + base) * out_rows, (k + base + 1) * out_rows)
        taken = 0.0
        for i, source in enumerate(sources, first):
            here = jnp.take_along_axis(source[rows], lane, axis=1, mode="promise_in_bounds")
            taken = jnp.where(lax.shift_right_logical(code, 7) == i, here, taken)
        total = total + taken
    return total


def own_kernel(channels, own_ref, other_ref, hpv_ref, code_ref, out_ref):
    out_rows, cells = out_ref.shape
    mean = mean_of(own_ref[...], other_ref[...], channels)[:, :channels]
    mixed = dot(hpv_ref[...], mean, NT, CLOSE)
    sources = [mixed[:, start : start + LANES] for start in range(0, cells, LANES)]
    for i, start in enumerate(range(0, cells, LANES)):
        out_ref[:, start : start + LANES] = picked(
            sources, 0, code_ref, sources[i][:out_rows], start, out_rows, 1
        )


def halo_kernel(channels, b_ref, a_ref, partial_ref, hpv_ref, code_ref, out_ref):
    out_rows, cells = out_ref.shape
    halo = jnp.concatenate([a_ref[...], b_ref[...]], axis=0)[:, :channels]
    gap = jnp.zeros((LANES - halo.shape[0], channels), jnp.float32)
    halo = jnp.concatenate([halo, gap], axis=0)
    edge = dot(hpv_ref[out_rows:, :], halo, NT, CLOSE)
    for start in range(0, cells, LANES):
        out_ref[:, start : start + LANES] = picked(
            [edge],
            cells // LANES,
            code_ref,
            partial_ref[:, start : start + LANES],
            start,
            out_rows,
            0,
        )


def swaps(sensors, cells):
    def listed(partner):
        return [(s * cells + c, partner(s, c)) for s in range(sensors) for c in range(cells)]

    def far(s, c):
        if c in (0, cells - 1):
            return (s ^ 1) * cells + c
        return s * cells + ((c - 1) ^ 1) + 1

    near = listed(lambda s, c: s * cells + (c ^ 1))

    def across(flip):
        return listed(lambda s, c: (s ^ flip) * cells + c)

    return near, listed(far), across


def on_device(
    swath,
    enc_weight,
    key_weight,
    value_weight,
    cell_query,
    quality,
    sample_cell,
    live,
    neighbours,
    hp_weight,
):
    sensors, ranges = lax.axis_size("sensor"), lax.axis_size("cell")
    channels = swath.shape[1]
    cells = cell_query.shape[1]
    side = math.isqrt(cells)
    out_rows = channels // sensors
    stencil = hp_weight.shape[1] // channels
    vmem = pl.BlockSpec(memory_space=pltpu.VMEM)
    axes = ("sensor", "cell")
    near, far, across = swaps(sensors, ranges)

    def shape(*sizes, dtype=jnp.float32):
        return jax.ShapeDtypeStruct(sizes, dtype)

    def call(kernel, args, outs, cost=None, **more):
        single = not isinstance(outs, list)
        specs = dict(in_specs=[vmem] * len(args), out_specs=vmem if single else [vmem] * len(outs))
        specs.update(more)
        return pl.pallas_call(
            kernel,
            out_shape=outs,
            compiler_params=pltpu.CompilerParams(vmem_limit_bytes=8 * 1024 * 1024),
            cost_estimate=cost
            and pl.CostEstimate(flops=cost, bytes_accessed=cost // 100, transcendentals=0),
            **specs,
        )(*args)

    def bound(kernel):
        return lambda *refs: kernel(channels, *refs)

    args = [
        swath,
        enc_weight,
        key_weight,
        value_weight,
        cell_query,
        quality,
        sample_cell,
        neighbours,
        hp_weight,
    ]
    loaded = call(
        load_kernel,
        [pltpu.with_memory_space_constraint(a, pltpu.HBM) for a in args],
        [shape(*a.shape, dtype=a.dtype) for a in args] + [shape(ROWS, LANES)],
        in_specs=[pl.BlockSpec(memory_space=pltpu.HBM)] * len(args),
        scratch_shapes=[pltpu.SemaphoreType.DMA((len(args),))],
    )
    swath, enc_weight, key_weight, value_weight, cell_query = loaded[:5]
    quality, sample_cell, neighbours, hp_weight, tail = loaded[5:]
    tail_b = lax.ppermute(tail, axes, far)
    tail_a = lax.ppermute(tail, axes, near)

    late, key_query, rest, edge_kq, edge_rest, ids = call(
        prepare_kernel,
        [swath, enc_weight, key_weight, cell_query, quality, sample_cell, live],
        [
            shape(ROWS, channels),
            shape(cells, channels),
            shape(cells, LANES),
            shape(2 * side, channels),
            shape(2 * side, LANES),
            shape(1, LANES, dtype=jnp.int32),
        ],
        cost=200_000_000,
        in_specs=[vmem] * 6 + [pl.BlockSpec(memory_space=pltpu.SMEM)],
    )
    edge, tokens = call(
        edge_kernel,
        [enc_weight, tail_a, tail_b, late, ids, quality, edge_kq, edge_rest],
        [shape(2 * side, LANES), shape(ROWS, LANES)],
    )

    def merge(mine, other):
        return call(bound(merge_kernel), [mine, other], shape(*mine.shape))

    flip = 1
    stats = None
    while flip * 2 < sensors:
        if stats is None:
            stats = call(
                pool_kernel, [tokens, ids, quality, key_query, rest], shape(cells, LANES)
            )
        edge = merge(edge, lax.ppermute(edge, axes, across(flip)))
        stats = merge(stats, lax.ppermute(stats, axes, across(flip)))
        flip *= 2

    other_edge = lax.ppermute(edge, axes, across(flip))
    if stats is None:
        stats = call(pool_kernel, [tokens, ids, quality, key_query, rest], shape(cells, LANES), cost=100_000_000)
    other = lax.ppermute(stats, axes, across(flip))
    mean_a, mean_b = call(
        bound(edge_mean_kernel),
        [edge, other_edge],
        [shape(side, LANES), shape(side, LANES)],
        cost=10_000_000_000,
    )
    halo_b = lax.ppermute(mean_b, axes, far)
    halo_a = lax.ppermute(mean_a, axes, near)
    hpv, code = call(
        weights_kernel,
        [value_weight, neighbours, hp_weight, mean_a],
        [shape(stencil * out_rows, channels), shape(*neighbours.shape, dtype=jnp.int32)],
    )
    partial = call(
        bound(own_kernel), [stats, other, hpv, code], shape(out_rows, cells), cost=200_000_000
    )
    return call(
        bound(halo_kernel), [halo_b, halo_a, partial, hpv, code], shape(out_rows, cells)
    )


def solution(mesh):
    in_specs = (
        P("sensor", None, "cell"),
        P("sensor", None, None),
        P(),
        P(),
        P(None, "cell"),
        P("sensor", "cell"),
        P("sensor", "cell"),
        P("sensor", "cell"),
        P(None, "cell"),
        P(),
    )
    out_specs = P("sensor", "cell")
    return jax.shard_map(
        on_device, mesh=mesh, in_specs=in_specs, out_specs=out_specs, check_vma=False
    )
```

```python
import math

import jax
import jax.numpy as jnp
from jax import lax
from jax.experimental import pallas as pl
from jax.experimental.pallas import tpu as pltpu
from jax.sharding import PartitionSpec as P

FLOOR = -1e30
LANES = 128
ROWS = 8
LATE = 2
EXACT = lax.Precision.HIGHEST
CLOSE = lax.Precision.HIGH
NN = ((1,), (0,))
NT = ((1,), (1,))


def dot(left, right, contract, precision=EXACT):
    return lax.dot_general(
        left,
        right,
        (contract, ((), ())),
        precision=precision,
        preferred_element_type=jnp.float32,
    )


def iota(shape, dim):
    return lax.broadcasted_iota(jnp.int32, shape, dim)


def gelu(x):
    return 0.5 * x * (1.0 + lax.erf(x * math.sqrt(0.5)))


def widened(value, lanes=LANES):
    gap = jnp.zeros((value.shape[0], lanes - value.shape[1]), value.dtype)
    return jnp.concatenate([value, gap], axis=1)


def with_peak(block, peak, channels):
    return jnp.where(iota(block.shape, 1) == channels + 1, peak, block)


def merged(first, second, channels):
    first_peak, second_peak = (v[:, channels + 1 : channels + 2] for v in (first, second))
    peak = jnp.maximum(first_peak, second_peak)
    both = first * jnp.exp(first_peak - peak) + second * jnp.exp(second_peak - peak)
    return both, peak


def mean_of(first, second, channels):
    both, _ = merged(first, second, channels)
    return both / both[:, channels : channels + 1]


def with_late(rest, key_query, late, cell_ids, slot_cells, slot_quality, channels):
    peak = rest[:, channels + 1 : channels + 2]
    scores = []
    for j in range(LATE):
        score = jnp.sum(key_query * late[j : j + 1, :channels], axis=1, keepdims=True)
        score = score + slot_quality[:, j : j + 1]
        score = jnp.where(cell_ids == slot_cells[:, j : j + 1], score, -jnp.inf)
        peak = jnp.maximum(peak, score)
        scores.append(score)
    block = rest * jnp.exp(rest[:, channels + 1 : channels + 2] - peak)
    for j, score in enumerate(scores):
        block = block + jnp.exp(score - peak) * late[j : j + 1, :]
    return with_peak(block, peak, channels)


def load_kernel(*refs):
    count = (len(refs) - 2) // 2
    sources, targets, tail_ref, sems = refs[:count], refs[count:-2], refs[-2], refs[-1]
    copies = [
        pltpu.make_async_copy(source, target, sems.at[i])
        for i, (source, target) in enumerate(zip(sources, targets))
    ]
    for copy in copies:
        copy.start()
    copies[0].wait()
    swath_ref = targets[0]
    last = swath_ref[0, :, swath_ref.shape[2] - LANES :]
    row, lane = iota((ROWS, LANES), 0), iota((ROWS, LANES), 1)
    first = ((lane == LANES - 2 + row) & (row < 2)).astype(jnp.float32)
    second = ((lane == LANES - 1) & (row == 0)).astype(jnp.float32)
    tail_ref[...] = jnp.concatenate([dot(first, last, NT), dot(second, last, NT)], axis=1)
    for copy in copies[1:]:
        copy.wait()


def scored(key_query, encoded, quality, ids, cells):
    score = dot(key_query, encoded, NN) + quality
    return jnp.where(cells == ids, score, -jnp.inf)


def block_of(score, encoded, query, key_query, counted, channels):
    own_score = jnp.sum(query * key_query, axis=1, keepdims=True)
    own_score = jnp.where(counted, own_score, -jnp.inf)
    peak = jnp.maximum(jnp.max(score, axis=1, keepdims=True), jnp.maximum(own_score, FLOOR))
    weights = jnp.exp(score - peak)
    place = iota((LANES - channels, encoded.shape[1]), 0)
    tokens = jnp.concatenate([encoded, (place == 0).astype(jnp.float32)], axis=0)
    own = widened(query)
    own = jnp.where(iota(own.shape, 1) == channels, 1.0, own)
    block = dot(weights, tokens, NT, CLOSE) + own * jnp.exp(own_score - peak)
    return block, peak


def prepare_kernel(
    swath_ref,
    enc_ref,
    key_ref,
    query_ref,
    quality_ref,
    cell_ref,
    live_ref,
    late_ref,
    kq_ref,
    rest_ref,
    ids_ref,
):
    sensor = lax.axis_index("sensor")
    channels, slots = swath_ref.shape[1:]
    cells = query_ref.shape[1]

    signal = swath_ref[0]
    one = jnp.concatenate([jnp.zeros((channels, 1), jnp.float32), signal[:, : slots - 1]], axis=1)
    two = jnp.concatenate([jnp.zeros((channels, 2), jnp.float32), signal[:, : slots - 2]], axis=1)
    stacked = jnp.concatenate([two, one, signal], axis=0)
    before = dot(enc_ref[0], stacked, NN)
    late_ref[...] = jnp.transpose(before[:, :LANES])[:ROWS, :]
    encoded = gelu(before)

    query = jnp.transpose(query_ref[...])
    key_query = dot(query, key_ref[...], NN) * (1.0 / math.sqrt(channels))
    kq_ref[...] = key_query

    slot = iota((1, slots), 1)
    ids = jnp.where(slot < live_ref[0, 0], cell_ref[...], -1)
    ids_ref[...] = ids[:, :LANES]
    ids = jnp.where(slot < LATE, -1, ids)
    score = scored(key_query, encoded, quality_ref[...], ids, iota((cells, 1), 0))
    block, peak = block_of(score, encoded, query, key_query, sensor == 0, channels)
    rest_ref[...] = with_peak(block, peak, channels)


def pool_kernel(
    enc_ref,
    tail_b_ref,
    tail_a_ref,
    late_ref,
    ids_ref,
    quality_ref,
    kq_ref,
    rest_ref,
    stats_ref,
    pack_ref,
    block_ref,
):
    cell = lax.axis_index("cell")
    odd = lax.rem(cell, 2)
    cells, channels = kq_ref.shape
    side, half = pack_ref.shape[0], cells // 2
    tail = jnp.where(odd == 1, tail_a_ref[...], tail_b_ref[...])
    tail = jnp.where(cell == 0, 0.0, tail)
    before = late_ref[...] + dot(tail, enc_ref[0, :, : 2 * channels], NT)
    tokens = widened(gelu(before))
    tokens = jnp.where(iota(tokens.shape, 1) == channels, 1.0, tokens)
    block = with_late(
        rest_ref[...],
        kq_ref[...],
        tokens,
        iota((cells, 1), 0),
        ids_ref[...],
        quality_ref[:, :LANES],
        channels,
    )
    block_ref[...] = block
    stats_ref[:half, :] = jnp.concatenate(
        [block[:half, :channels], block[half:, :channels]], axis=1
    )
    total, peak = (block[:, channels + i : channels + i + 1] for i in range(2))
    lane = iota((half, LANES), 1)
    columns = jnp.where(lane == 0, total[:half], jnp.where(lane == 1, total[half:], 0.0))
    columns = jnp.where(lane == 2, peak[:half], jnp.where(lane == 3, peak[half:], columns))
    stats_ref[half:, :] = jnp.transpose(columns)[:ROWS, :]
    left = block_ref[pl.ds(0, side, stride=side), :]
    right = block_ref[pl.ds(side - 1, side, stride=side), :]
    pack_ref[...] = jnp.where(odd == 1, right, left)


def shares(first, second):
    peak = jnp.maximum(first[2:4], second[2:4])
    first_factor = jnp.exp(first[2:4] - peak)
    second_factor = jnp.exp(second[2:4] - peak)
    total = first[0:2] * first_factor + second[0:2] * second_factor
    return first_factor, second_factor, total, peak


def spread(row_pair, width):
    square = jnp.concatenate(
        [row_pair, jnp.zeros((LANES - row_pair.shape[0], row_pair.shape[1]), jnp.float32)], axis=0
    )
    columns = jnp.transpose(square)
    lane = iota((columns.shape[0], width), 1)
    return jnp.where(lane < width // 2, columns[:, 0:1], columns[:, 1:2])


def merge_pack_kernel(channels, own_ref, other_ref, out_ref):
    both, peak = merged(own_ref[...], other_ref[...], channels)
    out_ref[...] = with_peak(both, peak, channels)


def merge_kernel(own_ref, other_ref, out_ref):
    half = own_ref.shape[0] - ROWS
    first_factor, second_factor, total, peak = shares(own_ref[half:, :], other_ref[half:, :])
    first_sum = own_ref[:half, :] * spread(first_factor, LANES)
    out_ref[:half, :] = first_sum + other_ref[:half, :] * spread(second_factor, LANES)
    rest = jnp.zeros((ROWS - 4, total.shape[1]), jnp.float32)
    out_ref[half:, :] = jnp.concatenate([total, peak, rest], axis=0)


def halves(value):
    high = value.astype(jnp.bfloat16)
    return high, (value - high.astype(jnp.float32)).astype(jnp.bfloat16)


def weights_kernel(value_ref, near_ref, hp_ref, after_ref, hpv_ref, taps_ref, code_ref):
    del after_ref
    sensor = lax.axis_index("sensor")
    cell = lax.axis_index("cell")
    channels = value_ref.shape[0]
    cells = near_ref.shape[1]
    side = math.isqrt(cells)
    out_rows = hpv_ref.shape[0] * channels // hp_ref.shape[1]
    own_hp = hp_ref[pl.ds(pl.multiple_of(sensor * out_rows, ROWS), out_rows), :]
    value = value_ref[...]
    taps = [
        own_hp[:, k * channels : (k + 1) * channels] for k in range(hp_ref.shape[1] // channels)
    ]
    hpv = dot(jnp.concatenate(taps, axis=0), value, NN)
    hpv_ref[...] = hpv
    high, low = halves(hpv[out_rows:])
    taps_ref[...] = jnp.concatenate([high, high, low], axis=1)

    shift = side.bit_length() - 1
    odd = lax.rem(cell, 2)
    offset = near_ref[...] - cell * cells
    after = cells + odd * side + lax.shift_right_arithmetic(offset - cells, shift)
    ahead = cells + (1 - odd) * side + lax.shift_right_arithmetic(offset + cells, shift)
    code_ref[...] = jnp.where(offset < 0, ahead, jnp.where(offset < cells, offset, after))


def mean_kernel(own_ref, other_ref, mean_ref, pack_ref):
    odd = lax.rem(lax.axis_index("cell"), 2)
    half = mean_ref.shape[0]
    side = half // pack_ref.shape[0]
    first_factor, second_factor, total, _ = shares(own_ref[half:, :], other_ref[half:, :])
    mean = own_ref[:half, :] * spread(first_factor / total, LANES)
    mean_ref[...] = mean + other_ref[:half, :] * spread(second_factor / total, LANES)
    left = mean_ref[pl.ds(0, half // side, stride=side), :]
    right = mean_ref[pl.ds(side - 1, half // side, stride=side), :]
    pack_ref[...] = jnp.where(odd == 1, left, right)


def picked(sources, first, code_ref, total, start, out_rows, base):
    for k in range(code_ref.shape[0]):
        code = jnp.broadcast_to(code_ref[k : k + 1, start : start + LANES], total.shape)
        lane = lax.bitwise_and(code, LANES - 1)
        rows = slice((k + base) * out_rows, (k + base + 1) * out_rows)
        taken = 0.0
        for i, source in enumerate(sources, first):
            here = jnp.take_along_axis(source[rows], lane, axis=1, mode="promise_in_bounds")
            taken = jnp.where(lax.shift_right_logical(code, 7) == i, here, taken)
        total = total + taken
    return total


def own_kernel(mean_ref, hpv_ref, code_ref, out_ref):
    out_rows, cells = out_ref.shape
    mean, hpv = mean_ref[...], hpv_ref[...]
    gap = jnp.zeros(hpv.shape, jnp.float32)
    mixed = [
        dot(jnp.concatenate(pair, axis=1), mean, NT, CLOSE) for pair in ((hpv, gap), (gap, hpv))
    ]
    for i, start in enumerate(range(0, cells, LANES)):
        out_ref[:, start : start + LANES] = picked(
            mixed, 0, code_ref, mixed[i][:out_rows], start, out_rows, 1
        )


def halo_kernel(
    channels, a_ref, own_b_ref, other_b_ref, partial_ref, taps_ref, code_ref, out_ref
):
    out_rows, cells = out_ref.shape
    a, b = a_ref[...], mean_of(own_b_ref[...], other_b_ref[...], channels)
    halo = jnp.concatenate([a[:, :channels], a[:, channels:], b[:, :channels]], axis=0)
    gap = jnp.zeros((LANES - halo.shape[0], channels), jnp.float32)
    high, low = halves(jnp.concatenate([halo, gap], axis=0))
    edge = dot(taps_ref[...], jnp.concatenate([high, low, high], axis=1), NT, None)
    for start in range(0, cells, LANES):
        out_ref[:, start : start + LANES] = picked(
            [edge],
            cells // LANES,
            code_ref,
            partial_ref[:, start : start + LANES],
            start,
            out_rows,
            0,
        )


def swaps(sensors, cells):
    def listed(partner):
        return [(s * cells + c, partner(s, c)) for s in range(sensors) for c in range(cells)]

    def far(flip):
        def partner(s, c):
            if c in (0, cells - 1):
                return (s ^ 1) * cells + c
            return (s ^ flip) * cells + ((c - 1) ^ 1) + 1

        return listed(partner)

    near = listed(lambda s, c: s * cells + (c ^ 1))

    def across(flip):
        return listed(lambda s, c: (s ^ flip) * cells + c)

    return near, far, across


def on_device(
    swath,
    enc_weight,
    key_weight,
    value_weight,
    cell_query,
    quality,
    sample_cell,
    live,
    neighbours,
    hp_weight,
):
    sensors, ranges = lax.axis_size("sensor"), lax.axis_size("cell")
    channels = swath.shape[1]
    cells = cell_query.shape[1]
    side = math.isqrt(cells)
    out_rows = channels // sensors
    stencil = hp_weight.shape[1] // channels
    vmem = pl.BlockSpec(memory_space=pltpu.VMEM)
    axes = ("sensor", "cell")
    near, far, across = swaps(sensors, ranges)

    def shape(*sizes, dtype=jnp.float32):
        return jax.ShapeDtypeStruct(sizes, dtype)

    def call(kernel, args, outs, cost=None, **more):
        single = not isinstance(outs, list)
        specs = dict(in_specs=[vmem] * len(args), out_specs=vmem if single else [vmem] * len(outs))
        specs.update(more)
        return pl.pallas_call(
            kernel,
            out_shape=outs,
            compiler_params=pltpu.CompilerParams(vmem_limit_bytes=8 * 1024 * 1024),
            cost_estimate=cost
            and pl.CostEstimate(flops=cost, bytes_accessed=cost // 100, transcendentals=0),
            **specs,
        )(*args)

    def bound(kernel):
        return lambda *refs: kernel(channels, *refs)

    args = [
        swath,
        enc_weight,
        key_weight,
        value_weight,
        cell_query,
        quality,
        sample_cell,
        neighbours,
        hp_weight,
    ]
    loaded = call(
        load_kernel,
        [pltpu.with_memory_space_constraint(a, pltpu.HBM) for a in args],
        [shape(*a.shape, dtype=a.dtype) for a in args] + [shape(ROWS, LANES)],
        in_specs=[pl.BlockSpec(memory_space=pltpu.HBM)] * len(args),
        scratch_shapes=[pltpu.SemaphoreType.DMA((len(args),))],
    )
    swath, enc_weight, key_weight, value_weight, cell_query = loaded[:5]
    quality, sample_cell, neighbours, hp_weight, tail = loaded[5:]
    tail_b = lax.ppermute(tail, axes, far(0))
    tail_a = lax.ppermute(tail, axes, near)

    late, key_query, rest, ids = call(
        prepare_kernel,
        [swath, enc_weight, key_weight, cell_query, quality, sample_cell, live],
        [
            shape(ROWS, channels),
            shape(cells, channels),
            shape(cells, LANES),
            shape(1, LANES, dtype=jnp.int32),
        ],
        cost=200_000_000,
        in_specs=[vmem] * 6 + [pl.BlockSpec(memory_space=pltpu.SMEM)],
    )
    stats, pack = call(
        pool_kernel,
        [enc_weight, tail_b, tail_a, late, ids, quality, key_query, rest],
        [shape(cells // 2 + ROWS, LANES), shape(side, LANES)],
        scratch_shapes=[pltpu.VMEM((cells, LANES), jnp.float32)],
    )

    flip = 1
    while flip * 2 < sensors:
        other, other_pack = (lax.ppermute(v, axes, across(flip)) for v in (stats, pack))
        stats = call(merge_kernel, [stats, other], shape(*stats.shape))
        pack = call(bound(merge_pack_kernel), [pack, other_pack], shape(*pack.shape))
        flip *= 2

    other = lax.ppermute(stats, axes, across(flip))
    other_b = lax.ppermute(pack, axes, far(flip))
    own_b = lax.ppermute(pack, axes, far(0))
    hpv, taps, code = call(
        weights_kernel,
        [value_weight, neighbours, hp_weight, stats],
        [
            shape(stencil * out_rows, channels),
            shape((stencil - 1) * out_rows, 3 * channels, dtype=jnp.bfloat16),
            shape(*neighbours.shape, dtype=jnp.int32),
        ],
        cost=100_000_000,
    )
    mean, mean_a = call(
        mean_kernel,
        [stats, other],
        [shape(cells // 2, LANES), shape(side // 2, LANES)],
    )
    halo_a = lax.ppermute(mean_a, axes, near)
    partial = call(own_kernel, [mean, hpv, code], shape(out_rows, cells), cost=200_000_000)
    return call(
        bound(halo_kernel),
        [halo_a, own_b, other_b, partial, taps, code],
        shape(out_rows, cells),
    )


def solution(mesh):
    in_specs = (
        P("sensor", None, "cell"),
        P("sensor", None, None),
        P(),
        P(),
        P(None, "cell"),
        P("sensor", "cell"),
        P("sensor", "cell"),
        P("sensor", "cell"),
        P(None, "cell"),
        P(),
    )
    out_specs = P("sensor", "cell")
    return jax.shard_map(
        on_device, mesh=mesh, in_specs=in_specs, out_specs=out_specs, check_vma=False
    )
```

```python
import math

import jax
import jax.numpy as jnp
from jax import lax
from jax.experimental import pallas as pl
from jax.experimental.pallas import tpu as pltpu
from jax.sharding import PartitionSpec as P

FLOOR = -1e30
LANES = 128
ROWS = 8
LATE = 2
EXACT = lax.Precision.HIGHEST
CLOSE = lax.Precision.HIGH
NN = ((1,), (0,))
NT = ((1,), (1,))
TN = ((0,), (0,))


def dot(left, right, contract, precision=EXACT):
    return lax.dot_general(
        left,
        right,
        (contract, ((), ())),
        precision=precision,
        preferred_element_type=jnp.float32,
    )


def iota(shape, dim):
    return lax.broadcasted_iota(jnp.int32, shape, dim)


def gelu(x):
    return 0.5 * x * (1.0 + lax.erf(x * math.sqrt(0.5)))


def widened(value, lanes=LANES):
    gap = jnp.zeros((value.shape[0], lanes - value.shape[1]), value.dtype)
    return jnp.concatenate([value, gap], axis=1)


def with_peak(block, peak, channels):
    return jnp.where(iota(block.shape, 1) == channels + 1, peak, block)


def merged(first, second, channels):
    first_peak, second_peak = (v[:, channels + 1 : channels + 2] for v in (first, second))
    peak = jnp.maximum(first_peak, second_peak)
    both = first * jnp.exp(first_peak - peak) + second * jnp.exp(second_peak - peak)
    return both, peak


def mean_of(first, second, channels):
    both, _ = merged(first, second, channels)
    return both / both[:, channels : channels + 1]


def load_kernel(*refs):
    *refs, tail_ref, last_ref, sems = refs
    count = len(refs) // 2
    sources, targets = refs[:count], refs[count:]
    swath_ref = sources[0]
    copies = [(swath_ref.at[0, :, pl.ds(swath_ref.shape[2] - LANES, LANES)], last_ref)]
    copies += list(zip(sources, targets))
    copies = [pltpu.make_async_copy(*ends, sems.at[i]) for i, ends in enumerate(copies)]
    for copy in copies:
        copy.start()
    copies[0].wait()
    last = last_ref[...]
    row, lane = iota((ROWS, LANES), 0), iota((ROWS, LANES), 1)
    first = ((lane == LANES - 2 + row) & (row < 2)).astype(jnp.float32)
    second = ((lane == LANES - 1) & (row == 0)).astype(jnp.float32)
    tail_ref[...] = jnp.concatenate([dot(first, last, NT), dot(second, last, NT)], axis=1)
    for copy in copies[1:]:
        copy.wait()


def halves(value):
    high = value.astype(jnp.bfloat16)
    return high, (value - high.astype(jnp.float32)).astype(jnp.bfloat16)


def parts(value):
    high = value.astype(jnp.bfloat16)
    rest = value - high.astype(jnp.float32)
    middle = rest.astype(jnp.bfloat16)
    return high, middle, (rest - middle.astype(jnp.float32)).astype(jnp.bfloat16)


def packed(block, channels):
    half = block.shape[0] // 2
    sums = jnp.concatenate([block[:half, :channels], block[half:, :channels]], axis=1)
    total, peak = (block[:, channels + i : channels + i + 1] for i in range(2))
    lane = iota((half, LANES), 1)
    columns = jnp.where(lane == 0, total[:half], jnp.where(lane == 1, total[half:], 0.0))
    columns = jnp.where(lane == 2, peak[:half], jnp.where(lane == 3, peak[half:], columns))
    return sums, jnp.transpose(columns)[:ROWS, :]


def prepare_kernel(
    swath_ref,
    enc_ref,
    key_ref,
    query_ref,
    quality_ref,
    cell_ref,
    live_ref,
    before_ref,
    ids_ref,
    late_kq_ref,
    late_rest_ref,
    stats_ref,
    pack_ref,
    kq_ref,
    block_ref,
):
    sensor = lax.axis_index("sensor")
    odd = lax.rem(lax.axis_index("cell"), 2)
    channels, slots = swath_ref.shape[1:]
    cells = query_ref.shape[1]
    side, half = pack_ref.shape[0], cells // 2

    signal = swath_ref[0]
    one = jnp.concatenate([jnp.zeros((channels, 1), jnp.float32), signal[:, : slots - 1]], axis=1)
    two = jnp.concatenate([jnp.zeros((channels, 2), jnp.float32), signal[:, : slots - 2]], axis=1)
    stacked = jnp.concatenate([two, one, signal], axis=0)
    before = dot(enc_ref[0], stacked, NN)
    before_ref[...] = jnp.transpose(before[:, :LANES])[:ROWS, :]
    encoded = gelu(before)

    query = query_ref[...]
    key_query = dot(key_ref[...], query, TN) * (1.0 / math.sqrt(channels))
    key_query = jnp.transpose(jnp.concatenate([key_query, key_query], axis=0))
    query = jnp.transpose(jnp.concatenate([query, jnp.zeros(query.shape, jnp.float32)], axis=0))
    kq_ref[...] = key_query
    own_score = jnp.sum(query * key_query, axis=1, keepdims=True)
    own_score = jnp.where(sensor == 0, own_score, -jnp.inf)

    high, middle, low = parts(key_query)
    mixed = jnp.where(iota(high.shape, 1) < channels, high, low)
    token_high, token_middle, token_low = parts(encoded)
    score = dot(
        jnp.concatenate([high, middle, mixed], axis=1),
        jnp.concatenate(
            [token_high, token_middle, token_high, token_middle, token_low, token_high], axis=0
        ),
        NN,
        None,
    )
    slot = iota((1, slots), 1)
    ids = jnp.where(slot < live_ref[0, 0], cell_ref[...], -1)
    ids_ref[...] = ids[:, :LANES]
    ids = jnp.where(slot < LATE, -1, ids)
    score = jnp.where(iota((cells, slots), 0) == ids, score + quality_ref[...], -jnp.inf)
    peak = jnp.maximum(jnp.max(score, axis=1, keepdims=True), jnp.maximum(own_score, FLOOR))
    weights = jnp.exp(score - peak)
    place = iota((LANES - channels, slots), 0)
    tokens = jnp.concatenate([encoded, (place == 0).astype(jnp.float32)], axis=0)
    high, low = halves(jnp.transpose(tokens))
    weights_high, weights_low = halves(weights)
    wide = dot(weights_high, jnp.concatenate([high, low], axis=1), NN, None)
    block = wide[:, :LANES] + wide[:, LANES:] + dot(weights_low, high, NN, None)
    own = jnp.where(iota(query.shape, 1) == channels, 1.0, query)
    block = with_peak(block + own * jnp.exp(own_score - peak), peak, channels)
    block_ref[...] = block
    stats_ref[:half, :], stats_ref[half:, :] = packed(block, channels)
    left = block_ref[pl.ds(0, side, stride=side), :]
    right = block_ref[pl.ds(side - 1, side, stride=side), :]
    pack_ref[...] = jnp.where(odd == 1, right, left)
    late_kq_ref[...] = jnp.zeros(late_kq_ref.shape, jnp.float32)
    late_rest_ref[...] = jnp.zeros(late_rest_ref.shape, jnp.float32)
    for j in range(LATE):
        at = cell_ref[0, j]
        late_kq_ref[j : j + 1, :] = kq_ref[pl.ds(at, 1), :]
        late_rest_ref[j : j + 1, :] = block_ref[pl.ds(at, 1), :]


def pool_kernel(
    enc_ref,
    tail_a_ref,
    tail_b_ref,
    before_ref,
    ids_ref,
    quality_ref,
    late_kq_ref,
    late_rest_ref,
    rest_ref,
    rest_pack_ref,
    stats_ref,
    pack_ref,
):
    cell = lax.axis_index("cell")
    odd = lax.rem(cell, 2)
    channels = before_ref.shape[1]
    side, half = pack_ref.shape[0], stats_ref.shape[0] - ROWS
    tail = jnp.where(odd == 1, tail_a_ref[...], tail_b_ref[...])
    tail = jnp.where(cell == 0, 0.0, tail)
    before = before_ref[...] + dot(tail, enc_ref[0, :, : 2 * channels], NT)
    tokens = widened(gelu(before))
    score = jnp.sum(tokens * late_kq_ref[...], axis=1, keepdims=True)
    tokens = jnp.where(iota(tokens.shape, 1) == channels, 1.0, tokens)
    rest = late_rest_ref[...]
    rest_peak = rest[:, channels + 1 : channels + 2]
    ids = ids_ref[...]
    rows = []
    for j in range(LATE):
        rest_peak = rest[j : j + 1, channels + 1 : channels + 2]
        peak, found = rest_peak, []
        for i in range(LATE):
            here = score[i : i + 1] + quality_ref[:, i : i + 1]
            if i != j:
                here = jnp.where(ids[:, i : i + 1] == ids[:, j : j + 1], here, -jnp.inf)
            found.append(here)
            peak = jnp.maximum(peak, here)
        row = rest[j : j + 1] * jnp.exp(rest_peak - peak)
        for i, here in enumerate(found):
            row = row + tokens[i : i + 1] * jnp.exp(here - peak)
        rows.append(with_peak(row, peak, channels))
    sums, ends, pack = rest_ref[:half, :], rest_ref[half:, :], rest_pack_ref[...]
    lane = iota(sums.shape, 1)
    of_sum = iota(sums.shape, 0) + jnp.where(lane < channels, 0, half)
    kind = iota(ends.shape, 0)
    of_end = iota(ends.shape, 1) + jnp.where(lax.rem(kind, 2) == 0, 0, half)
    of_pack = iota((side, 1), 0) * side + jnp.where(odd == 1, side - 1, 0)
    for j, row in enumerate(rows):
        at = ids[:, j : j + 1]
        twice = jnp.concatenate([row[:, :channels], row[:, :channels]], axis=1)
        sums = jnp.where(of_sum == at, twice, sums)
        total, peak = (row[:, channels + i : channels + i + 1] for i in range(2))
        ends = jnp.where((of_end == at) & (kind < 4), jnp.where(kind < 2, total, peak), ends)
        pack = jnp.where(of_pack == at, row, pack)
    stats_ref[:half, :], stats_ref[half:, :] = sums, ends
    pack_ref[...] = pack


def shares(first, second):
    peak = jnp.maximum(first[2:4], second[2:4])
    first_factor = jnp.exp(first[2:4] - peak)
    second_factor = jnp.exp(second[2:4] - peak)
    total = first[0:2] * first_factor + second[0:2] * second_factor
    return first_factor, second_factor, total, peak


def spread(row_pair, width):
    square = jnp.concatenate(
        [row_pair, jnp.zeros((LANES - row_pair.shape[0], row_pair.shape[1]), jnp.float32)], axis=0
    )
    columns = jnp.transpose(square)
    lane = iota((columns.shape[0], width), 1)
    return jnp.where(lane < width // 2, columns[:, 0:1], columns[:, 1:2])


def merge_pack_kernel(channels, own_ref, other_ref, out_ref):
    both, peak = merged(own_ref[...], other_ref[...], channels)
    out_ref[...] = with_peak(both, peak, channels)


def merge_kernel(own_ref, other_ref, out_ref):
    half = own_ref.shape[0] - ROWS
    first_factor, second_factor, total, peak = shares(own_ref[half:, :], other_ref[half:, :])
    first_sum = own_ref[:half, :] * spread(first_factor, LANES)
    out_ref[:half, :] = first_sum + other_ref[:half, :] * spread(second_factor, LANES)
    rest = jnp.zeros((ROWS - 4, total.shape[1]), jnp.float32)
    out_ref[half:, :] = jnp.concatenate([total, peak, rest], axis=0)


def copy_kernel(in_ref, out_ref):
    out_ref[...] = in_ref[...]


def weights_kernel(value_ref, near_ref, hp_ref, after_ref, hpv_ref, taps_ref, code_ref, halo_ref):
    del after_ref
    sensor = lax.axis_index("sensor")
    cell = lax.axis_index("cell")
    channels = value_ref.shape[0]
    cells = near_ref.shape[1]
    side = math.isqrt(cells)
    out_rows = hpv_ref.shape[0] * channels // hp_ref.shape[1]
    own_hp = hp_ref[pl.ds(pl.multiple_of(sensor * out_rows, ROWS), out_rows), :]
    value = value_ref[...]
    taps = [
        own_hp[:, k * channels : (k + 1) * channels] for k in range(hp_ref.shape[1] // channels)
    ]
    hpv = dot(jnp.concatenate(taps, axis=0), value, NN)
    hpv_ref[...] = hpv
    high, low = halves(hpv[out_rows:])
    taps_ref[...] = jnp.concatenate([high, high, low], axis=1)

    shift = side.bit_length() - 1
    odd = lax.rem(cell, 2)
    offset = near_ref[...] - cell * cells
    after = cells + odd * side + lax.shift_right_arithmetic(offset - cells, shift)
    ahead = cells + (1 - odd) * side + lax.shift_right_arithmetic(offset + cells, shift)
    code_ref[...] = jnp.where(offset < 0, ahead, jnp.where(offset < cells, offset, after))
    halo = jnp.where(offset < 0, ahead, after) - cells
    halo_ref[...] = jnp.where((offset < 0) | (offset >= cells), halo, LANES - 1)


def mean_kernel(own_ref, other_ref, mean_ref, pack_ref):
    odd = lax.rem(lax.axis_index("cell"), 2)
    half = mean_ref.shape[0]
    side = half // pack_ref.shape[0]
    first_factor, second_factor, total, _ = shares(own_ref[half:, :], other_ref[half:, :])
    mean = own_ref[:half, :] * spread(first_factor / total, LANES)
    mean_ref[...] = mean + other_ref[:half, :] * spread(second_factor / total, LANES)
    left = mean_ref[pl.ds(0, half // side, stride=side), :]
    right = mean_ref[pl.ds(side - 1, half // side, stride=side), :]
    pack_ref[...] = jnp.where(odd == 1, left, right)


def own_kernel(mean_ref, hpv_ref, code_ref, out_ref):
    out_rows, cells = out_ref.shape
    mean, hpv = mean_ref[...], hpv_ref[...]
    gap = jnp.zeros(hpv.shape, jnp.float32)
    mixed = [
        dot(jnp.concatenate(pair, axis=1), mean, NT, CLOSE) for pair in ((hpv, gap), (gap, hpv))
    ]
    lanes = lax.bitwise_and(code_ref[...], LANES - 1)
    places = lax.shift_right_logical(code_ref[...], LANES.bit_length() - 1)
    for i, start in enumerate(range(0, cells, LANES)):
        total = mixed[i][:out_rows]
        for k in range(code_ref.shape[0]):
            rows = slice((k + 1) * out_rows, (k + 2) * out_rows)
            lane, place = (
                jnp.broadcast_to(v[k : k + 1, start : start + LANES], total.shape)
                for v in (lanes, places)
            )
            taken = 0.0
            for source, values in enumerate(mixed):
                here = taken_lanes(values[rows], lane)
                taken = jnp.where(place == source, here, taken)
            total = total + taken
        out_ref[:, start : start + LANES] = total


def taken_lanes(values, lane):
    return jnp.take_along_axis(values, lane, axis=1, mode="promise_in_bounds")


def halo_kernel(
    channels, a_ref, own_b_ref, other_b_ref, partial_ref, taps_ref, lanes_ref, out_ref
):
    out_rows, cells = out_ref.shape
    a, b = a_ref[...], mean_of(own_b_ref[...], other_b_ref[...], channels)
    halo = jnp.concatenate([a[:, :channels], a[:, channels:], b[:, :channels]], axis=0)
    gap = jnp.zeros((LANES - halo.shape[0], channels), jnp.float32)
    high, low = halves(jnp.concatenate([halo, gap], axis=0))
    edge = dot(taps_ref[...], jnp.concatenate([high, low, high], axis=1), NT, None)
    lanes = lanes_ref[...]
    for start in range(0, cells, LANES):
        total = partial_ref[:, start : start + LANES]
        for k in range(lanes.shape[0]):
            lane = jnp.broadcast_to(lanes[k : k + 1, start : start + LANES], total.shape)
            total = total + taken_lanes(edge[k * out_rows : (k + 1) * out_rows], lane)
        out_ref[:, start : start + LANES] = total


def swaps(sensors, cells):
    def listed(partner):
        return [(s * cells + c, partner(s, c)) for s in range(sensors) for c in range(cells)]

    def far(flip):
        def partner(s, c):
            if c in (0, cells - 1):
                return (s ^ 1) * cells + c
            return (s ^ flip) * cells + ((c - 1) ^ 1) + 1

        return listed(partner)

    near = listed(lambda s, c: s * cells + (c ^ 1))

    def across(flip):
        return listed(lambda s, c: (s ^ flip) * cells + c)

    return near, far, across


def on_device(
    swath,
    enc_weight,
    key_weight,
    value_weight,
    cell_query,
    quality,
    sample_cell,
    live,
    neighbours,
    hp_weight,
):
    sensors, ranges = lax.axis_size("sensor"), lax.axis_size("cell")
    channels = swath.shape[1]
    cells = cell_query.shape[1]
    side = math.isqrt(cells)
    out_rows = channels // sensors
    stencil = hp_weight.shape[1] // channels
    vmem = pl.BlockSpec(memory_space=pltpu.VMEM)
    axes = ("sensor", "cell")
    near, far, across = swaps(sensors, ranges)

    def shape(*sizes, dtype=jnp.float32):
        return jax.ShapeDtypeStruct(sizes, dtype)

    def call(kernel, args, outs, cost=None, **more):
        single = not isinstance(outs, list)
        specs = dict(in_specs=[vmem] * len(args), out_specs=vmem if single else [vmem] * len(outs))
        specs.update(more)
        return pl.pallas_call(
            kernel,
            out_shape=outs,
            compiler_params=pltpu.CompilerParams(vmem_limit_bytes=8 * 1024 * 1024),
            cost_estimate=cost
            and pl.CostEstimate(flops=cost, bytes_accessed=cost // 100, transcendentals=0),
            **specs,
        )(*args)

    def bound(kernel):
        return lambda *refs: kernel(channels, *refs)

    args = [
        swath,
        enc_weight,
        key_weight,
        value_weight,
        cell_query,
        quality,
        sample_cell,
        neighbours,
        hp_weight,
    ]
    loaded = call(
        load_kernel,
        [pltpu.with_memory_space_constraint(a, pltpu.HBM) for a in args],
        [shape(*a.shape, dtype=a.dtype) for a in args] + [shape(ROWS, LANES)],
        in_specs=[pl.BlockSpec(memory_space=pltpu.HBM)] * len(args),
        scratch_shapes=[
            pltpu.VMEM((channels, LANES), jnp.float32),
            pltpu.SemaphoreType.DMA((len(args) + 1,)),
        ],
    )
    swath, enc_weight, key_weight, value_weight, cell_query = loaded[:5]
    quality, sample_cell, neighbours, hp_weight, tail = loaded[5:]
    tail_b = lax.ppermute(tail, axes, far(0))
    tail_a = lax.ppermute(tail, axes, near)

    before, ids, late_kq, late_rest, rest, rest_pack = call(
        prepare_kernel,
        [swath, enc_weight, key_weight, cell_query, quality, sample_cell, live],
        [
            shape(ROWS, channels),
            shape(1, LANES, dtype=jnp.int32),
            shape(ROWS, LANES),
            shape(ROWS, LANES),
            shape(cells // 2 + ROWS, LANES),
            shape(side, LANES),
        ],
        cost=200_000_000,
        in_specs=[vmem] * 6 + [pl.BlockSpec(memory_space=pltpu.SMEM)],
        scratch_shapes=[pltpu.VMEM((cells, LANES), jnp.float32)] * 2,
    )
    stats, pack = call(
        pool_kernel,
        [
            enc_weight,
            tail_a,
            tail_b,
            before,
            ids,
            quality,
            late_kq,
            late_rest,
            rest,
            rest_pack,
        ],
        [shape(*rest.shape), shape(*rest_pack.shape)],
    )

    flip = 1
    while flip * 2 < sensors:
        other, other_pack = (lax.ppermute(v, axes, across(flip)) for v in (stats, pack))
        stats = call(merge_kernel, [stats, other], shape(*stats.shape))
        pack = call(bound(merge_pack_kernel), [pack, other_pack], shape(*pack.shape))
        flip *= 2

    other = lax.ppermute(stats, axes, across(flip))
    other_b = lax.ppermute(pack, axes, far(flip))
    pack_again = call(copy_kernel, [pack], shape(*pack.shape), cost=100_000_000)
    hpv, taps, code, lanes = call(
        weights_kernel,
        [value_weight, neighbours, hp_weight, pack_again],
        [
            shape(stencil * out_rows, channels),
            shape((stencil - 1) * out_rows, 3 * channels, dtype=jnp.bfloat16),
            shape(*neighbours.shape, dtype=jnp.int32),
            shape(*neighbours.shape, dtype=jnp.int32),
        ],
        cost=100_000_000,
    )
    own_b = lax.ppermute(pack_again, axes, far(0))
    mean, mean_a = call(
        mean_kernel,
        [stats, other],
        [shape(cells // 2, LANES), shape(side // 2, LANES)],
    )
    halo_a = lax.ppermute(mean_a, axes, near)
    partial = call(own_kernel, [mean, hpv, code], shape(out_rows, cells), cost=200_000_000)
    return call(
        bound(halo_kernel),
        [halo_a, own_b, other_b, partial, taps, lanes],
        shape(out_rows, cells),
    )


def solution(mesh):
    in_specs = (
        P("sensor", None, "cell"),
        P("sensor", None, None),
        P(),
        P(),
        P(None, "cell"),
        P("sensor", "cell"),
        P("sensor", "cell"),
        P("sensor", "cell"),
        P(None, "cell"),
        P(),
    )
    out_specs = P("sensor", "cell")
    return jax.shard_map(
        on_device, mesh=mesh, in_specs=in_specs, out_specs=out_specs, check_vma=False
    )
```

```python
import functools
import math

import jax
import jax.numpy as jnp
from jax import lax
from jax.experimental import pallas as pl
from jax.experimental.pallas import tpu as pltpu
from jax.sharding import PartitionSpec as P

FLOOR = -1e30
LANES = 128
ROWS = 8
LATE = 2
EXACT = lax.Precision.HIGHEST
CLOSE = lax.Precision.HIGH
NN = ((1,), (0,))
NT = ((1,), (1,))
TN = ((0,), (0,))


def dot(left, right, contract, precision=EXACT):
    return lax.dot_general(
        left,
        right,
        (contract, ((), ())),
        precision=precision,
        preferred_element_type=jnp.float32,
    )


def iota(shape, dim):
    return lax.broadcasted_iota(jnp.int32, shape, dim)


def gelu(x):
    return 0.5 * x * (1.0 + lax.erf(x * math.sqrt(0.5)))


def widened(value, lanes=LANES):
    gap = jnp.zeros((value.shape[0], lanes - value.shape[1]), value.dtype)
    return jnp.concatenate([value, gap], axis=1)


def with_peak(block, peak, channels):
    return jnp.where(iota(block.shape, 1) == channels + 1, peak, block)


def merged(first, second, channels):
    first_peak, second_peak = (v[:, channels + 1 : channels + 2] for v in (first, second))
    peak = jnp.maximum(first_peak, second_peak)
    both = first * jnp.exp(first_peak - peak) + second * jnp.exp(second_peak - peak)
    return both, peak


def mean_of(first, second, channels):
    both, _ = merged(first, second, channels)
    return both / both[:, channels : channels + 1]


def load_kernel(*refs):
    *refs, tail_ref, last_ref, sems = refs
    count = len(refs) // 2
    sources, targets = refs[:count], refs[count:]
    swath_ref = sources[0]
    copies = [(swath_ref.at[0, :, pl.ds(swath_ref.shape[2] - LANES, LANES)], last_ref)]
    copies += list(zip(sources, targets))
    copies = [pltpu.make_async_copy(*ends, sems.at[i]) for i, ends in enumerate(copies)]
    for copy in copies:
        copy.start()
    copies[0].wait()
    last = jnp.transpose(last_ref[...])[LANES - LATE :, :]
    gap = jnp.zeros(last.shape, jnp.float32)
    two = jnp.concatenate([last, jnp.concatenate([last[1:], gap[1:]], axis=0)], axis=1)
    tail_ref[...] = jnp.concatenate([two] + [jnp.zeros(two.shape, jnp.float32)] * 3, axis=0)
    for copy in copies[1:]:
        copy.wait()


def halves(value):
    high = value.astype(jnp.bfloat16)
    return high, (value - high.astype(jnp.float32)).astype(jnp.bfloat16)


def parts(value):
    high = value.astype(jnp.bfloat16)
    rest = value - high.astype(jnp.float32)
    middle = rest.astype(jnp.bfloat16)
    return high, middle, (rest - middle.astype(jnp.float32)).astype(jnp.bfloat16)


def packed(block, channels):
    half = block.shape[0] // 2
    sums = jnp.concatenate([block[:half, :channels], block[half:, :channels]], axis=1)
    total, peak = (block[:, channels + i : channels + i + 1] for i in range(2))
    lane = iota((half, LANES), 1)
    columns = jnp.where(lane == 0, total[:half], jnp.where(lane == 1, total[half:], 0.0))
    columns = jnp.where(lane == 2, peak[:half], jnp.where(lane == 3, peak[half:], columns))
    return sums, jnp.transpose(columns)[:ROWS, :]


def prepare_kernel(
    swath_ref,
    enc_ref,
    key_ref,
    query_ref,
    quality_ref,
    cell_ref,
    live_ref,
    value_ref,
    near_ref,
    hp_ref,
    before_ref,
    taps_ref,
    ids_ref,
    late_kq_ref,
    late_rest_ref,
    stats_ref,
    pack_ref,
    loaded_value_ref,
    loaded_near_ref,
    loaded_hp_ref,
    kq_ref,
    block_ref,
    sems,
):
    ends = ((value_ref, loaded_value_ref), (near_ref, loaded_near_ref), (hp_ref, loaded_hp_ref))
    copies = [pltpu.make_async_copy(*pair, sems.at[i]) for i, pair in enumerate(ends)]
    for copy in copies:
        copy.start()
    sensor = lax.axis_index("sensor")
    odd = lax.rem(lax.axis_index("cell"), 2)
    channels, slots = swath_ref.shape[1:]
    cells = query_ref.shape[1]
    side, half = pack_ref.shape[0], cells // 2

    signal = swath_ref[0]
    one = jnp.concatenate([jnp.zeros((channels, 1), jnp.float32), signal[:, : slots - 1]], axis=1)
    two = jnp.concatenate([jnp.zeros((channels, 2), jnp.float32), signal[:, : slots - 2]], axis=1)
    stacked = jnp.concatenate([two, one, signal], axis=0)
    before = dot(enc_ref[0], stacked, NN)
    before_ref[...] = jnp.transpose(before[:, :LANES])[:ROWS, :]
    encoded = gelu(before)

    query = query_ref[...]
    key_query = dot(key_ref[...], query, TN) * (1.0 / math.sqrt(channels))
    key_query = jnp.transpose(jnp.concatenate([key_query, key_query], axis=0))
    query = jnp.transpose(jnp.concatenate([query, jnp.zeros(query.shape, jnp.float32)], axis=0))
    kq_ref[...] = key_query
    own_score = jnp.sum(query * key_query, axis=1, keepdims=True)
    own_score = jnp.where(sensor == 0, own_score, -jnp.inf)

    high, middle, low = parts(key_query)
    mixed = jnp.where(iota(high.shape, 1) < channels, high, low)
    token_high, token_middle, token_low = parts(encoded)
    score = dot(
        jnp.concatenate([high, middle, mixed], axis=1),
        jnp.concatenate(
            [token_high, token_middle, token_high, token_middle, token_low, token_high], axis=0
        ),
        NN,
        None,
    )
    slot = iota((1, slots), 1)
    ids = jnp.where(slot < live_ref[0, 0], cell_ref[...], -1)
    ids_ref[...] = ids[:, :LANES]
    ids = jnp.where(slot < LATE, -1, ids)
    score = jnp.where(iota((cells, slots), 0) == ids, score + quality_ref[...], -jnp.inf)
    peak = jnp.maximum(jnp.max(score, axis=1, keepdims=True), jnp.maximum(own_score, FLOOR))
    weights = jnp.exp(score - peak)
    place = iota((LANES - channels, slots), 0)
    tokens = jnp.concatenate([encoded, (place == 0).astype(jnp.float32)], axis=0)
    high, low = halves(jnp.transpose(tokens))
    weights_high, weights_low = halves(weights)
    wide = dot(weights_high, jnp.concatenate([high, low], axis=1), NN, None)
    block = wide[:, :LANES] + wide[:, LANES:] + dot(weights_low, high, NN, None)
    own = jnp.where(iota(query.shape, 1) == channels, 1.0, query)
    block = with_peak(block + own * jnp.exp(own_score - peak), peak, channels)
    block_ref[...] = block
    stats_ref[:half, :], stats_ref[half:, :] = packed(block, channels)
    left = block_ref[pl.ds(0, side, stride=side), :]
    right = block_ref[pl.ds(side - 1, side, stride=side), :]
    pack_ref[...] = jnp.where(odd == 1, right, left)
    late_kq_ref[...] = jnp.zeros(late_kq_ref.shape, jnp.float32)
    late_rest_ref[...] = jnp.zeros(late_rest_ref.shape, jnp.float32)
    for j in range(LATE):
        at = cell_ref[0, j]
        late_kq_ref[j : j + 1, :] = kq_ref[pl.ds(at, 1), :]
        late_rest_ref[j : j + 1, :] = block_ref[pl.ds(at, 1), :]
    high, middle, low = parts(enc_ref[0, :, : LATE * channels])
    taps_ref[...] = jnp.concatenate([high, high, middle, high, middle, low], axis=1)
    for copy in copies:
        copy.wait()


def pool_kernel(
    taps_ref,
    tail_a_ref,
    tail_b_ref,
    before_ref,
    ids_ref,
    quality_ref,
    late_kq_ref,
    late_rest_ref,
    rest_ref,
    rest_pack_ref,
    stats_ref,
    pack_ref,
):
    cell = lax.axis_index("cell")
    odd = lax.rem(cell, 2)
    channels = before_ref.shape[1]
    side, half = pack_ref.shape[0], stats_ref.shape[0] - ROWS
    tail = jnp.where(odd == 1, tail_a_ref[...], tail_b_ref[...])
    tail = jnp.where(cell == 0, 0.0, tail)
    high, middle, low = parts(jnp.concatenate([tail, jnp.zeros(tail.shape, jnp.float32)], axis=0))
    tail = jnp.concatenate([high, middle, high, low, middle, high], axis=1)
    before = before_ref[...] + dot(tail, taps_ref[...], NT, None)[:ROWS, :]
    tokens = widened(gelu(before))
    score = jnp.sum(tokens * late_kq_ref[...], axis=1, keepdims=True)
    tokens = jnp.where(iota(tokens.shape, 1) == channels, 1.0, tokens)
    rest = late_rest_ref[...]
    rest_peak = rest[:, channels + 1 : channels + 2]
    ids = ids_ref[...]
    rows = []
    for j in range(LATE):
        rest_peak = rest[j : j + 1, channels + 1 : channels + 2]
        peak, found = rest_peak, []
        for i in range(LATE):
            here = score[i : i + 1] + quality_ref[:, i : i + 1]
            if i != j:
                here = jnp.where(ids[:, i : i + 1] == ids[:, j : j + 1], here, -jnp.inf)
            found.append(here)
            peak = jnp.maximum(peak, here)
        row = rest[j : j + 1] * jnp.exp(rest_peak - peak)
        for i, here in enumerate(found):
            row = row + tokens[i : i + 1] * jnp.exp(here - peak)
        rows.append(with_peak(row, peak, channels))
    sums, ends, pack = rest_ref[:half, :], rest_ref[half:, :], rest_pack_ref[...]
    lane = iota(sums.shape, 1)
    of_sum = iota(sums.shape, 0) + jnp.where(lane < channels, 0, half)
    kind = iota(ends.shape, 0)
    of_end = iota(ends.shape, 1) + jnp.where(lax.rem(kind, 2) == 0, 0, half)
    of_pack = iota((side, 1), 0) * side + jnp.where(odd == 1, side - 1, 0)
    for j, row in enumerate(rows):
        at = ids[:, j : j + 1]
        twice = jnp.concatenate([row[:, :channels], row[:, :channels]], axis=1)
        sums = jnp.where(of_sum == at, twice, sums)
        total, peak = (row[:, channels + i : channels + i + 1] for i in range(2))
        ends = jnp.where((of_end == at) & (kind < 4), jnp.where(kind < 2, total, peak), ends)
        pack = jnp.where(of_pack == at, row, pack)
    stats_ref[:half, :], stats_ref[half:, :] = sums, ends
    pack_ref[...] = pack


def shares(first, second):
    peak = jnp.maximum(first[2:4], second[2:4])
    first_factor = jnp.exp(first[2:4] - peak)
    second_factor = jnp.exp(second[2:4] - peak)
    total = first[0:2] * first_factor + second[0:2] * second_factor
    return first_factor, second_factor, total, peak


def spread(*row_pairs):
    rows = jnp.concatenate(row_pairs, axis=0)
    gap = jnp.zeros((LANES - rows.shape[0], rows.shape[1]), jnp.float32)
    columns = jnp.transpose(jnp.concatenate([rows, gap], axis=0))
    left = iota((columns.shape[0], LANES), 1) < LANES // 2
    return [
        jnp.where(left, columns[:, 2 * i : 2 * i + 1], columns[:, 2 * i + 1 : 2 * i + 2])
        for i in range(len(row_pairs))
    ]


def merge_pack_kernel(channels, own_ref, other_ref, out_ref):
    both, peak = merged(own_ref[...], other_ref[...], channels)
    out_ref[...] = with_peak(both, peak, channels)


def merge_kernel(own_ref, other_ref, out_ref):
    half = own_ref.shape[0] - ROWS
    first_factor, second_factor, total, peak = shares(own_ref[half:, :], other_ref[half:, :])
    first_factor, second_factor = spread(first_factor, second_factor)
    out_ref[:half, :] = own_ref[:half, :] * first_factor + other_ref[:half, :] * second_factor
    rest = jnp.zeros((ROWS - 4, total.shape[1]), jnp.float32)
    out_ref[half:, :] = jnp.concatenate([total, peak, rest], axis=0)


def copy_kernel(in_ref, out_ref):
    out_ref[...] = in_ref[...]


def weights_kernel(value_ref, near_ref, hp_ref, after_ref, hpv_ref, taps_ref, code_ref, pick_ref):
    del after_ref
    sensor = lax.axis_index("sensor")
    cell = lax.axis_index("cell")
    channels = value_ref.shape[0]
    cells = near_ref.shape[1]
    side = math.isqrt(cells)
    out_rows = hpv_ref.shape[0] * channels // hp_ref.shape[1]
    own_hp = hp_ref[pl.ds(pl.multiple_of(sensor * out_rows, ROWS), out_rows), :]
    value = value_ref[...]
    taps = [
        own_hp[:, k * channels : (k + 1) * channels] for k in range(hp_ref.shape[1] // channels)
    ]
    hpv = dot(jnp.concatenate(taps, axis=0), value, NN)
    hpv_ref[...] = hpv
    high, low = halves(hpv[out_rows:])
    taps_ref[...] = jnp.concatenate([high, high, low], axis=1)

    shift = side.bit_length() - 1
    odd = lax.rem(cell, 2)
    offset = near_ref[...] - cell * cells
    after = cells + odd * side + lax.shift_right_arithmetic(offset - cells, shift)
    ahead = cells + (1 - odd) * side + lax.shift_right_arithmetic(offset + cells, shift)
    code_ref[...] = jnp.where(offset < 0, ahead, jnp.where(offset < cells, offset, after))
    halo = code_ref[...] - cells
    place = iota((2 * side, cells), 0)
    for k in range(halo.shape[0]):
        here = (place == halo[k : k + 1, :]).astype(jnp.float32).astype(jnp.bfloat16)
        pick_ref[2 * side * k : 2 * side * (k + 1), :] = here


def mean_kernel(own_ref, other_ref, mean_ref, pack_ref):
    odd = lax.rem(lax.axis_index("cell"), 2)
    half = mean_ref.shape[0]
    side = half // pack_ref.shape[0]
    first_factor, second_factor, total, _ = shares(own_ref[half:, :], other_ref[half:, :])
    first_share, second_share = spread(first_factor / total, second_factor / total)
    mean_ref[...] = own_ref[:half, :] * first_share + other_ref[:half, :] * second_share
    left = mean_ref[pl.ds(0, half // side, stride=side), :]
    right = mean_ref[pl.ds(side - 1, half // side, stride=side), :]
    pack_ref[...] = jnp.where(odd == 1, left, right)


def own_kernel(mean_ref, hpv_ref, code_ref, out_ref):
    out_rows, cells = out_ref.shape
    mean, hpv = mean_ref[...], hpv_ref[...]
    gap = jnp.zeros(hpv.shape, jnp.float32)
    mixed = [
        dot(jnp.concatenate(pair, axis=1), mean, NT, CLOSE) for pair in ((hpv, gap), (gap, hpv))
    ]
    lanes = lax.bitwise_and(code_ref[...], LANES - 1)
    places = lax.shift_right_logical(code_ref[...], LANES.bit_length() - 1)
    for i, start in enumerate(range(0, cells, LANES)):
        total = mixed[i][:out_rows]
        for k in range(code_ref.shape[0]):
            rows = slice((k + 1) * out_rows, (k + 2) * out_rows)
            lane, place = (
                jnp.broadcast_to(v[k : k + 1, start : start + LANES], total.shape)
                for v in (lanes, places)
            )
            taken = 0.0
            for source, values in enumerate(mixed):
                here = taken_lanes(values[rows], lane)
                taken = jnp.where(place == source, here, taken)
            total = total + taken
        out_ref[:, start : start + LANES] = total


def taken_lanes(values, lane):
    return jnp.take_along_axis(values, lane, axis=1, mode="promise_in_bounds")


def halo_kernel(
    channels, last, a_ref, own_b_ref, other_b_ref, partial_ref, taps_ref, pick_ref, out_ref
):
    out_rows = out_ref.shape[0]
    cell = lax.axis_index("cell")
    b = mean_of(own_b_ref[...], other_b_ref[...], channels)
    b = jnp.where((cell == 0) | (cell == last), 0.0, b)
    a = a_ref[...]
    halo = jnp.concatenate([a[:, :channels], a[:, channels:], b[:, :channels]], axis=0)
    high, low = halves(halo)
    cells = halo.shape[0]
    turns = LANES // cells
    halo = jnp.concatenate([jnp.concatenate([high, low, high], axis=1)] * turns, axis=0)
    edge = dot(taps_ref[...], halo, NT, None)
    lane = iota((out_rows, LANES), 1)
    groups = []
    for start in range(0, edge.shape[0], turns * out_rows):
        group = edge[start : start + out_rows]
        for turn in range(1, turns):
            rows = edge[start + turn * out_rows : start + (turn + 1) * out_rows]
            group = jnp.where(lane >= turn * cells, rows, group)
        groups.append(group)
    high, low = halves(jnp.concatenate(groups, axis=1))
    pick = pick_ref[...]
    out_ref[...] = partial_ref[...] + (dot(high, pick, NN, None) + dot(low, pick, NN, None))


def swaps(sensors, cells):
    def listed(partner):
        return [(s * cells + c, partner(s, c)) for s in range(sensors) for c in range(cells)]

    def far(flip):
        def partner(s, c):
            if c in (0, cells - 1):
                return (s ^ 1) * cells + c
            return (s ^ flip) * cells + ((c - 1) ^ 1) + 1

        return listed(partner)

    near = listed(lambda s, c: s * cells + (c ^ 1))

    def across(flip):
        return listed(lambda s, c: (s ^ flip) * cells + c)

    return near, far, across


def on_device(
    swath,
    enc_weight,
    key_weight,
    value_weight,
    cell_query,
    quality,
    sample_cell,
    live,
    neighbours,
    hp_weight,
):
    sensors, ranges = lax.axis_size("sensor"), lax.axis_size("cell")
    channels = swath.shape[1]
    cells = cell_query.shape[1]
    side = math.isqrt(cells)
    out_rows = channels // sensors
    stencil = hp_weight.shape[1] // channels
    vmem = pl.BlockSpec(memory_space=pltpu.VMEM)
    axes = ("sensor", "cell")
    near, far, across = swaps(sensors, ranges)

    def shape(*sizes, dtype=jnp.float32):
        return jax.ShapeDtypeStruct(sizes, dtype)

    def call(kernel, args, outs, cost=None, **more):
        single = not isinstance(outs, list)
        specs = dict(in_specs=[vmem] * len(args), out_specs=vmem if single else [vmem] * len(outs))
        specs.update(more)
        return pl.pallas_call(
            kernel,
            out_shape=outs,
            compiler_params=pltpu.CompilerParams(vmem_limit_bytes=8 * 1024 * 1024),
            cost_estimate=cost
            and pl.CostEstimate(flops=cost, bytes_accessed=cost // 100, transcendentals=0),
            **specs,
        )(*args)

    def bound(kernel):
        return lambda *refs: kernel(channels, *refs)

    hbm = pl.BlockSpec(memory_space=pltpu.HBM)

    def pinned(*args):
        return [pltpu.with_memory_space_constraint(a, pltpu.HBM) for a in args]

    def like(*args):
        return [shape(*a.shape, dtype=a.dtype) for a in args]

    args = [swath, enc_weight, key_weight, cell_query, quality, sample_cell]
    swath, enc_weight, key_weight, cell_query, quality, sample_cell, tail = call(
        load_kernel,
        pinned(*args),
        like(*args) + [shape(ROWS, LANES)],
        in_specs=[hbm] * len(args),
        scratch_shapes=[
            pltpu.VMEM((channels, LANES), jnp.float32),
            pltpu.SemaphoreType.DMA((len(args) + 1,)),
        ],
    )
    tail_b = lax.ppermute(tail, axes, far(0))
    tail_again = call(copy_kernel, [tail], shape(*tail.shape), cost=100_000_000)
    tail_a = lax.ppermute(tail_again, axes, near)

    args = [value_weight, neighbours, hp_weight]
    before, late_taps, ids, late_kq, late_rest, rest, rest_pack, *loaded = call(
        prepare_kernel,
        [swath, enc_weight, key_weight, cell_query, quality, sample_cell, live] + pinned(*args),
        [
            shape(ROWS, channels),
            shape(channels, 6 * LATE * channels, dtype=jnp.bfloat16),
            shape(1, LANES, dtype=jnp.int32),
            shape(ROWS, LANES),
            shape(ROWS, LANES),
            shape(cells // 2 + ROWS, LANES),
            shape(side, LANES),
        ]
        + like(*args),
        cost=200_000_000,
        in_specs=[vmem] * 6 + [pl.BlockSpec(memory_space=pltpu.SMEM)] + [hbm] * len(args),
        scratch_shapes=[pltpu.VMEM((cells, LANES), jnp.float32)] * 2
        + [pltpu.SemaphoreType.DMA((len(args),))],
    )
    stats, pack = call(
        pool_kernel,
        [
            late_taps,
            tail_a,
            tail_b,
            before,
            ids,
            quality,
            late_kq,
            late_rest,
            rest,
            rest_pack,
        ],
        [shape(*rest.shape), shape(*rest_pack.shape)],
    )

    flip = 1
    while flip * 2 < sensors:
        other, other_pack = (lax.ppermute(v, axes, across(flip)) for v in (stats, pack))
        stats = call(merge_kernel, [stats, other], shape(*stats.shape))
        pack = call(bound(merge_pack_kernel), [pack, other_pack], shape(*pack.shape))
        flip *= 2

    other = lax.ppermute(stats, axes, across(flip))
    other_b = lax.ppermute(pack, axes, far(flip))
    pack_again = call(copy_kernel, [pack], shape(*pack.shape), cost=100_000_000)
    hpv, taps, code, pick = call(
        weights_kernel,
        loaded + [pack_again],
        [
            shape(stencil * out_rows, channels),
            shape((stencil - 1) * out_rows, 3 * channels, dtype=jnp.bfloat16),
            shape(*neighbours.shape, dtype=jnp.int32),
            shape((stencil - 1) * 2 * side, cells, dtype=jnp.bfloat16),
        ],
        cost=100_000_000,
    )
    own_b = lax.ppermute(pack_again, axes, far(0))
    mean, mean_a = call(
        mean_kernel,
        [stats, other],
        [shape(cells // 2, LANES), shape(side // 2, LANES)],
    )
    halo_a = lax.ppermute(mean_a, axes, near)
    partial = call(own_kernel, [mean, hpv, code], shape(out_rows, cells), cost=200_000_000)
    return call(
        functools.partial(halo_kernel, channels, ranges - 1),
        [halo_a, own_b, other_b, partial, taps, pick],
        shape(out_rows, cells),
    )


def solution(mesh):
    in_specs = (
        P("sensor", None, "cell"),
        P("sensor", None, None),
        P(),
        P(),
        P(None, "cell"),
        P("sensor", "cell"),
        P("sensor", "cell"),
        P("sensor", "cell"),
        P(None, "cell"),
        P(),
    )
    out_specs = P("sensor", "cell")
    return jax.shard_map(
        on_device, mesh=mesh, in_specs=in_specs, out_specs=out_specs, check_vma=False
    )
```

```python
import functools
import math

import jax
import jax.numpy as jnp
from jax import lax
from jax.experimental import pallas as pl
from jax.experimental.pallas import tpu as pltpu
from jax.sharding import PartitionSpec as P

FLOOR = -1e30
LANES = 128
ROWS = 8
LATE = 2
EXACT = lax.Precision.HIGHEST
CLOSE = lax.Precision.HIGH
NN = ((1,), (0,))
NT = ((1,), (1,))
TN = ((0,), (0,))


def dot(left, right, contract, precision=EXACT):
    return lax.dot_general(
        left,
        right,
        (contract, ((), ())),
        precision=precision,
        preferred_element_type=jnp.float32,
    )


def iota(shape, dim):
    return lax.broadcasted_iota(jnp.int32, shape, dim)


def gelu(x):
    return 0.5 * x * (1.0 + lax.erf(x * math.sqrt(0.5)))


def widened(value, lanes=LANES):
    gap = jnp.zeros((value.shape[0], lanes - value.shape[1]), value.dtype)
    return jnp.concatenate([value, gap], axis=1)


def with_peak(block, peak, channels):
    return jnp.where(iota(block.shape, 1) == channels + 1, peak, block)


def merged(first, second, channels):
    first_peak, second_peak = (v[:, channels + 1 : channels + 2] for v in (first, second))
    peak = jnp.maximum(first_peak, second_peak)
    both = first * jnp.exp(first_peak - peak) + second * jnp.exp(second_peak - peak)
    return both, peak


def twice(value):
    half = value[:, : LANES // 2]
    return jnp.concatenate([half, half], axis=1)


def mean_of(first, second, channels):
    (first_total, first_peak), (second_total, second_peak) = (
        [v[:, channels + i : channels + i + 1] for i in range(2)] for v in (first, second)
    )
    peak = jnp.maximum(first_peak, second_peak)
    first_factor, second_factor = jnp.exp(first_peak - peak), jnp.exp(second_peak - peak)
    total = first_total * first_factor + second_total * second_factor
    return twice(first) * (first_factor / total) + twice(second) * (second_factor / total)


def load_kernel(*refs):
    *refs, tail_ref, last_ref, sems = refs
    count = len(refs) // 2
    sources, targets = refs[:count], refs[count:]
    swath_ref = sources[0]
    copies = [(swath_ref.at[0, :, pl.ds(swath_ref.shape[2] - LANES, LANES)], last_ref)]
    hp_ref, own_hp_ref = sources[-1], targets[-1]
    out_rows = own_hp_ref.shape[0]
    start = pl.multiple_of(lax.axis_index("sensor") * out_rows, ROWS)
    copies += [(hp_ref.at[pl.ds(start, out_rows), :], own_hp_ref)]
    copies += list(zip(sources[:-1], targets[:-1]))
    copies = [pltpu.make_async_copy(*ends, sems.at[i]) for i, ends in enumerate(copies)]
    for copy in copies:
        copy.start()
    copies[0].wait()
    last = jnp.transpose(last_ref[...])[LANES - LATE :, :]
    gap = jnp.zeros(last.shape, jnp.float32)
    two = jnp.concatenate([last, jnp.concatenate([last[1:], gap[1:]], axis=0)], axis=1)
    tail_ref[...] = jnp.concatenate([two] + [jnp.zeros(two.shape, jnp.float32)] * 3, axis=0)
    for copy in copies[1:]:
        copy.wait()


def halves(value):
    high = value.astype(jnp.bfloat16)
    return high, (value - high.astype(jnp.float32)).astype(jnp.bfloat16)


def parts(value):
    high = value.astype(jnp.bfloat16)
    rest = value - high.astype(jnp.float32)
    middle = rest.astype(jnp.bfloat16)
    return high, middle, (rest - middle.astype(jnp.float32)).astype(jnp.bfloat16)


def packed(block, channels):
    half = block.shape[0] // 2
    sums = jnp.concatenate([block[:half, :channels], block[half:, :channels]], axis=1)
    total, peak = (block[:, channels + i : channels + i + 1] for i in range(2))
    lane = iota((half, LANES), 1)
    columns = jnp.where(lane == 0, total[:half], jnp.where(lane == 1, total[half:], 0.0))
    columns = jnp.where(lane == 2, peak[:half], jnp.where(lane == 3, peak[half:], columns))
    return sums, jnp.transpose(columns)[:ROWS, :]


def prepare_kernel(
    swath_ref,
    enc_ref,
    key_ref,
    query_ref,
    quality_ref,
    cell_ref,
    live_ref,
    before_ref,
    taps_ref,
    ids_ref,
    late_ref,
    stats_ref,
    pack_ref,
    kq_ref,
    block_ref,
):
    sensor = lax.axis_index("sensor")
    odd = lax.rem(lax.axis_index("cell"), 2)
    channels, slots = swath_ref.shape[1:]
    cells = query_ref.shape[1]
    side, half = pack_ref.shape[0], cells // 2

    signal = swath_ref[0]
    one = jnp.concatenate([jnp.zeros((channels, 1), jnp.float32), signal[:, : slots - 1]], axis=1)
    two = jnp.concatenate([jnp.zeros((channels, 2), jnp.float32), signal[:, : slots - 2]], axis=1)
    stacked = jnp.concatenate([two, one, signal], axis=0)
    before = dot(enc_ref[0], stacked, NN)
    first = before[:, :LANES]
    before_ref[...] = jnp.transpose(jnp.concatenate([first, first], axis=0))[:ROWS, :]
    encoded = gelu(before)

    query = query_ref[...]
    key_query = dot(key_ref[...], query, TN) * (1.0 / math.sqrt(channels))
    key_query = jnp.transpose(jnp.concatenate([key_query, key_query], axis=0))
    query = jnp.transpose(jnp.concatenate([query, jnp.zeros(query.shape, jnp.float32)], axis=0))
    kq_ref[...] = key_query
    own_score = jnp.sum(query * key_query, axis=1, keepdims=True)
    own_score = jnp.where(sensor == 0, own_score, -jnp.inf)

    high, middle, low = parts(key_query)
    mixed = jnp.where(iota(high.shape, 1) < channels, high, low)
    token_high, token_middle, token_low = parts(encoded)
    score = dot(
        jnp.concatenate([high, middle, mixed], axis=1),
        jnp.concatenate(
            [token_high, token_middle, token_high, token_middle, token_low, token_high], axis=0
        ),
        NN,
        None,
    )
    slot = iota((1, slots), 1)
    ids = jnp.where(slot < live_ref[0, 0], cell_ref[...], -1)
    late_ids = [ids[:, j : j + 1] for j in range(LATE)]
    ids = jnp.where(slot < LATE, -1, ids)
    score = jnp.where(iota((cells, slots), 0) == ids, score + quality_ref[...], -jnp.inf)
    peak = jnp.maximum(jnp.max(score, axis=1, keepdims=True), jnp.maximum(own_score, FLOOR))
    weights = jnp.exp(score - peak)
    place = iota((LANES - channels, slots), 0)
    tokens = jnp.concatenate([encoded, (place == 0).astype(jnp.float32)], axis=0)
    high, low = halves(jnp.transpose(tokens))
    weights_high, weights_low = halves(weights)
    wide = dot(weights_high, jnp.concatenate([high, low], axis=1), NN, None)
    block = wide[:, :LANES] + wide[:, LANES:] + dot(weights_low, high, NN, None)
    own = jnp.where(iota(query.shape, 1) == channels, 1.0, query)
    block = with_peak(block + own * jnp.exp(own_score - peak), peak, channels)
    block_ref[...] = block
    stats_ref[:half, :], stats_ref[half:, :] = packed(block, channels)
    left = block_ref[pl.ds(0, side, stride=side), :]
    right = block_ref[pl.ds(side - 1, side, stride=side), :]
    pack_ref[...] = jnp.where(odd == 1, right, left)
    gap = jnp.zeros((ROWS - LATE, LANES), jnp.float32)

    def listed(rows):
        return jnp.concatenate([jnp.broadcast_to(r, (1, LANES)) for r in rows] + [gap], axis=0)

    at = [pl.ds(cell_ref[0, j], 1) for j in range(LATE)]
    key_query = listed([kq_ref[a, :] for a in at])
    rest = listed([block_ref[a, :] for a in at])
    late_ref[0] = jnp.where(iota(key_query.shape, 1) < channels, key_query, 0.0)
    late_ref[1] = twice(rest)
    for i in range(2):
        late_ref[2 + i] = jnp.broadcast_to(rest[:, channels + i : channels + i + 1], rest.shape)
    late_ref[4] = listed([quality_ref[:, j : j + 1] for j in range(LATE)])
    same = jnp.where(late_ids[0] == late_ids[1], 0.0, -jnp.inf)
    late_ref[5] = listed([same] * LATE)
    ids_ref[...] = jnp.concatenate(
        [jnp.broadcast_to(i, (1, LANES)) for i in late_ids] + [gap.astype(jnp.int32)], axis=0
    )
    high, middle, low = parts(enc_ref[0, :, : LATE * channels])
    taps = jnp.concatenate([high, high, middle, high, middle, low], axis=1)
    taps_ref[...] = jnp.concatenate([taps, taps], axis=0)


def swapped(value):
    return jnp.concatenate([value[1:2], value[0:1], value[2:]], axis=0)


def pool_kernel(
    taps_ref,
    tail_a_ref,
    tail_b_ref,
    before_ref,
    ids_ref,
    late_ref,
    rest_ref,
    rest_pack_ref,
    stats_ref,
    pack_ref,
):
    cell = lax.axis_index("cell")
    odd = lax.rem(cell, 2)
    side, half = pack_ref.shape[0], stats_ref.shape[0] - ROWS
    channels = LANES // 2
    tail = jnp.where(odd == 1, tail_a_ref[...], tail_b_ref[...])
    tail = jnp.where(cell == 0, 0.0, tail)
    high, middle, low = parts(jnp.concatenate([tail, jnp.zeros(tail.shape, jnp.float32)], axis=0))
    tail = jnp.concatenate([high, middle, high, low, middle, high], axis=1)
    tokens = gelu(before_ref[...] + dot(tail, taps_ref[...], NT, None)[:ROWS, :])

    key_query, rest, rest_total, rest_peak, quality, same = (late_ref[i] for i in range(6))
    score = jnp.sum(tokens * key_query, axis=1, keepdims=True) + quality
    other = swapped(score) + same
    peak = jnp.maximum(rest_peak, jnp.maximum(score, other))
    rest_factor, weight, other_weight = (jnp.exp(v - peak) for v in (rest_peak, score, other))
    rows = rest * rest_factor + tokens * weight + swapped(tokens) * other_weight
    totals = rest_total * rest_factor + weight + other_weight

    sums, ends, pack = rest_ref[:half, :], rest_ref[half:, :], rest_pack_ref[...]
    of_sum = iota(sums.shape, 0) + jnp.where(iota(sums.shape, 1) < channels, 0, half)
    kind = iota(ends.shape, 0)
    of_end = iota(ends.shape, 1) + jnp.where(lax.rem(kind, 2) == 0, 0, half)
    of_end = jnp.where(kind < 4, of_end, 2 * half)
    of_pack = iota(pack.shape, 0) * side + jnp.where(odd == 1, side - 1, 0)
    lane = iota((1, LANES), 1)
    for j in range(LATE):
        at, row, total, top = (v[j : j + 1] for v in (ids_ref[...], rows, totals, peak))
        sums = jnp.where(of_sum == at, row, sums)
        ends = jnp.where(of_end == at, jnp.where(kind < 2, total, top), ends)
        row = jnp.where(lane < channels, row, jnp.where(lane == channels, total, top))
        pack = jnp.where(of_pack == at, row, pack)
    stats_ref[:half, :], stats_ref[half:, :] = sums, ends
    pack_ref[...] = pack


def shares(first, second):
    peak = jnp.maximum(first[2:4], second[2:4])
    first_factor = jnp.exp(first[2:4] - peak)
    second_factor = jnp.exp(second[2:4] - peak)
    total = first[0:2] * first_factor + second[0:2] * second_factor
    return first_factor, second_factor, total, peak


def turned(*rows):
    rows = jnp.concatenate(rows, axis=0)
    gap = jnp.zeros((LANES - rows.shape[0], rows.shape[1]), jnp.float32)
    return jnp.transpose(jnp.concatenate([rows, gap], axis=0))


def spread(columns, count):
    left = iota((columns.shape[0], LANES), 1) < LANES // 2
    return [
        jnp.where(left, columns[:, 2 * i : 2 * i + 1], columns[:, 2 * i + 1 : 2 * i + 2])
        for i in range(count)
    ]


def merge_pack_kernel(channels, own_ref, other_ref, out_ref):
    both, peak = merged(own_ref[...], other_ref[...], channels)
    out_ref[...] = with_peak(both, peak, channels)


def merge_kernel(own_ref, other_ref, out_ref):
    half = own_ref.shape[0] - ROWS
    first_factor, second_factor, total, peak = shares(own_ref[half:, :], other_ref[half:, :])
    first_factor, second_factor = spread(turned(first_factor, second_factor), 2)
    out_ref[:half, :] = own_ref[:half, :] * first_factor + other_ref[:half, :] * second_factor
    rest = jnp.zeros((ROWS - 4, total.shape[1]), jnp.float32)
    out_ref[half:, :] = jnp.concatenate([total, peak, rest], axis=0)


def copy_kernel(in_ref, out_ref):
    out_ref[...] = in_ref[...]


def weights_kernel(value_ref, near_ref, hp_ref, after_ref, hpv_ref, taps_ref, code_ref, pick_ref):
    del after_ref
    cell = lax.axis_index("cell")
    channels = value_ref.shape[0]
    cells = near_ref.shape[1]
    side = math.isqrt(cells)
    out_rows, own_hp = hp_ref.shape[0], hp_ref[...]
    value = value_ref[...]
    taps = [
        own_hp[:, k * channels : (k + 1) * channels] for k in range(hp_ref.shape[1] // channels)
    ]
    hpv = dot(jnp.concatenate(taps, axis=0), value, NN)
    hpv_ref[...] = hpv
    high, low = halves(hpv[out_rows:])
    gap = jnp.zeros(low.shape, jnp.float32).astype(jnp.bfloat16)
    taps_ref[...] = jnp.concatenate([high, high, low, gap], axis=1)

    shift = side.bit_length() - 1
    odd = lax.rem(cell, 2)
    offset = near_ref[...] - cell * cells
    after = cells + odd * side + lax.shift_right_arithmetic(offset - cells, shift)
    ahead = cells + (1 - odd) * side + lax.shift_right_arithmetic(offset + cells, shift)
    code_ref[...] = jnp.where(offset < 0, ahead, jnp.where(offset < cells, offset, after))
    halo = code_ref[...] - cells
    place = iota((2 * side, cells), 0)
    for k in range(halo.shape[0]):
        here = (place == halo[k : k + 1, :]).astype(jnp.float32).astype(jnp.bfloat16)
        pick_ref[2 * side * k : 2 * side * (k + 1), :] = here


def mean_kernel(own_ref, other_ref, pack_ref, columns_ref):
    odd = lax.rem(lax.axis_index("cell"), 2)
    half = own_ref.shape[0] - ROWS
    count = pack_ref.shape[0]
    side = half // count
    first_factor, second_factor, total, _ = shares(own_ref[half:, :], other_ref[half:, :])
    columns_ref[...] = turned(first_factor / total, second_factor / total)

    def column(ref):
        left = ref[pl.ds(0, count, stride=side), :]
        return jnp.where(odd == 1, left, ref[pl.ds(side - 1, count, stride=side), :])

    first_share, second_share = spread(column(columns_ref), 2)
    pack_ref[...] = column(own_ref) * first_share + column(other_ref) * second_share


def own_kernel(own_ref, other_ref, hpv_ref, code_ref, out_ref):
    out_rows, cells = out_ref.shape
    half = own_ref.shape[0] - ROWS
    first_factor, second_factor, total, _ = shares(own_ref[half:, :], other_ref[half:, :])
    columns = turned(first_factor / total, second_factor / total)
    first_share, second_share = spread(columns, 2)
    mean = own_ref[:half, :] * first_share + other_ref[:half, :] * second_share
    hpv = hpv_ref[...]
    gap = jnp.zeros(hpv.shape, jnp.float32)
    mixed = [
        dot(jnp.concatenate(pair, axis=1), mean, NT, CLOSE) for pair in ((hpv, gap), (gap, hpv))
    ]
    lanes = lax.bitwise_and(code_ref[...], LANES - 1)
    places = lax.shift_right_logical(code_ref[...], LANES.bit_length() - 1)
    for i, start in enumerate(range(0, cells, LANES)):
        total = mixed[i][:out_rows]
        for k in range(code_ref.shape[0]):
            rows = slice((k + 1) * out_rows, (k + 2) * out_rows)
            lane, place = (
                jnp.broadcast_to(v[k : k + 1, start : start + LANES], total.shape)
                for v in (lanes, places)
            )
            taken = 0.0
            for source, values in enumerate(mixed):
                here = taken_lanes(values[rows], lane)
                taken = jnp.where(place == source, here, taken)
            total = total + taken
        out_ref[:, start : start + LANES] = total


def taken_lanes(values, lane):
    return jnp.take_along_axis(values, lane, axis=1, mode="promise_in_bounds")


def halo_kernel(
    channels, last, a_ref, own_b_ref, other_b_ref, partial_ref, taps_ref, pick_ref, out_ref
):
    out_rows = out_ref.shape[0]
    cell = lax.axis_index("cell")
    b = mean_of(own_b_ref[...], other_b_ref[...], channels)
    b = jnp.where((cell == 0) | (cell == last), 0.0, b)
    a = a_ref[...]
    a = [twice(a), twice(jnp.concatenate([a[:, channels:], a[:, :channels]], axis=1))]
    halo = jnp.concatenate(a + [b], axis=0)
    cells = halo.shape[0]
    turns = LANES // cells
    left = iota(halo.shape, 1) < channels
    high = halo.astype(jnp.bfloat16).astype(jnp.float32)
    halo = jnp.concatenate(
        [jnp.where(left, high, halo - high), jnp.where(left, high, 0.0)], axis=1
    ).astype(jnp.bfloat16)
    edge = dot(taps_ref[...], jnp.concatenate([halo] * turns, axis=0), NT, None)
    lane = iota((out_rows, LANES), 1)
    groups = []
    for start in range(0, edge.shape[0], turns * out_rows):
        group = edge[start : start + out_rows]
        for turn in range(1, turns):
            rows = edge[start + turn * out_rows : start + (turn + 1) * out_rows]
            group = jnp.where(lane >= turn * cells, rows, group)
        groups.append(group)
    high, low = halves(jnp.concatenate(groups, axis=1))
    pick = pick_ref[...]
    out_ref[...] = partial_ref[...] + (dot(high, pick, NN, None) + dot(low, pick, NN, None))


def swaps(sensors, cells):
    def listed(partner):
        return [(s * cells + c, partner(s, c)) for s in range(sensors) for c in range(cells)]

    def far(flip):
        def partner(s, c):
            if c in (0, cells - 1):
                return (s ^ 1) * cells + c
            return (s ^ flip) * cells + ((c - 1) ^ 1) + 1

        return listed(partner)

    near = listed(lambda s, c: s * cells + (c ^ 1))

    def across(flip):
        return listed(lambda s, c: (s ^ flip) * cells + c)

    return near, far, across


def on_device(
    swath,
    enc_weight,
    key_weight,
    value_weight,
    cell_query,
    quality,
    sample_cell,
    live,
    neighbours,
    hp_weight,
):
    sensors, ranges = lax.axis_size("sensor"), lax.axis_size("cell")
    channels = swath.shape[1]
    cells = cell_query.shape[1]
    side = math.isqrt(cells)
    out_rows = channels // sensors
    stencil = hp_weight.shape[1] // channels
    vmem = pl.BlockSpec(memory_space=pltpu.VMEM)
    axes = ("sensor", "cell")
    near, far, across = swaps(sensors, ranges)

    def shape(*sizes, dtype=jnp.float32):
        return jax.ShapeDtypeStruct(sizes, dtype)

    def call(kernel, args, outs, cost=None, **more):
        single = not isinstance(outs, list)
        specs = dict(in_specs=[vmem] * len(args), out_specs=vmem if single else [vmem] * len(outs))
        specs.update(more)
        return pl.pallas_call(
            kernel,
            out_shape=outs,
            compiler_params=pltpu.CompilerParams(vmem_limit_bytes=8 * 1024 * 1024),
            cost_estimate=cost
            and pl.CostEstimate(flops=cost, bytes_accessed=cost // 100, transcendentals=0),
            **specs,
        )(*args)

    def bound(kernel):
        return lambda *refs: kernel(channels, *refs)

    hbm = pl.BlockSpec(memory_space=pltpu.HBM)

    def pinned(*args):
        return [pltpu.with_memory_space_constraint(a, pltpu.HBM) for a in args]

    def like(*args):
        return [shape(*a.shape, dtype=a.dtype) for a in args]

    args = [
        swath,
        cell_query,
        enc_weight,
        key_weight,
        quality,
        sample_cell,
        value_weight,
        neighbours,
        hp_weight,
    ]
    *loaded, tail = call(
        load_kernel,
        pinned(*args),
        like(*args[:-1]) + [shape(out_rows, hp_weight.shape[1]), shape(ROWS, LANES)],
        in_specs=[hbm] * len(args),
        scratch_shapes=[
            pltpu.VMEM((channels, LANES), jnp.float32),
            pltpu.SemaphoreType.DMA((len(args) + 1,)),
        ],
    )
    swath, cell_query, enc_weight, key_weight, quality, sample_cell, *loaded = loaded
    tail_b = lax.ppermute(tail, axes, far(0))
    tail_again = call(copy_kernel, [tail], shape(*tail.shape), cost=100_000_000)
    tail_a = lax.ppermute(tail_again, axes, near)

    before, late_taps, ids, late, rest, rest_pack = call(
        prepare_kernel,
        [swath, enc_weight, key_weight, cell_query, quality, sample_cell, live],
        [
            shape(ROWS, 2 * channels),
            shape(2 * channels, 6 * LATE * channels, dtype=jnp.bfloat16),
            shape(ROWS, LANES, dtype=jnp.int32),
            shape(6, ROWS, LANES),
            shape(cells // 2 + ROWS, LANES),
            shape(side, LANES),
        ],
        cost=200_000_000,
        in_specs=[vmem] * 6 + [pl.BlockSpec(memory_space=pltpu.SMEM)],
        scratch_shapes=[pltpu.VMEM((cells, LANES), jnp.float32)] * 2,
    )
    stats, pack = call(
        pool_kernel,
        [
            late_taps,
            tail_a,
            tail_b,
            before,
            ids,
            late,
            rest,
            rest_pack,
        ],
        [shape(*rest.shape), shape(*rest_pack.shape)],
    )

    flip = 1
    while flip * 2 < sensors:
        other, other_pack = (lax.ppermute(v, axes, across(flip)) for v in (stats, pack))
        stats = call(merge_kernel, [stats, other], shape(*stats.shape))
        pack = call(bound(merge_pack_kernel), [pack, other_pack], shape(*pack.shape))
        flip *= 2

    other = lax.ppermute(stats, axes, across(flip))
    other_b = lax.ppermute(pack, axes, far(flip))
    pack_again = call(copy_kernel, [pack], shape(*pack.shape), cost=100_000_000)
    hpv, taps, code, pick = call(
        weights_kernel,
        loaded + [pack_again],
        [
            shape(stencil * out_rows, channels),
            shape((stencil - 1) * out_rows, 4 * channels, dtype=jnp.bfloat16),
            shape(*neighbours.shape, dtype=jnp.int32),
            shape((stencil - 1) * 2 * side, cells, dtype=jnp.bfloat16),
        ],
        cost=100_000_000,
    )
    own_b = lax.ppermute(pack_again, axes, far(0))
    mean_a = call(
        mean_kernel,
        [stats, other],
        shape(side // 2, LANES),
        scratch_shapes=[pltpu.VMEM((cells // 2, LANES), jnp.float32)],
    )
    halo_a = lax.ppermute(mean_a, axes, near)
    partial = call(own_kernel, [stats, other, hpv, code], shape(out_rows, cells), cost=200_000_000)
    return call(
        functools.partial(halo_kernel, channels, ranges - 1),
        [halo_a, own_b, other_b, partial, taps, pick],
        shape(out_rows, cells),
    )


def solution(mesh):
    in_specs = (
        P("sensor", None, "cell"),
        P("sensor", None, None),
        P(),
        P(),
        P(None, "cell"),
        P("sensor", "cell"),
        P("sensor", "cell"),
        P("sensor", "cell"),
        P(None, "cell"),
        P(),
    )
    out_specs = P("sensor", "cell")
    return jax.shard_map(
        on_device, mesh=mesh, in_specs=in_specs, out_specs=out_specs, check_vma=False
    )
```

```python
import functools
import math

import jax
import jax.numpy as jnp
from jax import lax
from jax.experimental import pallas as pl
from jax.experimental.pallas import tpu as pltpu
from jax.sharding import PartitionSpec as P

FLOOR = -1e30
LANES = 128
ROWS = 8
LATE = 2
EXACT = lax.Precision.HIGHEST
CLOSE = lax.Precision.HIGH
NN = ((1,), (0,))
NT = ((1,), (1,))


def dot(left, right, contract, precision=EXACT):
    return lax.dot_general(
        left,
        right,
        (contract, ((), ())),
        precision=precision,
        preferred_element_type=jnp.float32,
    )


def by_half(left, right, contract):
    half = left.shape[0] // 2
    return jnp.concatenate(
        [dot(rows, right, contract, None) for rows in (left[:half], left[half:])], axis=0
    )


def iota(shape, dim):
    return lax.broadcasted_iota(jnp.int32, shape, dim)


def gelu(x):
    return 0.5 * x * (1.0 + lax.erf(x * math.sqrt(0.5)))


def widened(value, lanes=LANES):
    gap = jnp.zeros((value.shape[0], lanes - value.shape[1]), value.dtype)
    return jnp.concatenate([value, gap], axis=1)


def with_peak(block, peak, channels):
    return jnp.where(iota(block.shape, 1) == channels + 1, peak, block)


def merged(first, second, channels):
    first_peak, second_peak = (v[:, channels + 1 : channels + 2] for v in (first, second))
    peak = jnp.maximum(first_peak, second_peak)
    both = first * jnp.exp(first_peak - peak) + second * jnp.exp(second_peak - peak)
    return both, peak


def twice(value):
    half = value[:, : LANES // 2]
    return jnp.concatenate([half, half], axis=1)


def mean_of(first, second, channels):
    (first_total, first_peak), (second_total, second_peak) = (
        [v[:, channels + i : channels + i + 1] for i in range(2)] for v in (first, second)
    )
    peak = jnp.maximum(first_peak, second_peak)
    first_factor, second_factor = jnp.exp(first_peak - peak), jnp.exp(second_peak - peak)
    total = first_total * first_factor + second_total * second_factor
    return twice(first) * (first_factor / total) + twice(second) * (second_factor / total)


def load_kernel(*refs):
    *refs, tail_ref, last_ref, sems = refs
    count = len(refs) // 2
    sources, targets = refs[:count], refs[count:]
    swath_ref = sources[0]
    copies = [(swath_ref.at[0, :, pl.ds(swath_ref.shape[2] - LANES, LANES)], last_ref)]
    hp_ref, own_hp_ref = sources[-1], targets[-1]
    out_rows = own_hp_ref.shape[0]
    start = pl.multiple_of(lax.axis_index("sensor") * out_rows, ROWS)
    copies += [(hp_ref.at[pl.ds(start, out_rows), :], own_hp_ref)]
    copies += list(zip(sources[:-1], targets[:-1]))
    copies = [pltpu.make_async_copy(*ends, sems.at[i]) for i, ends in enumerate(copies)]
    for copy in copies:
        copy.start()
    copies[0].wait()
    last = jnp.transpose(last_ref[...])[LANES - LATE :, :]
    gap = jnp.zeros(last.shape, jnp.float32)
    two = jnp.concatenate([last, jnp.concatenate([last[1:], gap[1:]], axis=0)], axis=1)
    tail_ref[...] = jnp.concatenate([two] + [jnp.zeros(two.shape, jnp.float32)] * 3, axis=0)
    for copy in copies[1:]:
        copy.wait()


def halves(value):
    high = value.astype(jnp.bfloat16)
    return high, (value - high.astype(jnp.float32)).astype(jnp.bfloat16)


def parts(value):
    high = value.astype(jnp.bfloat16)
    rest = value - high.astype(jnp.float32)
    middle = rest.astype(jnp.bfloat16)
    return high, middle, (rest - middle.astype(jnp.float32)).astype(jnp.bfloat16)


def exact(twofold, right):
    high, middle, low = parts(twofold)
    mixed = jnp.where(iota(high.shape, 1) < right.shape[0], high, low)
    right_high, right_middle, right_low = parts(right)
    return dot(
        jnp.concatenate([high, middle, mixed], axis=1),
        jnp.concatenate(
            [right_high, right_middle, right_high, right_middle, right_low, right_high], axis=0
        ),
        NN,
        None,
    )


def packed(block, channels):
    half = block.shape[0] // 2
    sums = jnp.concatenate([block[:half, :channels], block[half:, :channels]], axis=1)
    total, peak = (block[:, channels + i : channels + i + 1] for i in range(2))
    lane = iota((half, LANES), 1)
    columns = jnp.where(lane == 0, total[:half], jnp.where(lane == 1, total[half:], 0.0))
    columns = jnp.where(lane == 2, peak[:half], jnp.where(lane == 3, peak[half:], columns))
    return sums, jnp.transpose(columns)[:ROWS, :]


def prepare_kernel(
    swath_ref,
    enc_ref,
    key_ref,
    query_ref,
    quality_ref,
    cell_ref,
    live_ref,
    before_ref,
    taps_ref,
    ids_ref,
    late_ref,
    stats_ref,
    pack_ref,
    kq_ref,
    block_ref,
):
    sensor = lax.axis_index("sensor")
    odd = lax.rem(lax.axis_index("cell"), 2)
    channels, slots = swath_ref.shape[1:]
    cells = query_ref.shape[1]
    side, half = pack_ref.shape[0], cells // 2

    signal = swath_ref[0]
    one = jnp.concatenate([jnp.zeros((channels, 1), jnp.float32), signal[:, : slots - 1]], axis=1)
    two = jnp.concatenate([jnp.zeros((channels, 2), jnp.float32), signal[:, : slots - 2]], axis=1)
    stacked = jnp.concatenate([two, one, signal], axis=0)
    before = dot(enc_ref[0], stacked, NN)
    first = before[:, :LANES]
    before_ref[...] = jnp.transpose(jnp.concatenate([first, first], axis=0))[:ROWS, :]
    encoded = gelu(before)

    query = query_ref[...]
    key = jnp.concatenate([key_ref[...]] * 2, axis=1)
    key = jnp.transpose(jnp.concatenate([key, key], axis=0))
    key_query = jnp.transpose(exact(key, query) * (1.0 / math.sqrt(channels)))
    query = jnp.transpose(jnp.concatenate([query, jnp.zeros(query.shape, jnp.float32)], axis=0))
    kq_ref[...] = key_query
    own_score = jnp.sum(query * key_query, axis=1, keepdims=True)
    own_score = jnp.where(sensor == 0, own_score, -jnp.inf)

    score = exact(key_query, encoded)
    slot = iota((1, slots), 1)
    ids = jnp.where(slot < live_ref[0, 0], cell_ref[...], -1)
    late_ids = [ids[:, j : j + 1] for j in range(LATE)]
    ids = jnp.where(slot < LATE, -1, ids)
    score = jnp.where(iota((cells, slots), 0) == ids, score + quality_ref[...], -jnp.inf)
    peak = jnp.maximum(jnp.max(score, axis=1, keepdims=True), jnp.maximum(own_score, FLOOR))
    weights = jnp.exp(score - peak)
    place = iota((LANES - channels, slots), 0)
    tokens = jnp.concatenate([encoded, (place == 0).astype(jnp.float32)], axis=0)
    high, low = halves(jnp.transpose(tokens))
    weights_high, weights_low = halves(weights)
    both = jnp.concatenate([high, low], axis=1)
    wide = by_half(weights_high, both, NN)
    block = wide[:, :LANES] + wide[:, LANES:] + by_half(weights_low, high, NN)
    own = jnp.where(iota(query.shape, 1) == channels, 1.0, query)
    block = with_peak(block + own * jnp.exp(own_score - peak), peak, channels)
    block_ref[...] = block
    stats_ref[:half, :], stats_ref[half:, :] = packed(block, channels)
    left = block_ref[pl.ds(0, side, stride=side), :]
    right = block_ref[pl.ds(side - 1, side, stride=side), :]
    pack_ref[...] = jnp.where(odd == 1, right, left)
    gap = jnp.zeros((ROWS - LATE, LANES), jnp.float32)

    def listed(rows):
        return jnp.concatenate([jnp.broadcast_to(r, (1, LANES)) for r in rows] + [gap], axis=0)

    at = [pl.ds(cell_ref[0, j], 1) for j in range(LATE)]
    key_query = listed([kq_ref[a, :] for a in at])
    rest = listed([block_ref[a, :] for a in at])
    late_ref[0] = jnp.where(iota(key_query.shape, 1) < channels, key_query, 0.0)
    late_ref[1] = twice(rest)
    for i in range(2):
        late_ref[2 + i] = jnp.broadcast_to(rest[:, channels + i : channels + i + 1], rest.shape)
    late_ref[4] = listed([quality_ref[:, j : j + 1] for j in range(LATE)])
    same = jnp.where(late_ids[0] == late_ids[1], 0.0, -jnp.inf)
    late_ref[5] = listed([same] * LATE)
    ids_ref[...] = jnp.concatenate(
        [jnp.broadcast_to(i, (1, LANES)) for i in late_ids] + [gap.astype(jnp.int32)], axis=0
    )
    high, middle, low = parts(enc_ref[0, :, : LATE * channels])
    taps = jnp.concatenate([high, high, middle, high, middle, low], axis=1)
    taps_ref[...] = jnp.concatenate([taps, taps], axis=0)


def swapped(value):
    return jnp.concatenate([value[1:2], value[0:1], value[2:]], axis=0)


def pool_kernel(
    taps_ref,
    tail_a_ref,
    tail_b_ref,
    before_ref,
    ids_ref,
    late_ref,
    rest_ref,
    rest_pack_ref,
    stats_ref,
    pack_ref,
):
    cell = lax.axis_index("cell")
    odd = lax.rem(cell, 2)
    side, half = pack_ref.shape[0], stats_ref.shape[0] - ROWS
    channels = LANES // 2
    tail = jnp.where(odd == 1, tail_a_ref[...], tail_b_ref[...])
    tail = jnp.where(cell == 0, 0.0, tail)
    high, middle, low = parts(jnp.concatenate([tail, jnp.zeros(tail.shape, jnp.float32)], axis=0))
    tail = jnp.concatenate([high, middle, high, low, middle, high], axis=1)
    tokens = gelu(before_ref[...] + dot(tail, taps_ref[...], NT, None)[:ROWS, :])

    key_query, rest, rest_total, rest_peak, quality, same = (late_ref[i] for i in range(6))
    score = jnp.sum(tokens * key_query, axis=1, keepdims=True) + quality
    other = swapped(score) + same
    peak = jnp.maximum(rest_peak, jnp.maximum(score, other))
    rest_factor, weight, other_weight = (jnp.exp(v - peak) for v in (rest_peak, score, other))
    rows = rest * rest_factor + tokens * weight + swapped(tokens) * other_weight
    totals = rest_total * rest_factor + weight + other_weight

    sums, ends, pack = rest_ref[:half, :], rest_ref[half:, :], rest_pack_ref[...]
    of_sum = iota(sums.shape, 0) + jnp.where(iota(sums.shape, 1) < channels, 0, half)
    kind = iota(ends.shape, 0)
    of_end = iota(ends.shape, 1) + jnp.where(lax.rem(kind, 2) == 0, 0, half)
    of_end = jnp.where(kind < 4, of_end, 2 * half)
    of_pack = iota(pack.shape, 0) * side + jnp.where(odd == 1, side - 1, 0)
    lane = iota((1, LANES), 1)
    for j in range(LATE):
        at, row, total, top = (v[j : j + 1] for v in (ids_ref[...], rows, totals, peak))
        sums = jnp.where(of_sum == at, row, sums)
        ends = jnp.where(of_end == at, jnp.where(kind < 2, total, top), ends)
        row = jnp.where(lane < channels, row, jnp.where(lane == channels, total, top))
        pack = jnp.where(of_pack == at, row, pack)
    stats_ref[:half, :], stats_ref[half:, :] = sums, ends
    pack_ref[...] = pack


def shares(first, second):
    peak = jnp.maximum(first[2:4], second[2:4])
    first_factor = jnp.exp(first[2:4] - peak)
    second_factor = jnp.exp(second[2:4] - peak)
    total = first[0:2] * first_factor + second[0:2] * second_factor
    return first_factor, second_factor, total, peak


def turned(*rows):
    rows = jnp.concatenate(rows, axis=0)
    gap = jnp.zeros((LANES - rows.shape[0], rows.shape[1]), jnp.float32)
    return jnp.transpose(jnp.concatenate([rows, gap], axis=0))


def spread(columns, count):
    left = iota((columns.shape[0], LANES), 1) < LANES // 2
    return [
        jnp.where(left, columns[:, 2 * i : 2 * i + 1], columns[:, 2 * i + 1 : 2 * i + 2])
        for i in range(count)
    ]


def merge_pack_kernel(channels, own_ref, other_ref, out_ref):
    both, peak = merged(own_ref[...], other_ref[...], channels)
    out_ref[...] = with_peak(both, peak, channels)


def merge_kernel(own_ref, other_ref, out_ref):
    half = own_ref.shape[0] - ROWS
    first_factor, second_factor, total, peak = shares(own_ref[half:, :], other_ref[half:, :])
    first_factor, second_factor = spread(turned(first_factor, second_factor), 2)
    out_ref[:half, :] = own_ref[:half, :] * first_factor + other_ref[:half, :] * second_factor
    rest = jnp.zeros((ROWS - 4, total.shape[1]), jnp.float32)
    out_ref[half:, :] = jnp.concatenate([total, peak, rest], axis=0)


def copy_kernel(in_ref, out_ref):
    out_ref[...] = in_ref[...]


def weights_kernel(value_ref, near_ref, hp_ref, after_ref, hpv_ref, taps_ref, code_ref, pick_ref):
    del after_ref
    cell = lax.axis_index("cell")
    channels = value_ref.shape[0]
    cells = near_ref.shape[1]
    side = math.isqrt(cells)
    out_rows, own_hp = hp_ref.shape[0], hp_ref[...]
    value = value_ref[...]
    taps = [
        own_hp[:, k * channels : (k + 1) * channels] for k in range(hp_ref.shape[1] // channels)
    ]
    hpv = dot(jnp.concatenate(taps, axis=0), value, NN)
    hpv_ref[...] = hpv
    high, low = halves(hpv[out_rows:])
    gap = jnp.zeros(low.shape, jnp.float32).astype(jnp.bfloat16)
    taps_ref[...] = jnp.concatenate([high, high, low, gap], axis=1)

    shift = side.bit_length() - 1
    odd = lax.rem(cell, 2)
    offset = near_ref[...] - cell * cells
    after = cells + odd * side + lax.shift_right_arithmetic(offset - cells, shift)
    ahead = cells + (1 - odd) * side + lax.shift_right_arithmetic(offset + cells, shift)
    code_ref[...] = jnp.where(offset < 0, ahead, jnp.where(offset < cells, offset, after))
    halo = code_ref[...] - cells
    place = iota((2 * side, cells), 0)
    for k in range(halo.shape[0]):
        here = (place == halo[k : k + 1, :]).astype(jnp.float32).astype(jnp.bfloat16)
        pick_ref[2 * side * k : 2 * side * (k + 1), :] = here


def mean_kernel(own_ref, other_ref, pack_ref, columns_ref):
    odd = lax.rem(lax.axis_index("cell"), 2)
    half = own_ref.shape[0] - ROWS
    count = pack_ref.shape[0]
    side = half // count
    first_factor, second_factor, total, _ = shares(own_ref[half:, :], other_ref[half:, :])
    columns_ref[...] = turned(first_factor / total, second_factor / total)

    def column(ref):
        left = ref[pl.ds(0, count, stride=side), :]
        return jnp.where(odd == 1, left, ref[pl.ds(side - 1, count, stride=side), :])

    first_share, second_share = spread(column(columns_ref), 2)
    pack_ref[...] = column(own_ref) * first_share + column(other_ref) * second_share


def own_kernel(own_ref, other_ref, hpv_ref, code_ref, out_ref):
    out_rows, cells = out_ref.shape
    half = own_ref.shape[0] - ROWS
    first_factor, second_factor, total, _ = shares(own_ref[half:, :], other_ref[half:, :])
    columns = turned(first_factor / total, second_factor / total)
    first_share, second_share = spread(columns, 2)
    mean = own_ref[:half, :] * first_share + other_ref[:half, :] * second_share
    hpv = hpv_ref[...]
    gap = jnp.zeros(hpv.shape, jnp.float32)
    mixed = [
        dot(jnp.concatenate(pair, axis=1), mean, NT, CLOSE) for pair in ((hpv, gap), (gap, hpv))
    ]
    lanes = lax.bitwise_and(code_ref[...], LANES - 1)
    places = lax.shift_right_logical(code_ref[...], LANES.bit_length() - 1)
    for i, start in enumerate(range(0, cells, LANES)):
        total = mixed[i][:out_rows]
        for k in range(code_ref.shape[0]):
            rows = slice((k + 1) * out_rows, (k + 2) * out_rows)
            lane, place = (
                jnp.broadcast_to(v[k : k + 1, start : start + LANES], total.shape)
                for v in (lanes, places)
            )
            taken = 0.0
            for source, values in enumerate(mixed):
                here = taken_lanes(values[rows], lane)
                taken = jnp.where(place == source, here, taken)
            total = total + taken
        out_ref[:, start : start + LANES] = total


def taken_lanes(values, lane):
    return jnp.take_along_axis(values, lane, axis=1, mode="promise_in_bounds")


def halo_kernel(
    channels, last, a_ref, own_b_ref, other_b_ref, partial_ref, taps_ref, pick_ref, out_ref
):
    out_rows = out_ref.shape[0]
    cell = lax.axis_index("cell")
    b = mean_of(own_b_ref[...], other_b_ref[...], channels)
    b = jnp.where((cell == 0) | (cell == last), 0.0, b)
    a = a_ref[...]
    a = [twice(a), twice(jnp.concatenate([a[:, channels:], a[:, :channels]], axis=1))]
    halo = jnp.concatenate(a + [b], axis=0)
    cells = halo.shape[0]
    turns = LANES // cells
    left = iota(halo.shape, 1) < channels
    high = halo.astype(jnp.bfloat16).astype(jnp.float32)
    halo = jnp.concatenate(
        [jnp.where(left, high, halo - high), jnp.where(left, high, 0.0)], axis=1
    ).astype(jnp.bfloat16)
    edge = by_half(taps_ref[...], jnp.concatenate([halo] * turns, axis=0), NT)
    lane = iota((out_rows, LANES), 1)
    groups = []
    for start in range(0, edge.shape[0], turns * out_rows):
        group = edge[start : start + out_rows]
        for turn in range(1, turns):
            rows = edge[start + turn * out_rows : start + (turn + 1) * out_rows]
            group = jnp.where(lane >= turn * cells, rows, group)
        groups.append(group)
    high, low = halves(jnp.concatenate(groups, axis=1))
    pick = pick_ref[...]
    both = dot(jnp.concatenate([high, low], axis=0), pick, NN, None)
    out_ref[...] = partial_ref[...] + (both[:out_rows] + both[out_rows:])


def swaps(sensors, cells):
    def listed(partner):
        return [(s * cells + c, partner(s, c)) for s in range(sensors) for c in range(cells)]

    def far(flip):
        def partner(s, c):
            if c in (0, cells - 1):
                return (s ^ 1) * cells + c
            return (s ^ flip) * cells + ((c - 1) ^ 1) + 1

        return listed(partner)

    near = listed(lambda s, c: s * cells + (c ^ 1))

    def across(flip):
        return listed(lambda s, c: (s ^ flip) * cells + c)

    return near, far, across


def on_device(
    swath,
    enc_weight,
    key_weight,
    value_weight,
    cell_query,
    quality,
    sample_cell,
    live,
    neighbours,
    hp_weight,
):
    sensors, ranges = lax.axis_size("sensor"), lax.axis_size("cell")
    channels = swath.shape[1]
    cells = cell_query.shape[1]
    side = math.isqrt(cells)
    out_rows = channels // sensors
    stencil = hp_weight.shape[1] // channels
    vmem = pl.BlockSpec(memory_space=pltpu.VMEM)
    axes = ("sensor", "cell")
    near, far, across = swaps(sensors, ranges)

    def shape(*sizes, dtype=jnp.float32):
        return jax.ShapeDtypeStruct(sizes, dtype)

    def call(kernel, args, outs, cost=None, **more):
        single = not isinstance(outs, list)
        specs = dict(in_specs=[vmem] * len(args), out_specs=vmem if single else [vmem] * len(outs))
        specs.update(more)
        return pl.pallas_call(
            kernel,
            out_shape=outs,
            compiler_params=pltpu.CompilerParams(vmem_limit_bytes=8 * 1024 * 1024),
            cost_estimate=cost
            and pl.CostEstimate(flops=cost, bytes_accessed=cost // 100, transcendentals=0),
            **specs,
        )(*args)

    def bound(kernel):
        return lambda *refs: kernel(channels, *refs)

    hbm = pl.BlockSpec(memory_space=pltpu.HBM)

    def pinned(*args):
        return [pltpu.with_memory_space_constraint(a, pltpu.HBM) for a in args]

    def like(*args):
        return [shape(*a.shape, dtype=a.dtype) for a in args]

    args = [
        swath,
        cell_query,
        enc_weight,
        key_weight,
        quality,
        sample_cell,
        value_weight,
        neighbours,
        hp_weight,
    ]
    *loaded, tail = call(
        load_kernel,
        pinned(*args),
        like(*args[:-1]) + [shape(out_rows, hp_weight.shape[1]), shape(ROWS, LANES)],
        in_specs=[hbm] * len(args),
        scratch_shapes=[
            pltpu.VMEM((channels, LANES), jnp.float32),
            pltpu.SemaphoreType.DMA((len(args) + 1,)),
        ],
    )
    swath, cell_query, enc_weight, key_weight, quality, sample_cell, *loaded = loaded
    tail_b = lax.ppermute(tail, axes, far(0))
    tail_again = call(copy_kernel, [tail], shape(*tail.shape), cost=100_000_000)
    tail_a = lax.ppermute(tail_again, axes, near)

    before, late_taps, ids, late, rest, rest_pack = call(
        prepare_kernel,
        [swath, enc_weight, key_weight, cell_query, quality, sample_cell, live],
        [
            shape(ROWS, 2 * channels),
            shape(2 * channels, 6 * LATE * channels, dtype=jnp.bfloat16),
            shape(ROWS, LANES, dtype=jnp.int32),
            shape(6, ROWS, LANES),
            shape(cells // 2 + ROWS, LANES),
            shape(side, LANES),
        ],
        cost=200_000_000,
        in_specs=[vmem] * 6 + [pl.BlockSpec(memory_space=pltpu.SMEM)],
        scratch_shapes=[pltpu.VMEM((cells, LANES), jnp.float32)] * 2,
    )
    stats, pack = call(
        pool_kernel,
        [
            late_taps,
            tail_a,
            tail_b,
            before,
            ids,
            late,
            rest,
            rest_pack,
        ],
        [shape(*rest.shape), shape(*rest_pack.shape)],
    )

    flip = 1
    while flip * 2 < sensors:
        other, other_pack = (lax.ppermute(v, axes, across(flip)) for v in (stats, pack))
        stats = call(merge_kernel, [stats, other], shape(*stats.shape))
        pack = call(bound(merge_pack_kernel), [pack, other_pack], shape(*pack.shape))
        flip *= 2

    other = lax.ppermute(stats, axes, across(flip))
    other_b = lax.ppermute(pack, axes, far(flip))
    pack_again = call(copy_kernel, [pack], shape(*pack.shape), cost=100_000_000)
    hpv, taps, code, pick = call(
        weights_kernel,
        loaded + [pack_again],
        [
            shape(stencil * out_rows, channels),
            shape((stencil - 1) * out_rows, 4 * channels, dtype=jnp.bfloat16),
            shape(*neighbours.shape, dtype=jnp.int32),
            shape((stencil - 1) * 2 * side, cells, dtype=jnp.bfloat16),
        ],
        cost=100_000_000,
    )
    own_b = lax.ppermute(pack_again, axes, far(0))
    mean_a = call(
        mean_kernel,
        [stats, other],
        shape(side // 2, LANES),
        scratch_shapes=[pltpu.VMEM((cells // 2, LANES), jnp.float32)],
    )
    halo_a = lax.ppermute(mean_a, axes, near)
    partial = call(own_kernel, [stats, other, hpv, code], shape(out_rows, cells), cost=200_000_000)
    return call(
        functools.partial(halo_kernel, channels, ranges - 1),
        [halo_a, own_b, other_b, partial, taps, pick],
        shape(out_rows, cells),
    )


def solution(mesh):
    in_specs = (
        P("sensor", None, "cell"),
        P("sensor", None, None),
        P(),
        P(),
        P(None, "cell"),
        P("sensor", "cell"),
        P("sensor", "cell"),
        P("sensor", "cell"),
        P(None, "cell"),
        P(),
    )
    out_specs = P("sensor", "cell")
    return jax.shard_map(
        on_device, mesh=mesh, in_specs=in_specs, out_specs=out_specs, check_vma=False
    )
```

```python
import functools
import math

import jax
import jax.numpy as jnp
from jax import lax
from jax.experimental import pallas as pl
from jax.experimental.pallas import tpu as pltpu
from jax.sharding import PartitionSpec as P

FLOOR = -1e30
LANES = 128
ROWS = 8
LATE = 2
EXACT = lax.Precision.HIGHEST
CLOSE = lax.Precision.HIGH
NN = ((1,), (0,))
NT = ((1,), (1,))


def dot(left, right, contract, precision=EXACT):
    return lax.dot_general(
        left,
        right,
        (contract, ((), ())),
        precision=precision,
        preferred_element_type=jnp.float32,
    )


def by_half(left, right, contract):
    half = left.shape[0] // 2
    return jnp.concatenate(
        [dot(rows, right, contract, None) for rows in (left[:half], left[half:])], axis=0
    )


def iota(shape, dim):
    return lax.broadcasted_iota(jnp.int32, shape, dim)


def gelu(x):
    return 0.5 * x * (1.0 + lax.erf(x * math.sqrt(0.5)))


def widened(value, lanes=LANES):
    gap = jnp.zeros((value.shape[0], lanes - value.shape[1]), value.dtype)
    return jnp.concatenate([value, gap], axis=1)


def with_peak(block, peak, channels):
    return jnp.where(iota(block.shape, 1) == channels + 1, peak, block)


def merged(first, second, channels):
    first_peak, second_peak = (v[:, channels + 1 : channels + 2] for v in (first, second))
    peak = jnp.maximum(first_peak, second_peak)
    both = first * jnp.exp(first_peak - peak) + second * jnp.exp(second_peak - peak)
    return both, peak


def twice(value):
    half = value[:, : LANES // 2]
    return jnp.concatenate([half, half], axis=1)


def shares_of(first, second, channels):
    (first_total, first_peak), (second_total, second_peak) = (
        [v[:, channels + i : channels + i + 1] for i in range(2)] for v in (first, second)
    )
    peak = jnp.maximum(first_peak, second_peak)
    first_factor, second_factor = jnp.exp(first_peak - peak), jnp.exp(second_peak - peak)
    total = first_total * first_factor + second_total * second_factor
    return first_factor / total, second_factor / total


def load_kernel(*refs):
    *refs, tail_ref, last_ref, sems = refs
    count = len(refs) // 2
    sources, targets = refs[:count], refs[count:]
    swath_ref = sources[0]
    copies = [(swath_ref.at[0, :, pl.ds(swath_ref.shape[2] - LANES, LANES)], last_ref)]
    hp_ref, own_hp_ref = sources[-1], targets[-1]
    out_rows = own_hp_ref.shape[0]
    start = pl.multiple_of(lax.axis_index("sensor") * out_rows, ROWS)
    copies += [(hp_ref.at[pl.ds(start, out_rows), :], own_hp_ref)]
    copies += list(zip(sources[:-1], targets[:-1]))
    copies = [pltpu.make_async_copy(*ends, sems.at[i]) for i, ends in enumerate(copies)]
    for copy in copies:
        copy.start()
    copies[0].wait()
    last = jnp.transpose(last_ref[...])[LANES - LATE :, :]
    gap = jnp.zeros(last.shape, jnp.float32)
    two = jnp.concatenate([last, jnp.concatenate([last[1:], gap[1:]], axis=0)], axis=1)
    tail_ref[...] = jnp.concatenate([two] + [jnp.zeros(two.shape, jnp.float32)] * 3, axis=0)
    for copy in copies[1:]:
        copy.wait()


def halves(value):
    high = value.astype(jnp.bfloat16)
    return high, (value - high.astype(jnp.float32)).astype(jnp.bfloat16)


def parts(value):
    high = value.astype(jnp.bfloat16)
    rest = value - high.astype(jnp.float32)
    middle = rest.astype(jnp.bfloat16)
    return high, middle, (rest - middle.astype(jnp.float32)).astype(jnp.bfloat16)


def exact(twofold, right):
    high, middle, low = parts(twofold)
    mixed = jnp.where(iota(high.shape, 1) < right.shape[0], high, low)
    right_high, right_middle, right_low = parts(right)
    return dot(
        jnp.concatenate([high, middle, mixed], axis=1),
        jnp.concatenate(
            [right_high, right_middle, right_high, right_middle, right_low, right_high], axis=0
        ),
        NN,
        None,
    )


def packed(block, channels):
    half = block.shape[0] // 2
    sums = jnp.concatenate([block[:half, :channels], block[half:, :channels]], axis=1)
    total, peak = (block[:, channels + i : channels + i + 1] for i in range(2))
    lane = iota((half, LANES), 1)
    columns = jnp.where(lane == 0, total[:half], jnp.where(lane == 1, total[half:], 0.0))
    columns = jnp.where(lane == 2, peak[:half], jnp.where(lane == 3, peak[half:], columns))
    return sums, jnp.transpose(columns)[:ROWS, :]


def prepare_kernel(
    swath_ref,
    enc_ref,
    key_ref,
    query_ref,
    quality_ref,
    cell_ref,
    live_ref,
    before_ref,
    taps_ref,
    ids_ref,
    late_ref,
    stats_ref,
    pack_ref,
    kq_ref,
    block_ref,
):
    sensor = lax.axis_index("sensor")
    odd = lax.rem(lax.axis_index("cell"), 2)
    channels, slots = swath_ref.shape[1:]
    cells = query_ref.shape[1]
    side, half = pack_ref.shape[0], cells // 2

    signal = swath_ref[0]
    one = jnp.concatenate([jnp.zeros((channels, 1), jnp.float32), signal[:, : slots - 1]], axis=1)
    two = jnp.concatenate([jnp.zeros((channels, 2), jnp.float32), signal[:, : slots - 2]], axis=1)
    stacked = jnp.concatenate([two, one, signal], axis=0)
    before = dot(enc_ref[0], stacked, NN)
    first = before[:, :LANES]
    before_ref[...] = jnp.transpose(jnp.concatenate([first, first], axis=0))[:ROWS, :]
    encoded = gelu(before)

    query = query_ref[...]
    key = jnp.concatenate([key_ref[...]] * 2, axis=1)
    key = jnp.transpose(jnp.concatenate([key, key], axis=0))
    key_query = jnp.transpose(exact(key, query) * (1.0 / math.sqrt(channels)))
    query = jnp.transpose(jnp.concatenate([query, jnp.zeros(query.shape, jnp.float32)], axis=0))
    kq_ref[...] = key_query
    own_score = jnp.sum(query * key_query, axis=1, keepdims=True)
    own_score = jnp.where(sensor == 0, own_score, -jnp.inf)

    score = exact(key_query, encoded)
    slot = iota((1, slots), 1)
    ids = jnp.where(slot < live_ref[0, 0], cell_ref[...], -1)
    late_ids = [ids[:, j : j + 1] for j in range(LATE)]
    ids = jnp.where(slot < LATE, -1, ids)
    score = jnp.where(iota((cells, slots), 0) == ids, score + quality_ref[...], -jnp.inf)
    peak = jnp.maximum(jnp.max(score, axis=1, keepdims=True), jnp.maximum(own_score, FLOOR))
    weights = jnp.exp(score - peak)
    place = iota((LANES - channels, slots), 0)
    tokens = jnp.concatenate([encoded, (place == 0).astype(jnp.float32)], axis=0)
    high, low = halves(jnp.transpose(tokens))
    weights_high, weights_low = halves(weights)
    both = jnp.concatenate([high, low], axis=1)
    wide = by_half(weights_high, both, NN)
    block = wide[:, :LANES] + wide[:, LANES:] + by_half(weights_low, high, NN)
    own = jnp.where(iota(query.shape, 1) == channels, 1.0, query)
    block = with_peak(block + own * jnp.exp(own_score - peak), peak, channels)
    block_ref[...] = block
    stats_ref[:half, :], stats_ref[half:, :] = packed(block, channels)
    left = block_ref[pl.ds(0, side, stride=side), :]
    right = block_ref[pl.ds(side - 1, side, stride=side), :]
    pack_ref[...] = jnp.where(odd == 1, right, left)
    gap = jnp.zeros((ROWS - LATE, LANES), jnp.float32)

    def listed(rows):
        return jnp.concatenate([jnp.broadcast_to(r, (1, LANES)) for r in rows] + [gap], axis=0)

    at = [pl.ds(cell_ref[0, j], 1) for j in range(LATE)]
    key_query = listed([kq_ref[a, :] for a in at])
    rest = listed([block_ref[a, :] for a in at])
    late_ref[0] = jnp.where(iota(key_query.shape, 1) < channels, key_query, 0.0)
    late_ref[1] = twice(rest)
    for i in range(2):
        late_ref[2 + i] = jnp.broadcast_to(rest[:, channels + i : channels + i + 1], rest.shape)
    late_ref[4] = listed([quality_ref[:, j : j + 1] for j in range(LATE)])
    same = jnp.where(late_ids[0] == late_ids[1], 0.0, -jnp.inf)
    late_ref[5] = listed([same] * LATE)
    ids_ref[...] = jnp.concatenate(
        [jnp.broadcast_to(i, (1, LANES)) for i in late_ids] + [gap.astype(jnp.int32)], axis=0
    )
    first = enc_ref[0, :, : LATE * channels]
    high, middle, low = parts(jnp.transpose(jnp.concatenate([first, first], axis=0)))
    taps_ref[...] = jnp.concatenate([high, high, middle, high, middle, low], axis=0)


def swapped(value):
    return jnp.concatenate([value[1:2], value[0:1], value[2:]], axis=0)


def pool_kernel(
    taps_ref,
    tail_a_ref,
    tail_b_ref,
    before_ref,
    ids_ref,
    late_ref,
    rest_ref,
    rest_pack_ref,
    stats_ref,
    pack_ref,
):
    cell = lax.axis_index("cell")
    odd = lax.rem(cell, 2)
    side, half = pack_ref.shape[0], stats_ref.shape[0] - ROWS
    channels = LANES // 2
    tail = jnp.where(odd == 1, tail_a_ref[...], tail_b_ref[...])
    tail = jnp.where(cell == 0, 0.0, tail)
    high, middle, low = parts(jnp.concatenate([tail, jnp.zeros(tail.shape, jnp.float32)], axis=0))
    tail = jnp.concatenate([high, middle, high, low, middle, high], axis=1)
    tokens = gelu(before_ref[...] + dot(tail, taps_ref[...], NN, None)[:ROWS, :])

    key_query, rest, rest_total, rest_peak, quality, same = (late_ref[i] for i in range(6))
    score = jnp.sum(tokens * key_query, axis=1, keepdims=True) + quality
    other = swapped(score) + same
    peak = jnp.maximum(rest_peak, jnp.maximum(score, other))
    rest_factor, weight, other_weight = (jnp.exp(v - peak) for v in (rest_peak, score, other))
    rows = rest * rest_factor + tokens * weight + swapped(tokens) * other_weight
    totals = rest_total * rest_factor + weight + other_weight

    sums, ends, pack = rest_ref[:half, :], rest_ref[half:, :], rest_pack_ref[...]
    of_sum = iota(sums.shape, 0) + jnp.where(iota(sums.shape, 1) < channels, 0, half)
    kind = iota(ends.shape, 0)
    of_end = iota(ends.shape, 1) + jnp.where(lax.rem(kind, 2) == 0, 0, half)
    of_end = jnp.where(kind < 4, of_end, 2 * half)
    of_pack = iota(pack.shape, 0) * side + jnp.where(odd == 1, side - 1, 0)
    lane = iota((1, LANES), 1)
    for j in range(LATE):
        at, row, total, top = (v[j : j + 1] for v in (ids_ref[...], rows, totals, peak))
        sums = jnp.where(of_sum == at, row, sums)
        ends = jnp.where(of_end == at, jnp.where(kind < 2, total, top), ends)
        row = jnp.where(lane < channels, row, jnp.where(lane == channels, total, top))
        pack = jnp.where(of_pack == at, row, pack)
    stats_ref[:half, :], stats_ref[half:, :] = sums, ends
    pack_ref[...] = pack


def shares(first, second):
    peak = jnp.maximum(first[2:4], second[2:4])
    first_factor = jnp.exp(first[2:4] - peak)
    second_factor = jnp.exp(second[2:4] - peak)
    total = first[0:2] * first_factor + second[0:2] * second_factor
    return first_factor, second_factor, total, peak


def turned(*rows):
    rows = jnp.concatenate(rows, axis=0)
    gap = jnp.zeros((LANES - rows.shape[0], rows.shape[1]), jnp.float32)
    return jnp.transpose(jnp.concatenate([rows, gap], axis=0))


def spread(columns, count):
    left = iota((columns.shape[0], LANES), 1) < LANES // 2
    return [
        jnp.where(left, columns[:, 2 * i : 2 * i + 1], columns[:, 2 * i + 1 : 2 * i + 2])
        for i in range(count)
    ]


def merge_pack_kernel(channels, own_ref, other_ref, out_ref):
    both, peak = merged(own_ref[...], other_ref[...], channels)
    out_ref[...] = with_peak(both, peak, channels)


def merge_kernel(own_ref, other_ref, out_ref):
    half = own_ref.shape[0] - ROWS
    first_factor, second_factor, total, peak = shares(own_ref[half:, :], other_ref[half:, :])
    first_factor, second_factor = spread(turned(first_factor, second_factor), 2)
    out_ref[:half, :] = own_ref[:half, :] * first_factor + other_ref[:half, :] * second_factor
    rest = jnp.zeros((ROWS - 4, total.shape[1]), jnp.float32)
    out_ref[half:, :] = jnp.concatenate([total, peak, rest], axis=0)


def copy_kernel(in_ref, out_ref):
    out_ref[...] = in_ref[...]


def weights_kernel(value_ref, near_ref, hp_ref, after_ref, hpv_ref, taps_ref, code_ref, pick_ref):
    del after_ref
    cell = lax.axis_index("cell")
    channels = value_ref.shape[0]
    cells = near_ref.shape[1]
    side = math.isqrt(cells)
    out_rows, own_hp = hp_ref.shape[0], hp_ref[...]
    value = value_ref[...]
    taps = [
        own_hp[:, k * channels : (k + 1) * channels] for k in range(hp_ref.shape[1] // channels)
    ]
    hpv = dot(jnp.concatenate(taps, axis=0), value, NN)
    hpv_ref[...] = hpv
    high, low = halves(hpv[out_rows:])
    gap = jnp.zeros(low.shape, jnp.float32).astype(jnp.bfloat16)
    taps_ref[...] = jnp.concatenate([high, high, low, gap], axis=1)

    shift = side.bit_length() - 1
    odd = lax.rem(cell, 2)
    offset = near_ref[...] - cell * cells
    after = cells + odd * side + lax.shift_right_arithmetic(offset - cells, shift)
    ahead = cells + (1 - odd) * side + lax.shift_right_arithmetic(offset + cells, shift)
    code_ref[...] = jnp.where(offset < 0, ahead, jnp.where(offset < cells, offset, after))
    halo = code_ref[...] - cells
    place = iota((4 * side, cells), 0)
    place = jnp.where(place < 2 * side, place, jnp.where(place < 3 * side, place - side, -1))
    for k in range(halo.shape[0]):
        here = (place == halo[k : k + 1, :]).astype(jnp.float32).astype(jnp.bfloat16)
        pick_ref[4 * side * k : 4 * side * (k + 1), :] = here


def mean_kernel(own_ref, other_ref, pack_ref, columns_ref):
    odd = lax.rem(lax.axis_index("cell"), 2)
    half = own_ref.shape[0] - ROWS
    count = pack_ref.shape[0]
    side = half // count
    first_factor, second_factor, total, _ = shares(own_ref[half:, :], other_ref[half:, :])
    columns_ref[...] = turned(first_factor / total, second_factor / total)

    def column(ref):
        left = ref[pl.ds(0, count, stride=side), :]
        return jnp.where(odd == 1, left, ref[pl.ds(side - 1, count, stride=side), :])

    first_share, second_share = spread(column(columns_ref), 2)
    pack_ref[...] = column(own_ref) * first_share + column(other_ref) * second_share


def own_kernel(own_ref, other_ref, hpv_ref, code_ref, out_ref):
    out_rows, cells = out_ref.shape
    half = own_ref.shape[0] - ROWS
    first_factor, second_factor, total, _ = shares(own_ref[half:, :], other_ref[half:, :])
    columns = turned(first_factor / total, second_factor / total)
    first_share, second_share = spread(columns, 2)
    mean = own_ref[:half, :] * first_share + other_ref[:half, :] * second_share
    hpv = hpv_ref[...]
    gap = jnp.zeros(hpv.shape, jnp.float32)
    mixed = [
        dot(jnp.concatenate(pair, axis=1), mean, NT, CLOSE) for pair in ((hpv, gap), (gap, hpv))
    ]
    lanes = lax.bitwise_and(code_ref[...], LANES - 1)
    places = lax.shift_right_logical(code_ref[...], LANES.bit_length() - 1)
    for i, start in enumerate(range(0, cells, LANES)):
        total = mixed[i][:out_rows]
        for k in range(code_ref.shape[0]):
            rows = slice((k + 1) * out_rows, (k + 2) * out_rows)
            lane, place = (
                jnp.broadcast_to(v[k : k + 1, start : start + LANES], total.shape)
                for v in (lanes, places)
            )
            taken = 0.0
            for source, values in enumerate(mixed):
                here = taken_lanes(values[rows], lane)
                taken = jnp.where(place == source, here, taken)
            total = total + taken
        out_ref[:, start : start + LANES] = total


def taken_lanes(values, lane):
    return jnp.take_along_axis(values, lane, axis=1, mode="promise_in_bounds")


def halo_kernel(
    channels, last, a_ref, own_b_ref, other_b_ref, partial_ref, taps_ref, pick_ref, out_ref
):
    out_rows = out_ref.shape[0]
    cell = lax.axis_index("cell")
    own_b, other_b = own_b_ref[...], other_b_ref[...]
    a = a_ref[...]
    a = [twice(a), twice(jnp.concatenate([a[:, channels:], a[:, :channels]], axis=1))]
    gap = jnp.zeros(own_b.shape, jnp.float32)
    halo = jnp.concatenate(a + [twice(own_b), twice(other_b), gap], axis=0)
    cells = halo.shape[0]
    turns = LANES // cells
    alone = (cell == 0) | (cell == last)
    share = [
        jnp.broadcast_to(jnp.where(alone, 0.0, v), own_b.shape)
        for v in shares_of(own_b, other_b, channels)
    ]
    share = jnp.concatenate([gap + 1.0] + share + [gap], axis=0)
    share = jnp.transpose(jnp.concatenate([share] * turns, axis=0))[:out_rows]
    left = iota(halo.shape, 1) < channels
    high = halo.astype(jnp.bfloat16).astype(jnp.float32)
    halo = jnp.concatenate(
        [jnp.where(left, high, halo - high), jnp.where(left, high, 0.0)], axis=1
    ).astype(jnp.bfloat16)
    edge = by_half(taps_ref[...], jnp.concatenate([halo] * turns, axis=0), NT)
    lane = iota((out_rows, LANES), 1)
    groups = []
    for start in range(0, edge.shape[0], turns * out_rows):
        group = edge[start : start + out_rows]
        for turn in range(1, turns):
            rows = edge[start + turn * out_rows : start + (turn + 1) * out_rows]
            group = jnp.where(lane >= turn * cells, rows, group)
        groups.append(group * share)
    high, low = halves(jnp.concatenate(groups, axis=1))
    pick = pick_ref[...]
    both = dot(jnp.concatenate([high, low], axis=0), pick, NN, None)
    out_ref[...] = partial_ref[...] + (both[:out_rows] + both[out_rows:])


def swaps(sensors, cells):
    def listed(partner):
        return [(s * cells + c, partner(s, c)) for s in range(sensors) for c in range(cells)]

    def far(flip):
        def partner(s, c):
            if c in (0, cells - 1):
                return (s ^ 1) * cells + c
            return (s ^ flip) * cells + ((c - 1) ^ 1) + 1

        return listed(partner)

    near = listed(lambda s, c: s * cells + (c ^ 1))

    def across(flip):
        return listed(lambda s, c: (s ^ flip) * cells + c)

    return near, far, across


def on_device(
    swath,
    enc_weight,
    key_weight,
    value_weight,
    cell_query,
    quality,
    sample_cell,
    live,
    neighbours,
    hp_weight,
):
    sensors, ranges = lax.axis_size("sensor"), lax.axis_size("cell")
    channels = swath.shape[1]
    cells = cell_query.shape[1]
    side = math.isqrt(cells)
    out_rows = channels // sensors
    stencil = hp_weight.shape[1] // channels
    vmem = pl.BlockSpec(memory_space=pltpu.VMEM)
    axes = ("sensor", "cell")
    near, far, across = swaps(sensors, ranges)

    def shape(*sizes, dtype=jnp.float32):
        return jax.ShapeDtypeStruct(sizes, dtype)

    def call(kernel, args, outs, cost=None, **more):
        single = not isinstance(outs, list)
        specs = dict(in_specs=[vmem] * len(args), out_specs=vmem if single else [vmem] * len(outs))
        specs.update(more)
        return pl.pallas_call(
            kernel,
            out_shape=outs,
            compiler_params=pltpu.CompilerParams(vmem_limit_bytes=8 * 1024 * 1024),
            cost_estimate=cost
            and pl.CostEstimate(flops=cost, bytes_accessed=cost // 100, transcendentals=0),
            **specs,
        )(*args)

    def bound(kernel):
        return lambda *refs: kernel(channels, *refs)

    hbm = pl.BlockSpec(memory_space=pltpu.HBM)

    def pinned(*args):
        return [pltpu.with_memory_space_constraint(a, pltpu.HBM) for a in args]

    def like(*args):
        return [shape(*a.shape, dtype=a.dtype) for a in args]

    args = [
        swath,
        cell_query,
        enc_weight,
        key_weight,
        quality,
        sample_cell,
        value_weight,
        neighbours,
        hp_weight,
    ]
    *loaded, tail = call(
        load_kernel,
        pinned(*args),
        like(*args[:-1]) + [shape(out_rows, hp_weight.shape[1]), shape(ROWS, LANES)],
        in_specs=[hbm] * len(args),
        scratch_shapes=[
            pltpu.VMEM((channels, LANES), jnp.float32),
            pltpu.SemaphoreType.DMA((len(args) + 1,)),
        ],
    )
    swath, cell_query, enc_weight, key_weight, quality, sample_cell, *loaded = loaded
    tail_b = lax.ppermute(tail, axes, far(0))
    tail_again = call(copy_kernel, [tail], shape(*tail.shape), cost=100_000_000)
    tail_a = lax.ppermute(tail_again, axes, near)

    before, late_taps, ids, late, rest, rest_pack = call(
        prepare_kernel,
        [swath, enc_weight, key_weight, cell_query, quality, sample_cell, live],
        [
            shape(ROWS, 2 * channels),
            shape(6 * LATE * channels, 2 * channels, dtype=jnp.bfloat16),
            shape(ROWS, LANES, dtype=jnp.int32),
            shape(6, ROWS, LANES),
            shape(cells // 2 + ROWS, LANES),
            shape(side, LANES),
        ],
        cost=200_000_000,
        in_specs=[vmem] * 6 + [pl.BlockSpec(memory_space=pltpu.SMEM)],
        scratch_shapes=[pltpu.VMEM((cells, LANES), jnp.float32)] * 2,
    )
    stats, pack = call(
        pool_kernel,
        [
            late_taps,
            tail_a,
            tail_b,
            before,
            ids,
            late,
            rest,
            rest_pack,
        ],
        [shape(*rest.shape), shape(*rest_pack.shape)],
    )

    flip = 1
    while flip * 2 < sensors:
        other, other_pack = (lax.ppermute(v, axes, across(flip)) for v in (stats, pack))
        stats = call(merge_kernel, [stats, other], shape(*stats.shape))
        pack = call(bound(merge_pack_kernel), [pack, other_pack], shape(*pack.shape))
        flip *= 2

    other = lax.ppermute(stats, axes, across(flip))
    other_b = lax.ppermute(pack, axes, far(flip))
    pack_again = call(copy_kernel, [pack], shape(*pack.shape), cost=100_000_000)
    hpv, taps, code, pick = call(
        weights_kernel,
        loaded + [pack_again],
        [
            shape(stencil * out_rows, channels),
            shape((stencil - 1) * out_rows, 4 * channels, dtype=jnp.bfloat16),
            shape(*neighbours.shape, dtype=jnp.int32),
            shape((stencil - 1) * 4 * side, cells, dtype=jnp.bfloat16),
        ],
        cost=100_000_000,
    )
    own_b = lax.ppermute(pack_again, axes, far(0))
    mean_a = call(
        mean_kernel,
        [stats, other],
        shape(side // 2, LANES),
        scratch_shapes=[pltpu.VMEM((cells // 2, LANES), jnp.float32)],
    )
    halo_a = lax.ppermute(mean_a, axes, near)
    partial = call(own_kernel, [stats, other, hpv, code], shape(out_rows, cells), cost=200_000_000)
    return call(
        functools.partial(halo_kernel, channels, ranges - 1),
        [halo_a, own_b, other_b, partial, taps, pick],
        shape(out_rows, cells),
    )


def solution(mesh):
    in_specs = (
        P("sensor", None, "cell"),
        P("sensor", None, None),
        P(),
        P(),
        P(None, "cell"),
        P("sensor", "cell"),
        P("sensor", "cell"),
        P("sensor", "cell"),
        P(None, "cell"),
        P(),
    )
    out_specs = P("sensor", "cell")
    return jax.shard_map(
        on_device, mesh=mesh, in_specs=in_specs, out_specs=out_specs, check_vma=False
    )
```

```python
import functools
import math

import jax
import jax.numpy as jnp
from jax import lax
from jax.experimental import pallas as pl
from jax.experimental.pallas import tpu as pltpu
from jax.sharding import PartitionSpec as P

FLOOR = -1e30
LANES = 128
ROWS = 8
LATE = 2
EXACT = lax.Precision.HIGHEST
CLOSE = lax.Precision.HIGH
NN = ((1,), (0,))
NT = ((1,), (1,))


def dot(left, right, contract, precision=EXACT):
    return lax.dot_general(
        left,
        right,
        (contract, ((), ())),
        precision=precision,
        preferred_element_type=jnp.float32,
    )


def by_half(left, right, contract):
    half = left.shape[0] // 2
    return jnp.concatenate(
        [dot(rows, right, contract, None) for rows in (left[:half], left[half:])], axis=0
    )


def iota(shape, dim):
    return lax.broadcasted_iota(jnp.int32, shape, dim)


def gelu(x):
    return 0.5 * x * (1.0 + lax.erf(x * math.sqrt(0.5)))


def widened(value, lanes=LANES):
    gap = jnp.zeros((value.shape[0], lanes - value.shape[1]), value.dtype)
    return jnp.concatenate([value, gap], axis=1)


def with_peak(block, peak, channels):
    return jnp.where(iota(block.shape, 1) == channels + 1, peak, block)


def merged(first, second, channels):
    first_peak, second_peak = (v[:, channels + 1 : channels + 2] for v in (first, second))
    peak = jnp.maximum(first_peak, second_peak)
    both = first * jnp.exp(first_peak - peak) + second * jnp.exp(second_peak - peak)
    return both, peak


def twice(value):
    half = value[:, : LANES // 2]
    return jnp.concatenate([half, half], axis=1)


def shares_of(first, second, channels):
    (first_total, first_peak), (second_total, second_peak) = (
        [v[:, channels + i : channels + i + 1] for i in range(2)] for v in (first, second)
    )
    peak = jnp.maximum(first_peak, second_peak)
    first_factor, second_factor = jnp.exp(first_peak - peak), jnp.exp(second_peak - peak)
    total = first_total * first_factor + second_total * second_factor
    return first_factor / total, second_factor / total


def load_kernel(*refs):
    *refs, tail_ref, last_ref, sems = refs
    count = len(refs) // 2
    sources, targets = refs[:count], refs[count:]
    swath_ref = sources[0]
    copies = [(swath_ref.at[0, :, pl.ds(swath_ref.shape[2] - LANES, LANES)], last_ref)]
    hp_ref, own_hp_ref = sources[-1], targets[-1]
    out_rows = own_hp_ref.shape[0]
    start = pl.multiple_of(lax.axis_index("sensor") * out_rows, ROWS)
    copies += [(hp_ref.at[pl.ds(start, out_rows), :], own_hp_ref)]
    copies += list(zip(sources[:-1], targets[:-1]))
    copies = [pltpu.make_async_copy(*ends, sems.at[i]) for i, ends in enumerate(copies)]
    for copy in copies:
        copy.start()
    copies[0].wait()
    last = jnp.transpose(last_ref[...])[LANES - LATE :, :]
    gap = jnp.zeros(last.shape, jnp.float32)
    two = jnp.concatenate([last, jnp.concatenate([last[1:], gap[1:]], axis=0)], axis=1)
    tail_ref[...] = jnp.concatenate([two] + [jnp.zeros(two.shape, jnp.float32)] * 3, axis=0)
    for copy in copies[1:]:
        copy.wait()


def halves(value):
    high = value.astype(jnp.bfloat16)
    return high, (value - high.astype(jnp.float32)).astype(jnp.bfloat16)


def parts(value):
    high = value.astype(jnp.bfloat16)
    rest = value - high.astype(jnp.float32)
    middle = rest.astype(jnp.bfloat16)
    return high, middle, (rest - middle.astype(jnp.float32)).astype(jnp.bfloat16)


def exact(twofold, right):
    high, middle, low = parts(twofold)
    mixed = jnp.where(iota(high.shape, 1) < right.shape[0], high, low)
    right_high, right_middle, right_low = parts(right)
    return dot(
        jnp.concatenate([high, middle, mixed], axis=1),
        jnp.concatenate(
            [right_high, right_middle, right_high, right_middle, right_low, right_high], axis=0
        ),
        NN,
        None,
    )


def packed(block, channels):
    half = block.shape[0] // 2
    sums = jnp.concatenate([block[:half, :channels], block[half:, :channels]], axis=1)
    total, peak = (block[:, channels + i : channels + i + 1] for i in range(2))
    lane = iota((half, LANES), 1)
    columns = jnp.where(lane == 0, total[:half], jnp.where(lane == 1, total[half:], 0.0))
    columns = jnp.where(lane == 2, peak[:half], jnp.where(lane == 3, peak[half:], columns))
    return sums, jnp.transpose(columns)[:ROWS, :]


def prepare_kernel(
    swath_ref,
    enc_ref,
    key_ref,
    query_ref,
    quality_ref,
    cell_ref,
    live_ref,
    before_ref,
    taps_ref,
    ids_ref,
    late_ref,
    stats_ref,
    pack_ref,
    kq_ref,
    block_ref,
):
    sensor = lax.axis_index("sensor")
    odd = lax.rem(lax.axis_index("cell"), 2)
    channels, slots = swath_ref.shape[1:]
    cells = query_ref.shape[1]
    side, half = pack_ref.shape[0], cells // 2

    signal = swath_ref[0]
    one = jnp.concatenate([jnp.zeros((channels, 1), jnp.float32), signal[:, : slots - 1]], axis=1)
    two = jnp.concatenate([jnp.zeros((channels, 2), jnp.float32), signal[:, : slots - 2]], axis=1)
    stacked = jnp.concatenate([two, one, signal], axis=0)
    before = dot(enc_ref[0], stacked, NN)
    first = before[:, :LANES]
    before_ref[...] = jnp.transpose(jnp.concatenate([first, first], axis=0))[:ROWS, :]
    encoded = gelu(before)

    query = query_ref[...]
    key = jnp.concatenate([key_ref[...]] * 2, axis=1)
    key = jnp.transpose(jnp.concatenate([key, key], axis=0))
    key_query = jnp.transpose(exact(key, query) * (1.0 / math.sqrt(channels)))
    query = jnp.transpose(jnp.concatenate([query, jnp.zeros(query.shape, jnp.float32)], axis=0))
    kq_ref[...] = key_query
    own_score = jnp.sum(query * key_query, axis=1, keepdims=True)
    own_score = jnp.where(sensor == 0, own_score, -jnp.inf)

    score = exact(key_query, encoded)
    slot = iota((1, slots), 1)
    ids = jnp.where(slot < live_ref[0, 0], cell_ref[...], -1)
    late_ids = [ids[:, j : j + 1] for j in range(LATE)]
    ids = jnp.where(slot < LATE, -1, ids)
    score = jnp.where(iota((cells, slots), 0) == ids, score + quality_ref[...], -jnp.inf)
    peak = jnp.maximum(jnp.max(score, axis=1, keepdims=True), jnp.maximum(own_score, FLOOR))
    weights = jnp.exp(score - peak)
    place = iota((LANES - channels, slots), 0)
    tokens = jnp.concatenate([encoded, (place == 0).astype(jnp.float32)], axis=0)
    high, low = halves(jnp.transpose(tokens))
    weights_high, weights_low = halves(weights)
    both = jnp.concatenate([high, low], axis=1)
    wide = by_half(weights_high, both, NN)
    block = wide[:, :LANES] + wide[:, LANES:] + by_half(weights_low, high, NN)
    own = jnp.where(iota(query.shape, 1) == channels, 1.0, query)
    block = with_peak(block + own * jnp.exp(own_score - peak), peak, channels)
    block_ref[...] = block
    stats_ref[:half, :], stats_ref[half:, :] = packed(block, channels)
    left = block_ref[pl.ds(0, side, stride=side), :]
    right = block_ref[pl.ds(side - 1, side, stride=side), :]
    pack_ref[...] = jnp.where(odd == 1, right, left)
    gap = jnp.zeros((ROWS - LATE, LANES), jnp.float32)

    def listed(rows):
        return jnp.concatenate([jnp.broadcast_to(r, (1, LANES)) for r in rows] + [gap], axis=0)

    at = [pl.ds(cell_ref[0, j], 1) for j in range(LATE)]
    key_query = listed([kq_ref[a, :] for a in at])
    rest = listed([block_ref[a, :] for a in at])
    late_ref[0] = jnp.where(iota(key_query.shape, 1) < channels, key_query, 0.0)
    late_ref[1] = twice(rest)
    for i in range(2):
        late_ref[2 + i] = jnp.broadcast_to(rest[:, channels + i : channels + i + 1], rest.shape)
    late_ref[4] = listed([quality_ref[:, j : j + 1] for j in range(LATE)])
    same = jnp.where(late_ids[0] == late_ids[1], 0.0, -jnp.inf)
    late_ref[5] = listed([same] * LATE)
    ids_ref[...] = jnp.concatenate(
        [jnp.broadcast_to(i, (1, LANES)) for i in late_ids] + [gap.astype(jnp.int32)], axis=0
    )
    first = enc_ref[0, :, : LATE * channels]
    high, middle, low = parts(jnp.transpose(jnp.concatenate([first, first], axis=0)))
    taps_ref[...] = jnp.concatenate([high, high, middle, high, middle, low], axis=0)


def swapped(value):
    return jnp.concatenate([value[1:2], value[0:1], value[2:]], axis=0)


def pool_kernel(
    taps_ref,
    tail_a_ref,
    tail_b_ref,
    before_ref,
    ids_ref,
    late_ref,
    rest_ref,
    rest_pack_ref,
    stats_ref,
    pack_ref,
):
    cell = lax.axis_index("cell")
    odd = lax.rem(cell, 2)
    side, half = pack_ref.shape[0], stats_ref.shape[0] - ROWS
    channels = LANES // 2
    tail = jnp.where(odd == 1, tail_a_ref[...], tail_b_ref[...])
    tail = jnp.where(cell == 0, 0.0, tail)
    high, middle, low = parts(jnp.concatenate([tail, jnp.zeros(tail.shape, jnp.float32)], axis=0))
    tail = jnp.concatenate([high, middle, high, low, middle, high], axis=1)
    third = tail.shape[1] // 3
    late = [
        dot(tail[:, at : at + third], taps_ref[at : at + third, :], NN, None)[:ROWS, :]
        for at in range(0, 3 * third, third)
    ]
    tokens = gelu(before_ref[...] + (late[0] + (late[1] + late[2])))

    key_query, rest, rest_total, rest_peak, quality, same = (late_ref[i] for i in range(6))
    score = jnp.sum(tokens * key_query, axis=1, keepdims=True) + quality
    other = swapped(score) + same
    peak = jnp.maximum(rest_peak, jnp.maximum(score, other))
    rest_factor, weight, other_weight = (jnp.exp(v - peak) for v in (rest_peak, score, other))
    rows = rest * rest_factor + tokens * weight + swapped(tokens) * other_weight
    totals = rest_total * rest_factor + weight + other_weight

    sums, ends, pack = rest_ref[:half, :], rest_ref[half:, :], rest_pack_ref[...]
    of_sum = iota(sums.shape, 0) + jnp.where(iota(sums.shape, 1) < channels, 0, half)
    kind = iota(ends.shape, 0)
    of_end = iota(ends.shape, 1) + jnp.where(lax.rem(kind, 2) == 0, 0, half)
    of_end = jnp.where(kind < 4, of_end, 2 * half)
    of_pack = iota(pack.shape, 0) * side + jnp.where(odd == 1, side - 1, 0)
    lane = iota((1, LANES), 1)
    for j in range(LATE):
        at, row, total, top = (v[j : j + 1] for v in (ids_ref[...], rows, totals, peak))
        sums = jnp.where(of_sum == at, row, sums)
        ends = jnp.where(of_end == at, jnp.where(kind < 2, total, top), ends)
        row = jnp.where(lane < channels, row, jnp.where(lane == channels, total, top))
        pack = jnp.where(of_pack == at, row, pack)
    stats_ref[:half, :], stats_ref[half:, :] = sums, ends
    pack_ref[...] = pack


def shares(first, second):
    peak = jnp.maximum(first[2:4], second[2:4])
    first_factor = jnp.exp(first[2:4] - peak)
    second_factor = jnp.exp(second[2:4] - peak)
    total = first[0:2] * first_factor + second[0:2] * second_factor
    return first_factor, second_factor, total, peak


def turned(*rows):
    rows = jnp.concatenate(rows, axis=0)
    gap = jnp.zeros((LANES - rows.shape[0], rows.shape[1]), jnp.float32)
    return jnp.transpose(jnp.concatenate([rows, gap], axis=0))


def spread(columns, count):
    left = iota((columns.shape[0], LANES), 1) < LANES // 2
    return [
        jnp.where(left, columns[:, 2 * i : 2 * i + 1], columns[:, 2 * i + 1 : 2 * i + 2])
        for i in range(count)
    ]


def merge_pack_kernel(channels, own_ref, other_ref, out_ref):
    both, peak = merged(own_ref[...], other_ref[...], channels)
    out_ref[...] = with_peak(both, peak, channels)


def merge_kernel(own_ref, other_ref, out_ref):
    half = own_ref.shape[0] - ROWS
    first_factor, second_factor, total, peak = shares(own_ref[half:, :], other_ref[half:, :])
    first_factor, second_factor = spread(turned(first_factor, second_factor), 2)
    out_ref[:half, :] = own_ref[:half, :] * first_factor + other_ref[:half, :] * second_factor
    rest = jnp.zeros((ROWS - 4, total.shape[1]), jnp.float32)
    out_ref[half:, :] = jnp.concatenate([total, peak, rest], axis=0)


def copy_kernel(in_ref, out_ref):
    out_ref[...] = in_ref[...]


def weights_kernel(value_ref, near_ref, hp_ref, after_ref, hpv_ref, taps_ref, code_ref, pick_ref):
    del after_ref
    cell = lax.axis_index("cell")
    channels = value_ref.shape[0]
    cells = near_ref.shape[1]
    side = math.isqrt(cells)
    out_rows, own_hp = hp_ref.shape[0], hp_ref[...]
    value = value_ref[...]
    taps = [
        own_hp[:, k * channels : (k + 1) * channels] for k in range(hp_ref.shape[1] // channels)
    ]
    hpv = dot(jnp.concatenate(taps, axis=0), value, NN)
    hpv_ref[...] = hpv
    high, low = halves(hpv[out_rows:])
    gap = jnp.zeros(low.shape, jnp.float32).astype(jnp.bfloat16)
    taps_ref[...] = jnp.concatenate([high, high, low, gap], axis=1)

    shift = side.bit_length() - 1
    odd = lax.rem(cell, 2)
    offset = near_ref[...] - cell * cells
    after = cells + odd * side + lax.shift_right_arithmetic(offset - cells, shift)
    ahead = cells + (1 - odd) * side + lax.shift_right_arithmetic(offset + cells, shift)
    code_ref[...] = jnp.where(offset < 0, ahead, jnp.where(offset < cells, offset, after))
    halo = code_ref[...] - cells
    place = iota((4 * side, cells), 0)
    place = jnp.where(place < 2 * side, place, jnp.where(place < 3 * side, place - side, -1))
    for k in range(halo.shape[0]):
        here = (place == halo[k : k + 1, :]).astype(jnp.float32).astype(jnp.bfloat16)
        pick_ref[4 * side * k : 4 * side * (k + 1), :] = here


def mean_kernel(own_ref, other_ref, pack_ref, columns_ref):
    odd = lax.rem(lax.axis_index("cell"), 2)
    half = own_ref.shape[0] - ROWS
    count = pack_ref.shape[0]
    side = half // count
    first_factor, second_factor, total, _ = shares(own_ref[half:, :], other_ref[half:, :])
    columns_ref[...] = turned(first_factor / total, second_factor / total)

    def column(ref):
        left = ref[pl.ds(0, count, stride=side), :]
        return jnp.where(odd == 1, left, ref[pl.ds(side - 1, count, stride=side), :])

    first_share, second_share = spread(column(columns_ref), 2)
    pack_ref[...] = column(own_ref) * first_share + column(other_ref) * second_share


def own_kernel(own_ref, other_ref, hpv_ref, code_ref, out_ref):
    out_rows, cells = out_ref.shape
    half = own_ref.shape[0] - ROWS
    first_factor, second_factor, total, _ = shares(own_ref[half:, :], other_ref[half:, :])
    columns = turned(first_factor / total, second_factor / total)
    first_share, second_share = spread(columns, 2)
    mean = own_ref[:half, :] * first_share + other_ref[:half, :] * second_share
    hpv = hpv_ref[...]
    gap = jnp.zeros(hpv.shape, jnp.float32)
    mixed = [
        dot(jnp.concatenate(pair, axis=1), mean, NT, CLOSE) for pair in ((hpv, gap), (gap, hpv))
    ]
    lanes = lax.bitwise_and(code_ref[...], LANES - 1)
    places = lax.shift_right_logical(code_ref[...], LANES.bit_length() - 1)
    for i, start in enumerate(range(0, cells, LANES)):
        total = mixed[i][:out_rows]
        for k in range(code_ref.shape[0]):
            rows = slice((k + 1) * out_rows, (k + 2) * out_rows)
            lane, place = (
                jnp.broadcast_to(v[k : k + 1, start : start + LANES], total.shape)
                for v in (lanes, places)
            )
            taken = 0.0
            for source, values in enumerate(mixed):
                here = taken_lanes(values[rows], lane)
                taken = jnp.where(place == source, here, taken)
            total = total + taken
        out_ref[:, start : start + LANES] = total


def taken_lanes(values, lane):
    return jnp.take_along_axis(values, lane, axis=1, mode="promise_in_bounds")


def halo_kernel(
    channels, last, a_ref, own_b_ref, other_b_ref, partial_ref, taps_ref, pick_ref, out_ref
):
    out_rows = out_ref.shape[0]
    cell = lax.axis_index("cell")
    own_b, other_b = own_b_ref[...], other_b_ref[...]
    a = a_ref[...]
    a = [twice(a), twice(jnp.concatenate([a[:, channels:], a[:, :channels]], axis=1))]
    gap = jnp.zeros(own_b.shape, jnp.float32)
    halo = jnp.concatenate(a + [twice(own_b), twice(other_b), gap], axis=0)
    cells = halo.shape[0]
    turns = LANES // cells
    alone = (cell == 0) | (cell == last)
    share = [
        jnp.broadcast_to(jnp.where(alone, 0.0, v), own_b.shape)
        for v in shares_of(own_b, other_b, channels)
    ]
    share = jnp.concatenate([gap + 1.0] + share + [gap], axis=0)
    share = jnp.transpose(jnp.concatenate([share] * turns, axis=0))[:out_rows]
    left = iota(halo.shape, 1) < channels
    high = halo.astype(jnp.bfloat16).astype(jnp.float32)
    halo = jnp.concatenate(
        [jnp.where(left, high, halo - high), high], axis=1
    ).astype(jnp.bfloat16)
    edge = by_half(taps_ref[...], jnp.concatenate([halo] * turns, axis=0), NT)
    lane = iota((out_rows, LANES), 1)
    groups = []
    for start in range(0, edge.shape[0], turns * out_rows):
        group = edge[start : start + out_rows]
        for turn in range(1, turns):
            rows = edge[start + turn * out_rows : start + (turn + 1) * out_rows]
            group = jnp.where(lane >= turn * cells, rows, group)
        groups.append(group * share)
    high, low = halves(jnp.concatenate(groups, axis=1))
    pick = pick_ref[...]
    both = dot(jnp.concatenate([high, low], axis=0), pick, NN, None)
    out_ref[...] = partial_ref[...] + (both[:out_rows] + both[out_rows:])


def swaps(sensors, cells):
    def listed(partner):
        return [(s * cells + c, partner(s, c)) for s in range(sensors) for c in range(cells)]

    def far(flip):
        def partner(s, c):
            if c in (0, cells - 1):
                return (s ^ 1) * cells + c
            return (s ^ flip) * cells + ((c - 1) ^ 1) + 1

        return listed(partner)

    near = listed(lambda s, c: s * cells + (c ^ 1))

    def across(flip):
        return listed(lambda s, c: (s ^ flip) * cells + c)

    return near, far, across


def on_device(
    swath,
    enc_weight,
    key_weight,
    value_weight,
    cell_query,
    quality,
    sample_cell,
    live,
    neighbours,
    hp_weight,
):
    sensors, ranges = lax.axis_size("sensor"), lax.axis_size("cell")
    channels = swath.shape[1]
    cells = cell_query.shape[1]
    side = math.isqrt(cells)
    out_rows = channels // sensors
    stencil = hp_weight.shape[1] // channels
    vmem = pl.BlockSpec(memory_space=pltpu.VMEM)
    axes = ("sensor", "cell")
    near, far, across = swaps(sensors, ranges)

    def shape(*sizes, dtype=jnp.float32):
        return jax.ShapeDtypeStruct(sizes, dtype)

    def call(kernel, args, outs, cost=None, **more):
        single = not isinstance(outs, list)
        specs = dict(in_specs=[vmem] * len(args), out_specs=vmem if single else [vmem] * len(outs))
        specs.update(more)
        return pl.pallas_call(
            kernel,
            out_shape=outs,
            compiler_params=pltpu.CompilerParams(vmem_limit_bytes=8 * 1024 * 1024),
            cost_estimate=cost
            and pl.CostEstimate(flops=cost, bytes_accessed=cost // 100, transcendentals=0),
            **specs,
        )(*args)

    def bound(kernel):
        return lambda *refs: kernel(channels, *refs)

    hbm = pl.BlockSpec(memory_space=pltpu.HBM)

    def pinned(*args):
        return [pltpu.with_memory_space_constraint(a, pltpu.HBM) for a in args]

    def like(*args):
        return [shape(*a.shape, dtype=a.dtype) for a in args]

    args = [
        swath,
        cell_query,
        enc_weight,
        key_weight,
        quality,
        sample_cell,
        value_weight,
        neighbours,
        hp_weight,
    ]
    *loaded, tail = call(
        load_kernel,
        pinned(*args),
        like(*args[:-1]) + [shape(out_rows, hp_weight.shape[1]), shape(ROWS, LANES)],
        in_specs=[hbm] * len(args),
        scratch_shapes=[
            pltpu.VMEM((channels, LANES), jnp.float32),
            pltpu.SemaphoreType.DMA((len(args) + 1,)),
        ],
    )
    swath, cell_query, enc_weight, key_weight, quality, sample_cell, *loaded = loaded
    tail_b = lax.ppermute(tail, axes, far(0))
    tail_again = call(copy_kernel, [tail], shape(*tail.shape), cost=100_000_000)
    tail_a = lax.ppermute(tail_again, axes, near)

    before, late_taps, ids, late, rest, rest_pack = call(
        prepare_kernel,
        [swath, enc_weight, key_weight, cell_query, quality, sample_cell, live],
        [
            shape(ROWS, 2 * channels),
            shape(6 * LATE * channels, 2 * channels, dtype=jnp.bfloat16),
            shape(ROWS, LANES, dtype=jnp.int32),
            shape(6, ROWS, LANES),
            shape(cells // 2 + ROWS, LANES),
            shape(side, LANES),
        ],
        cost=200_000_000,
        in_specs=[vmem] * 6 + [pl.BlockSpec(memory_space=pltpu.SMEM)],
        scratch_shapes=[pltpu.VMEM((cells, LANES), jnp.float32)] * 2,
    )
    stats, pack = call(
        pool_kernel,
        [
            late_taps,
            tail_a,
            tail_b,
            before,
            ids,
            late,
            rest,
            rest_pack,
        ],
        [shape(*rest.shape), shape(*rest_pack.shape)],
    )

    flip = 1
    while flip * 2 < sensors:
        other, other_pack = (lax.ppermute(v, axes, across(flip)) for v in (stats, pack))
        stats = call(merge_kernel, [stats, other], shape(*stats.shape))
        pack = call(bound(merge_pack_kernel), [pack, other_pack], shape(*pack.shape))
        flip *= 2

    other = lax.ppermute(stats, axes, across(flip))
    other_b = lax.ppermute(pack, axes, far(flip))
    pack_again = call(copy_kernel, [pack], shape(*pack.shape), cost=100_000_000)
    hpv, taps, code, pick = call(
        weights_kernel,
        loaded + [pack_again],
        [
            shape(stencil * out_rows, channels),
            shape((stencil - 1) * out_rows, 4 * channels, dtype=jnp.bfloat16),
            shape(*neighbours.shape, dtype=jnp.int32),
            shape((stencil - 1) * 4 * side, cells, dtype=jnp.bfloat16),
        ],
        cost=100_000_000,
    )
    own_b = lax.ppermute(pack_again, axes, far(0))
    mean_a = call(
        mean_kernel,
        [stats, other],
        shape(side // 2, LANES),
        scratch_shapes=[pltpu.VMEM((cells // 2, LANES), jnp.float32)],
    )
    halo_a = lax.ppermute(mean_a, axes, near)
    partial = call(own_kernel, [stats, other, hpv, code], shape(out_rows, cells), cost=200_000_000)
    return call(
        functools.partial(halo_kernel, channels, ranges - 1),
        [halo_a, own_b, other_b, partial, taps, pick],
        shape(out_rows, cells),
    )


def solution(mesh):
    in_specs = (
        P("sensor", None, "cell"),
        P("sensor", None, None),
        P(),
        P(),
        P(None, "cell"),
        P("sensor", "cell"),
        P("sensor", "cell"),
        P("sensor", "cell"),
        P(None, "cell"),
        P(),
    )
    out_specs = P("sensor", "cell")
    return jax.shard_map(
        on_device, mesh=mesh, in_specs=in_specs, out_specs=out_specs, check_vma=False
    )
```

```python
import functools
import math

import jax
import jax.numpy as jnp
from jax import lax
from jax.experimental import pallas as pl
from jax.experimental.pallas import tpu as pltpu
from jax.sharding import PartitionSpec as P

FLOOR = -1e30
LANES = 128
ROWS = 8
LATE = 2
EXACT = lax.Precision.HIGHEST
CLOSE = lax.Precision.HIGH
NN = ((1,), (0,))
NT = ((1,), (1,))


def dot(left, right, contract, precision=EXACT):
    return lax.dot_general(
        left,
        right,
        (contract, ((), ())),
        precision=precision,
        preferred_element_type=jnp.float32,
    )


def by_half(left, right, contract):
    half = left.shape[0] // 2
    return jnp.concatenate(
        [dot(rows, right, contract, None) for rows in (left[:half], left[half:])], axis=0
    )


def iota(shape, dim):
    return lax.broadcasted_iota(jnp.int32, shape, dim)


def gelu(x):
    return 0.5 * x * (1.0 + lax.erf(x * math.sqrt(0.5)))


def widened(value, lanes=LANES):
    gap = jnp.zeros((value.shape[0], lanes - value.shape[1]), value.dtype)
    return jnp.concatenate([value, gap], axis=1)


def with_peak(block, peak, channels):
    return jnp.where(iota(block.shape, 1) == channels + 1, peak, block)


def merged(first, second, channels):
    first_peak, second_peak = (v[:, channels + 1 : channels + 2] for v in (first, second))
    peak = jnp.maximum(first_peak, second_peak)
    both = first * jnp.exp(first_peak - peak) + second * jnp.exp(second_peak - peak)
    return both, peak


def twice(value):
    half = value[:, : LANES // 2]
    return jnp.concatenate([half, half], axis=1)


def shares_of(first, second, channels):
    (first_total, first_peak), (second_total, second_peak) = (
        [v[:, channels + i : channels + i + 1] for i in range(2)] for v in (first, second)
    )
    peak = jnp.maximum(first_peak, second_peak)
    first_factor, second_factor = jnp.exp(first_peak - peak), jnp.exp(second_peak - peak)
    total = first_total * first_factor + second_total * second_factor
    return first_factor / total, second_factor / total


def load_kernel(*refs):
    *refs, tail_ref, last_ref, sems = refs
    count = len(refs) // 2
    sources, targets = refs[:count], refs[count:]
    swath_ref = sources[0]
    copies = [(swath_ref.at[0, :, pl.ds(swath_ref.shape[2] - LANES, LANES)], last_ref)]
    hp_ref, own_hp_ref = sources[-1], targets[-1]
    out_rows = own_hp_ref.shape[0]
    start = pl.multiple_of(lax.axis_index("sensor") * out_rows, ROWS)
    copies += [(sources[0], targets[0]), (hp_ref.at[pl.ds(start, out_rows), :], own_hp_ref)]
    copies += list(zip(sources[1:-1], targets[1:-1]))
    copies = [pltpu.make_async_copy(*ends, sems.at[i]) for i, ends in enumerate(copies)]
    for copy in copies:
        copy.start()
    copies[0].wait()
    last = jnp.transpose(last_ref[...])[LANES - LATE :, :]
    gap = jnp.zeros(last.shape, jnp.float32)
    two = jnp.concatenate([last, jnp.concatenate([last[1:], gap[1:]], axis=0)], axis=1)
    tail_ref[...] = jnp.concatenate([two] + [jnp.zeros(two.shape, jnp.float32)] * 3, axis=0)
    for copy in copies[1:]:
        copy.wait()


def halves(value):
    high = value.astype(jnp.bfloat16)
    return high, (value - high.astype(jnp.float32)).astype(jnp.bfloat16)


def parts(value):
    high = value.astype(jnp.bfloat16)
    rest = value - high.astype(jnp.float32)
    middle = rest.astype(jnp.bfloat16)
    return high, middle, (rest - middle.astype(jnp.float32)).astype(jnp.bfloat16)


def exact(twofold, right):
    high, middle, low = parts(twofold)
    mixed = jnp.where(iota(high.shape, 1) < right.shape[0], high, low)
    right_high, right_middle, right_low = parts(right)
    return by_half(
        jnp.concatenate([high, middle, mixed], axis=1),
        jnp.concatenate(
            [right_high, right_middle, right_high, right_middle, right_low, right_high], axis=0
        ),
        NN,
    )


def packed(block, channels):
    half = block.shape[0] // 2
    sums = jnp.concatenate([block[:half, :channels], block[half:, :channels]], axis=1)
    total, peak = (block[:, channels + i : channels + i + 1] for i in range(2))
    lane = iota((half, LANES), 1)
    columns = jnp.where(lane == 0, total[:half], jnp.where(lane == 1, total[half:], 0.0))
    columns = jnp.where(lane == 2, peak[:half], jnp.where(lane == 3, peak[half:], columns))
    return sums, jnp.transpose(columns)[:ROWS, :]


def prepare_kernel(
    swath_ref,
    enc_ref,
    key_ref,
    query_ref,
    quality_ref,
    cell_ref,
    live_ref,
    before_ref,
    taps_ref,
    ids_ref,
    late_ref,
    stats_ref,
    pack_ref,
    kq_ref,
    block_ref,
):
    sensor = lax.axis_index("sensor")
    odd = lax.rem(lax.axis_index("cell"), 2)
    channels, slots = swath_ref.shape[1:]
    cells = query_ref.shape[1]
    side, half = pack_ref.shape[0], cells // 2

    signal = swath_ref[0]
    one = jnp.concatenate([jnp.zeros((channels, 1), jnp.float32), signal[:, : slots - 1]], axis=1)
    two = jnp.concatenate([jnp.zeros((channels, 2), jnp.float32), signal[:, : slots - 2]], axis=1)
    stacked = jnp.concatenate([two, one, signal], axis=0)
    before = dot(enc_ref[0], stacked, NN)
    first = before[:, :LANES]
    before_ref[...] = jnp.transpose(jnp.concatenate([first, first], axis=0))[:ROWS, :]
    encoded = gelu(before)

    query = query_ref[...]
    key = jnp.concatenate([key_ref[...]] * 2, axis=1)
    key = jnp.transpose(jnp.concatenate([key, key], axis=0))
    key_query = jnp.transpose(exact(key, query) * (1.0 / math.sqrt(channels)))
    query = jnp.transpose(jnp.concatenate([query, jnp.zeros(query.shape, jnp.float32)], axis=0))
    kq_ref[...] = key_query
    own_score = jnp.sum(query * key_query, axis=1, keepdims=True)
    own_score = jnp.where(sensor == 0, own_score, -jnp.inf)

    score = exact(key_query, encoded)
    slot = iota((1, slots), 1)
    ids = jnp.where(slot < live_ref[0, 0], cell_ref[...], -1)
    late_ids = [ids[:, j : j + 1] for j in range(LATE)]
    ids = jnp.where(slot < LATE, -1, ids)
    score = jnp.where(iota((cells, slots), 0) == ids, score + quality_ref[...], -jnp.inf)
    peak = jnp.maximum(jnp.max(score, axis=1, keepdims=True), jnp.maximum(own_score, FLOOR))
    weights = jnp.exp(score - peak)
    place = iota((LANES - channels, slots), 0)
    tokens = jnp.concatenate([encoded, (place == 0).astype(jnp.float32)], axis=0)
    high, low = halves(jnp.transpose(tokens))
    weights_high, weights_low = halves(weights)
    both = jnp.concatenate([high, low], axis=1)
    wide = by_half(weights_high, both, NN)
    block = wide[:, :LANES] + wide[:, LANES:] + by_half(weights_low, high, NN)
    own = jnp.where(iota(query.shape, 1) == channels, 1.0, query)
    block = with_peak(block + own * jnp.exp(own_score - peak), peak, channels)
    block_ref[...] = block
    stats_ref[:half, :], stats_ref[half:, :] = packed(block, channels)
    left = block_ref[pl.ds(0, side, stride=side), :]
    right = block_ref[pl.ds(side - 1, side, stride=side), :]
    pack_ref[...] = jnp.where(odd == 1, right, left)
    gap = jnp.zeros((ROWS - LATE, LANES), jnp.float32)

    def listed(rows):
        return jnp.concatenate([jnp.broadcast_to(r, (1, LANES)) for r in rows] + [gap], axis=0)

    at = [pl.ds(cell_ref[0, j], 1) for j in range(LATE)]
    key_query = listed([kq_ref[a, :] for a in at])
    rest = listed([block_ref[a, :] for a in at])
    late_ref[0] = jnp.where(iota(key_query.shape, 1) < channels, key_query, 0.0)
    late_ref[1] = twice(rest)
    for i in range(2):
        late_ref[2 + i] = jnp.broadcast_to(rest[:, channels + i : channels + i + 1], rest.shape)
    late_ref[4] = listed([quality_ref[:, j : j + 1] for j in range(LATE)])
    same = jnp.where(late_ids[0] == late_ids[1], 0.0, -jnp.inf)
    late_ref[5] = listed([same] * LATE)
    ids_ref[...] = jnp.concatenate(
        [jnp.broadcast_to(i, (1, LANES)) for i in late_ids] + [gap.astype(jnp.int32)], axis=0
    )
    first = enc_ref[0, :, : LATE * channels]
    high, middle, low = parts(jnp.transpose(jnp.concatenate([first, first], axis=0)))
    taps_ref[...] = jnp.concatenate([high, high, middle, high, middle, low], axis=0)


def swapped(value):
    return jnp.concatenate([value[1:2], value[0:1], value[2:]], axis=0)


def pool_kernel(
    taps_ref,
    tail_a_ref,
    tail_b_ref,
    before_ref,
    ids_ref,
    late_ref,
    rest_ref,
    rest_pack_ref,
    stats_ref,
    pack_ref,
):
    cell = lax.axis_index("cell")
    odd = lax.rem(cell, 2)
    side, half = pack_ref.shape[0], stats_ref.shape[0] - ROWS
    channels = LANES // 2
    tail = jnp.where(odd == 1, tail_a_ref[...], tail_b_ref[...])
    tail = jnp.where(cell == 0, 0.0, tail)
    high, middle, low = parts(jnp.concatenate([tail, jnp.zeros(tail.shape, jnp.float32)], axis=0))
    tail = jnp.concatenate([high, middle, high, low, middle, high], axis=1)
    third = tail.shape[1] // 3
    late = [
        dot(tail[:, at : at + third], taps_ref[at : at + third, :], NN, None)[:ROWS, :]
        for at in range(0, 3 * third, third)
    ]
    tokens = gelu(before_ref[...] + (late[0] + (late[1] + late[2])))

    key_query, rest, rest_total, rest_peak, quality, same = (late_ref[i] for i in range(6))
    score = jnp.sum(tokens * key_query, axis=1, keepdims=True) + quality
    other = swapped(score) + same
    peak = jnp.maximum(rest_peak, jnp.maximum(score, other))
    rest_factor, weight, other_weight = (jnp.exp(v - peak) for v in (rest_peak, score, other))
    rows = rest * rest_factor + tokens * weight + swapped(tokens) * other_weight
    totals = rest_total * rest_factor + weight + other_weight

    sums, ends, pack = rest_ref[:half, :], rest_ref[half:, :], rest_pack_ref[...]
    of_sum = iota(sums.shape, 0) + jnp.where(iota(sums.shape, 1) < channels, 0, half)
    kind = iota(ends.shape, 0)
    of_end = iota(ends.shape, 1) + jnp.where(lax.rem(kind, 2) == 0, 0, half)
    of_end = jnp.where(kind < 4, of_end, 2 * half)
    of_pack = iota(pack.shape, 0) * side + jnp.where(odd == 1, side - 1, 0)
    lane = iota((1, LANES), 1)
    for j in range(LATE):
        at, row, total, top = (v[j : j + 1] for v in (ids_ref[...], rows, totals, peak))
        sums = jnp.where(of_sum == at, row, sums)
        ends = jnp.where(of_end == at, jnp.where(kind < 2, total, top), ends)
        row = jnp.where(lane < channels, row, jnp.where(lane == channels, total, top))
        pack = jnp.where(of_pack == at, row, pack)
    stats_ref[:half, :], stats_ref[half:, :] = sums, ends
    pack_ref[...] = pack


def shares(first, second):
    peak = jnp.maximum(first[2:4], second[2:4])
    first_factor = jnp.exp(first[2:4] - peak)
    second_factor = jnp.exp(second[2:4] - peak)
    total = first[0:2] * first_factor + second[0:2] * second_factor
    return first_factor, second_factor, total, peak


def turned(*rows):
    rows = jnp.concatenate(rows, axis=0)
    gap = jnp.zeros((LANES - rows.shape[0], rows.shape[1]), jnp.float32)
    return jnp.transpose(jnp.concatenate([rows, gap], axis=0))


def spread(columns, count):
    left = iota((columns.shape[0], LANES), 1) < LANES // 2
    return [
        jnp.where(left, columns[:, 2 * i : 2 * i + 1], columns[:, 2 * i + 1 : 2 * i + 2])
        for i in range(count)
    ]


def merge_pack_kernel(channels, own_ref, other_ref, out_ref):
    both, peak = merged(own_ref[...], other_ref[...], channels)
    out_ref[...] = with_peak(both, peak, channels)


def merge_kernel(own_ref, other_ref, out_ref):
    half = own_ref.shape[0] - ROWS
    first_factor, second_factor, total, peak = shares(own_ref[half:, :], other_ref[half:, :])
    first_factor, second_factor = spread(turned(first_factor, second_factor), 2)
    out_ref[:half, :] = own_ref[:half, :] * first_factor + other_ref[:half, :] * second_factor
    rest = jnp.zeros((ROWS - 4, total.shape[1]), jnp.float32)
    out_ref[half:, :] = jnp.concatenate([total, peak, rest], axis=0)


def copy_kernel(in_ref, out_ref):
    out_ref[...] = in_ref[...]


def weights_kernel(value_ref, near_ref, hp_ref, after_ref, hpv_ref, taps_ref, code_ref, pick_ref):
    del after_ref
    cell = lax.axis_index("cell")
    channels = value_ref.shape[0]
    cells = near_ref.shape[1]
    side = math.isqrt(cells)
    out_rows, own_hp = hp_ref.shape[0], hp_ref[...]
    value = value_ref[...]
    taps = [
        own_hp[:, k * channels : (k + 1) * channels] for k in range(hp_ref.shape[1] // channels)
    ]
    hpv = dot(jnp.concatenate(taps, axis=0), value, NN)
    hpv_ref[...] = hpv
    high, low = halves(hpv[out_rows:])
    gap = jnp.zeros(low.shape, jnp.float32).astype(jnp.bfloat16)
    taps_ref[...] = jnp.concatenate([high, high, low, gap], axis=1)

    shift = side.bit_length() - 1
    odd = lax.rem(cell, 2)
    offset = near_ref[...] - cell * cells
    after = cells + odd * side + lax.shift_right_arithmetic(offset - cells, shift)
    ahead = cells + (1 - odd) * side + lax.shift_right_arithmetic(offset + cells, shift)
    code_ref[...] = jnp.where(offset < 0, ahead, jnp.where(offset < cells, offset, after))
    halo = code_ref[...] - cells
    place = iota((4 * side, cells), 0)
    place = jnp.where(place < 2 * side, place, jnp.where(place < 3 * side, place - side, -1))
    for k in range(halo.shape[0]):
        here = (place == halo[k : k + 1, :]).astype(jnp.float32).astype(jnp.bfloat16)
        pick_ref[4 * side * k : 4 * side * (k + 1), :] = here


def mean_kernel(own_ref, other_ref, pack_ref, columns_ref):
    odd = lax.rem(lax.axis_index("cell"), 2)
    half = own_ref.shape[0] - ROWS
    count = pack_ref.shape[0]
    side = half // count
    first_factor, second_factor, total, _ = shares(own_ref[half:, :], other_ref[half:, :])
    columns_ref[...] = turned(first_factor / total, second_factor / total)

    def column(ref):
        left = ref[pl.ds(0, count, stride=side), :]
        return jnp.where(odd == 1, left, ref[pl.ds(side - 1, count, stride=side), :])

    first_share, second_share = spread(column(columns_ref), 2)
    pack_ref[...] = column(own_ref) * first_share + column(other_ref) * second_share


def own_kernel(own_ref, other_ref, hpv_ref, code_ref, out_ref):
    out_rows, cells = out_ref.shape
    half = own_ref.shape[0] - ROWS
    first_factor, second_factor, total, _ = shares(own_ref[half:, :], other_ref[half:, :])
    columns = turned(first_factor / total, second_factor / total)
    first_share, second_share = spread(columns, 2)
    mean = own_ref[:half, :] * first_share + other_ref[:half, :] * second_share
    hpv = hpv_ref[...]
    gap = jnp.zeros(hpv.shape, jnp.float32)
    mixed = [
        dot(jnp.concatenate(pair, axis=1), mean, NT, CLOSE) for pair in ((hpv, gap), (gap, hpv))
    ]
    lanes = lax.bitwise_and(code_ref[...], LANES - 1)
    places = lax.shift_right_logical(code_ref[...], LANES.bit_length() - 1)
    for i, start in enumerate(range(0, cells, LANES)):
        total = mixed[i][:out_rows]
        for k in range(code_ref.shape[0]):
            rows = slice((k + 1) * out_rows, (k + 2) * out_rows)
            lane, place = (
                jnp.broadcast_to(v[k : k + 1, start : start + LANES], total.shape)
                for v in (lanes, places)
            )
            taken = 0.0
            for source, values in enumerate(mixed):
                here = taken_lanes(values[rows], lane)
                taken = jnp.where(place == source, here, taken)
            total = total + taken
        out_ref[:, start : start + LANES] = total


def taken_lanes(values, lane):
    return jnp.take_along_axis(values, lane, axis=1, mode="promise_in_bounds")


def halo_kernel(
    channels, last, a_ref, own_b_ref, other_b_ref, partial_ref, taps_ref, pick_ref, out_ref
):
    out_rows = out_ref.shape[0]
    cell = lax.axis_index("cell")
    own_b, other_b = own_b_ref[...], other_b_ref[...]
    a = a_ref[...]
    a = [twice(a), twice(jnp.concatenate([a[:, channels:], a[:, :channels]], axis=1))]
    gap = jnp.zeros(own_b.shape, jnp.float32)
    halo = jnp.concatenate(a + [twice(own_b), twice(other_b), gap], axis=0)
    cells = halo.shape[0]
    turns = LANES // cells
    alone = (cell == 0) | (cell == last)
    share = [
        jnp.broadcast_to(jnp.where(alone, 0.0, v), own_b.shape)
        for v in shares_of(own_b, other_b, channels)
    ]
    share = jnp.concatenate([gap + 1.0] + share + [gap], axis=0)
    share = jnp.transpose(jnp.concatenate([share] * turns, axis=0))[:out_rows]
    left = iota(halo.shape, 1) < channels
    high = halo.astype(jnp.bfloat16).astype(jnp.float32)
    halo = jnp.concatenate(
        [jnp.where(left, high, halo - high), high], axis=1
    ).astype(jnp.bfloat16)
    edge = by_half(taps_ref[...], jnp.concatenate([halo] * turns, axis=0), NT)
    lane = iota((out_rows, LANES), 1)
    groups = []
    for start in range(0, edge.shape[0], turns * out_rows):
        group = edge[start : start + out_rows]
        for turn in range(1, turns):
            rows = edge[start + turn * out_rows : start + (turn + 1) * out_rows]
            group = jnp.where(lane >= turn * cells, rows, group)
        groups.append(group * share)
    high, low = halves(jnp.concatenate(groups, axis=1))
    pick = pick_ref[...]
    both = dot(jnp.concatenate([high, low], axis=0), pick, NN, None)
    out_ref[...] = partial_ref[...] + (both[:out_rows] + both[out_rows:])


def swaps(sensors, cells):
    def listed(partner):
        return [(s * cells + c, partner(s, c)) for s in range(sensors) for c in range(cells)]

    def far(flip):
        def partner(s, c):
            if c in (0, cells - 1):
                return (s ^ 1) * cells + c
            return (s ^ flip) * cells + ((c - 1) ^ 1) + 1

        return listed(partner)

    near = listed(lambda s, c: s * cells + (c ^ 1))

    def across(flip):
        return listed(lambda s, c: (s ^ flip) * cells + c)

    return near, far, across


def on_device(
    swath,
    enc_weight,
    key_weight,
    value_weight,
    cell_query,
    quality,
    sample_cell,
    live,
    neighbours,
    hp_weight,
):
    sensors, ranges = lax.axis_size("sensor"), lax.axis_size("cell")
    channels = swath.shape[1]
    cells = cell_query.shape[1]
    side = math.isqrt(cells)
    out_rows = channels // sensors
    stencil = hp_weight.shape[1] // channels
    vmem = pl.BlockSpec(memory_space=pltpu.VMEM)
    axes = ("sensor", "cell")
    near, far, across = swaps(sensors, ranges)

    def shape(*sizes, dtype=jnp.float32):
        return jax.ShapeDtypeStruct(sizes, dtype)

    def call(kernel, args, outs, cost=None, **more):
        single = not isinstance(outs, list)
        specs = dict(in_specs=[vmem] * len(args), out_specs=vmem if single else [vmem] * len(outs))
        specs.update(more)
        return pl.pallas_call(
            kernel,
            out_shape=outs,
            compiler_params=pltpu.CompilerParams(vmem_limit_bytes=8 * 1024 * 1024),
            cost_estimate=cost
            and pl.CostEstimate(flops=cost, bytes_accessed=cost // 100, transcendentals=0),
            **specs,
        )(*args)

    def bound(kernel):
        return lambda *refs: kernel(channels, *refs)

    hbm = pl.BlockSpec(memory_space=pltpu.HBM)

    def pinned(*args):
        return [pltpu.with_memory_space_constraint(a, pltpu.HBM) for a in args]

    def like(*args):
        return [shape(*a.shape, dtype=a.dtype) for a in args]

    args = [
        swath,
        cell_query,
        enc_weight,
        key_weight,
        quality,
        sample_cell,
        value_weight,
        neighbours,
        hp_weight,
    ]
    *loaded, tail = call(
        load_kernel,
        pinned(*args),
        like(*args[:-1]) + [shape(out_rows, hp_weight.shape[1]), shape(ROWS, LANES)],
        in_specs=[hbm] * len(args),
        scratch_shapes=[
            pltpu.VMEM((channels, LANES), jnp.float32),
            pltpu.SemaphoreType.DMA((len(args) + 1,)),
        ],
    )
    swath, cell_query, enc_weight, key_weight, quality, sample_cell, *loaded = loaded
    tail_b = lax.ppermute(tail, axes, far(0))
    tail_again = call(copy_kernel, [tail], shape(*tail.shape), cost=100_000_000)
    tail_a = lax.ppermute(tail_again, axes, near)

    before, late_taps, ids, late, rest, rest_pack = call(
        prepare_kernel,
        [swath, enc_weight, key_weight, cell_query, quality, sample_cell, live],
        [
            shape(ROWS, 2 * channels),
            shape(6 * LATE * channels, 2 * channels, dtype=jnp.bfloat16),
            shape(ROWS, LANES, dtype=jnp.int32),
            shape(6, ROWS, LANES),
            shape(cells // 2 + ROWS, LANES),
            shape(side, LANES),
        ],
        cost=200_000_000,
        in_specs=[vmem] * 6 + [pl.BlockSpec(memory_space=pltpu.SMEM)],
        scratch_shapes=[pltpu.VMEM((cells, LANES), jnp.float32)] * 2,
    )
    stats, pack = call(
        pool_kernel,
        [
            late_taps,
            tail_a,
            tail_b,
            before,
            ids,
            late,
            rest,
            rest_pack,
        ],
        [shape(*rest.shape), shape(*rest_pack.shape)],
    )

    flip = 1
    while flip * 2 < sensors:
        other, other_pack = (lax.ppermute(v, axes, across(flip)) for v in (stats, pack))
        stats = call(merge_kernel, [stats, other], shape(*stats.shape))
        pack = call(bound(merge_pack_kernel), [pack, other_pack], shape(*pack.shape))
        flip *= 2

    other = lax.ppermute(stats, axes, across(flip))
    other_b = lax.ppermute(pack, axes, far(flip))
    pack_again = call(copy_kernel, [pack], shape(*pack.shape), cost=100_000_000)
    hpv, taps, code, pick = call(
        weights_kernel,
        loaded + [pack_again],
        [
            shape(stencil * out_rows, channels),
            shape((stencil - 1) * out_rows, 4 * channels, dtype=jnp.bfloat16),
            shape(*neighbours.shape, dtype=jnp.int32),
            shape((stencil - 1) * 4 * side, cells, dtype=jnp.bfloat16),
        ],
        cost=100_000_000,
    )
    own_b = lax.ppermute(pack_again, axes, far(0))
    mean_a = call(
        mean_kernel,
        [stats, other],
        shape(side // 2, LANES),
        scratch_shapes=[pltpu.VMEM((cells // 2, LANES), jnp.float32)],
    )
    halo_a = lax.ppermute(mean_a, axes, near)
    partial = call(own_kernel, [stats, other, hpv, code], shape(out_rows, cells), cost=200_000_000)
    return call(
        functools.partial(halo_kernel, channels, ranges - 1),
        [halo_a, own_b, other_b, partial, taps, pick],
        shape(out_rows, cells),
    )


def solution(mesh):
    in_specs = (
        P("sensor", None, "cell"),
        P("sensor", None, None),
        P(),
        P(),
        P(None, "cell"),
        P("sensor", "cell"),
        P("sensor", "cell"),
        P("sensor", "cell"),
        P(None, "cell"),
        P(),
    )
    out_specs = P("sensor", "cell")
    return jax.shard_map(
        on_device, mesh=mesh, in_specs=in_specs, out_specs=out_specs, check_vma=False
    )
```
